256 devices in a mesh: vel: 16 (over x, y_lo, core), space: 16 (over z, y_hi).
Axes of the slice: x: 4, y: 4 (y_hi: 2, y_lo: 2; y = y_hi * 2 + y_lo), z: 8, core: 2. Of those that a mesh axis runs over, the one named last changes fastest.
Arguments:
- state: float32 [13824, 64, 256], P('vel', 'space'), as said below
- velocity_order: int32 [13824], P('vel'), may hold values from 0 to 13823, as said below
- wall_tag: int32 [64, 2, 32], replicated, may hold values from 0 to 2
Outputs:
- state_next: float32 [13824, 64, 256], P('vel', 'space')
- wall_heat: float32 [64, 2, 32], P('space')
The draws below stay inside these ranges and needn't reach their ends.
Inputs may be any that keep to these rules, and one draw needn't show every extreme that they name: `velocity_order`: a permutation; the slots below 6912 hold exactly the velocities with negative cx. `state`: every entry is positive.
All inputs are finite; a program needn't handle non-finite values.
Results may differ from the reference program's by a relative error of at most 0.0001.
Values sent between devices are 32-bit elements; how exact they have to be, the bound alone decides.
No kernel may reach another device: no remote copies, remote signals or barrier semaphores. Data moves between devices by JAX's collectives and lax.ppermute only.
A program may use at most 256 MiB of HBM per device.

```python
import math
import jax
import jax.numpy as jnp
from jax import lax

NV1 = 24
NVEL = 13824
NY = 32
NZ = 8
STEPS = 2
NX = 64


def ordering_common(key):
    half_size = NVEL // 2
    negative = jax.random.permutation(jax.random.fold_in(key, 101), half_size)
    positive = jax.random.permutation(jax.random.fold_in(key, 102), half_size) + half_size
    return jnp.concatenate([negative, positive]).astype(jnp.int32)


def draw_velocity_order(key, part):
    ordering = ordering_common(key)
    return ordering


def draw_state(key, part):
    ordering = ordering_common(key)
    key = jax.random.fold_in(key, 2)
    spacing = 12.0 / NV1

    def coordinate(level_index):
        return (2 * level_index - (NV1 - 1)).astype(jnp.float32) * (0.5 * spacing)
    vel_x = coordinate(ordering // (NV1 * NV1))[:, None, None]
    vel_y = coordinate(ordering // NV1 % NV1)[:, None, None]
    vel_z = coordinate(ordering % NV1)[:, None, None]
    lattice_extent = (1, NX, NY * NZ)
    full_shape = (NVEL, NX, NY * NZ)
    stochastic_seeds = jax.random.split(key, 6)
    particle_concentration = jnp.exp(jax.random.uniform(stochastic_seeds[0], lattice_extent, jnp.float32, math.log(0.6), math.log(1.6)))
    drift_x = 0.25 * jnp.clip(jax.random.normal(stochastic_seeds[1], lattice_extent, jnp.float32), -2.0, 2.0)
    drift_y = 0.25 * jnp.clip(jax.random.normal(stochastic_seeds[2], lattice_extent, jnp.float32), -2.0, 2.0)
    drift_z = 0.25 * jnp.clip(jax.random.normal(stochastic_seeds[3], lattice_extent, jnp.float32), -2.0, 2.0)
    pointwise_thermal_level = jax.random.uniform(stochastic_seeds[4], lattice_extent, jnp.float32, 0.8, 1.3)
    stochastic_disturbance = 1.0 + 0.25 * jax.random.uniform(stochastic_seeds[5], full_shape, jnp.float32, -1.0, 1.0)
    relative_motion_norm = (vel_x - drift_x) ** 2 + (vel_y - drift_y) ** 2 + (vel_z - drift_z) ** 2
    averaged_entries = particle_concentration * pointwise_thermal_level ** (-1.5) * jnp.exp(-relative_motion_norm / (2.0 * pointwise_thermal_level)) * stochastic_disturbance
    return averaged_entries.astype(jnp.float32)


def set_ends(entries, key, least, high):
    shape = entries.shape
    spot = [jax.random.randint(jax.random.fold_in(key, axis), (), 0, shape[axis]) for axis in range(len(shape))]
    entries = entries.at[tuple(spot)].set(least)
    longest = shape.index(max(shape))
    spot[longest] = (spot[longest] + 1) % shape[longest]
    return entries.at[tuple(spot)].set(high)


def setup_inputs(seed: int = 0) -> dict:
    keys = jax.random.split(jax.random.key(seed), 4)
    return {
        "state": draw_state(jax.random.fold_in(keys[3], 71), 0),
        "velocity_order": draw_velocity_order(jax.random.fold_in(keys[3], 71), 0),
        "wall_tag": set_ends(jax.random.randint(keys[2], (NX, 2, NY), 0, 3), jax.random.fold_in(keys[2], 1), 0, 2).astype(jnp.int32),
    }


VSPAN = 12.0
RAREFACTION = 0.05
SHEAR_EXPONENT = 0.81
PRANDTL = 2.0 / 3.0
COURANT = 0.3
BOTTOM_TEMP = 1.4
TOP_TEMP = 0.7
HIGHEST = lax.Precision.HIGHEST


def velocity_parts(index_all, per_dim):
    spacing = VSPAN / per_dim

    def coordinate(level_index):
        return (2 * level_index - (per_dim - 1)).astype(jnp.float32) * (0.5 * spacing)

    return (coordinate(index_all // (per_dim * per_dim)), coordinate((index_all // per_dim) % per_dim),
            coordinate(index_all % per_dim))


def velocity_weight(per_dim):
    return (VSPAN / per_dim) ** 3 / (2.0 * math.pi) ** 1.5


def wall_tables(per_dim):
    index_all = jnp.arange(per_dim ** 3, dtype=jnp.int32)
    vel_x, vel_y, vel_z = velocity_parts(index_all, per_dim)
    speed_sq = vel_x * vel_x + vel_y * vel_y + vel_z * vel_z
    levels = 0.7 + 0.3 * jnp.arange(3, dtype=jnp.float32)
    wall_temps = jnp.stack([BOTTOM_TEMP * levels, TOP_TEMP * levels])
    normal = jnp.stack([jnp.maximum(vel_z, 0.0), jnp.maximum(-vel_z, 0.0)]) * velocity_weight(per_dim)
    profile = wall_temps[:, :, None] ** -1.5 * jnp.exp(-speed_sq[None, None, :] / (2.0 * wall_temps[:, :, None]))
    mass_flux = jnp.sum(normal[:, None, :] * profile, axis=-1)
    energy = jnp.sum(normal[:, None, :] * profile * (0.5 * speed_sq)[None, None, :], axis=-1)
    return wall_temps, mass_flux, energy


def pick(lookup, wall_tags):
    onehot = (wall_tags[..., None] == jnp.arange(3, dtype=jnp.int32)).astype(jnp.float32)
    return jnp.sum(onehot * lookup[None, :, None, :], axis=-1)


def block_moments(centre, vel_x, vel_y, vel_z):
    number = centre.shape[0]
    speed_sq = vel_x * vel_x + vel_y * vel_y + vel_z * vel_z
    coefficients = jnp.stack([jnp.ones_like(vel_x), vel_x, vel_y, vel_z, speed_sq]) * velocity_weight(NV1)
    return jnp.dot(coefficients, centre.reshape(number, -1), precision=HIGHEST)


def block_walls(centre, vel_x, vel_y, vel_z, depth):
    number = centre.shape[0]
    speed_sq = vel_x * vel_x + vel_y * vel_y + vel_z * vel_z
    bottom = centre[:, :, 0::depth].reshape(number, -1)
    top_layer = centre[:, :, depth - 1::depth].reshape(number, -1)
    inward_bottom = jnp.maximum(-vel_z, 0.0) * velocity_weight(NV1)
    inward_top = jnp.maximum(vel_z, 0.0) * velocity_weight(NV1)
    low_sums = jnp.dot(jnp.stack([inward_bottom, inward_bottom * 0.5 * speed_sq]), bottom, precision=HIGHEST)
    high_sums = jnp.dot(jnp.stack([inward_top, inward_top * 0.5 * speed_sq]), top_layer, precision=HIGHEST)
    return jnp.concatenate([low_sums, high_sums], axis=0)


def site_average_arrays(hydrodynamic_averages):
    particle_concentration = hydrodynamic_averages[0]
    mean_flow_first = hydrodynamic_averages[1] / particle_concentration
    mean_flow_second = hydrodynamic_averages[2] / particle_concentration
    mean_flow_third = hydrodynamic_averages[3] / particle_concentration
    pointwise_thermal_level = (hydrodynamic_averages[4] / particle_concentration - (mean_flow_first * mean_flow_first + mean_flow_second * mean_flow_second + mean_flow_third * mean_flow_third)) / 3.0
    return particle_concentration, mean_flow_first, mean_flow_second, mean_flow_third, pointwise_thermal_level


def heat_terms(centre, vel_x, vel_y, vel_z, mean_flow_first, mean_flow_second, mean_flow_third):
    flat_block = centre.reshape(centre.shape[0], -1)
    rel_x = vel_x[:, None] - mean_flow_first[None]
    rel_y = vel_y[:, None] - mean_flow_second[None]
    rel_z = vel_z[:, None] - mean_flow_third[None]
    scaled = (0.5 * velocity_weight(NV1)) * (rel_x * rel_x + rel_y * rel_y + rel_z * rel_z) * flat_block
    return jnp.stack([jnp.sum(rel_x * scaled, axis=0), jnp.sum(rel_y * scaled, axis=0), jnp.sum(rel_z * scaled, axis=0)])


def wall_state(wall_sums, wall_tags, tables):
    wall_temps, mass_flux, energy = tables
    columns = wall_tags.shape[0]
    wall_parts = wall_sums.reshape(2, 2, columns, wall_tags.shape[2])
    incoming_mass = jnp.transpose(wall_parts[:, 0], (1, 0, 2))
    incoming_energy = jnp.transpose(wall_parts[:, 1], (1, 0, 2))
    wall_density = incoming_mass / pick(mass_flux, wall_tags)
    wall_heat = wall_density * pick(energy, wall_tags) - incoming_energy
    return wall_density, pick(wall_temps, wall_tags), wall_heat


def relax(extended, vel_x, vel_y, vel_z, averaged_arrays, wall_density, plate_temp, depth):
    centre = extended[:, 1:-1]
    left_cells = extended[:, :-2]
    right_cells = extended[:, 2:]
    number, columns, plane_size = centre.shape
    particle_concentration, mean_flow_first, mean_flow_second, mean_flow_third, pointwise_thermal_level, thermal_current_first, thermal_current_second, thermal_current_third = [
        field.reshape(columns, plane_size)[None] for field in averaged_arrays]

    def spread_v(velocity):
        return velocity[:, None, None]

    def transport(velocity, upwind_low, upwind_high):
        return (spread_v(jnp.maximum(velocity, 0.0)) * (centre - upwind_low)
                + spread_v(jnp.minimum(velocity, 0.0)) * (upwind_high - centre))

    speed_sq = vel_x * vel_x + vel_y * vel_y + vel_z * vel_z

    def emitted(wall_side):
        wall_t = plate_temp[:, wall_side][None]
        averaged_entries = (wall_density[:, wall_side] * plate_temp[:, wall_side] ** -1.5)[None] * jnp.exp(
            -spread_v(speed_sq) / (2.0 * wall_t))
        return jnp.repeat(averaged_entries, depth, axis=-1)

    z_layer = jnp.arange(plane_size, dtype=jnp.int32) % depth
    below_cells = jnp.where(z_layer == 0, emitted(0), jnp.roll(centre, 1, axis=-1))
    above_cells = jnp.where(z_layer == depth - 1, emitted(1), jnp.roll(centre, -1, axis=-1))
    transport_sum = (transport(vel_x, left_cells, right_cells)
                     + transport(vel_y, jnp.roll(centre, depth, axis=-1), jnp.roll(centre, -depth, axis=-1))
                     + transport(vel_z, below_cells, above_cells))
    rel_x = spread_v(vel_x) - mean_flow_first
    rel_y = spread_v(vel_y) - mean_flow_second
    rel_z = spread_v(vel_z) - mean_flow_third
    relative_motion_norm = rel_x * rel_x + rel_y * rel_y + rel_z * rel_z
    target_maxwellian = particle_concentration * pointwise_thermal_level ** -1.5 * jnp.exp(-relative_motion_norm / (2.0 * pointwise_thermal_level))
    factor = 1.0 + (1.0 - PRANDTL) * (rel_x * thermal_current_first + rel_y * thermal_current_second + rel_z * thermal_current_third) / (
        5.0 * particle_concentration * pointwise_thermal_level * pointwise_thermal_level) * (relative_motion_norm / pointwise_thermal_level - 5.0)
    relaxation_rate = particle_concentration * jnp.exp((1.0 - SHEAR_EXPONENT) * jnp.log(pointwise_thermal_level)) / RAREFACTION
    top_speed = (NV1 - 1) * 0.5 * VSPAN / NV1
    courant_ratio = COURANT / top_speed
    step_time = COURANT / (depth * top_speed)
    return centre - courant_ratio * transport_sum + step_time * relaxation_rate * (target_maxwellian * factor - centre)


def advance(state, wall_tags, vel_x, vel_y, vel_z, tables):
    blocks = 32
    number = state.shape[0] // blocks
    sectioned = state.reshape(blocks, number, state.shape[1], state.shape[2])
    velocities = (vel_x.reshape(blocks, number), vel_y.reshape(blocks, number), vel_z.reshape(blocks, number))
    cells = state.shape[1] * state.shape[2]

    def first_pass(running, scan_item):
        block_piece, part_x, part_y, part_z = scan_item
        return (running[0] + block_moments(block_piece, part_x, part_y, part_z),
                running[1] + block_walls(block_piece, part_x, part_y, part_z, NZ)), None

    initial = (jnp.zeros((5, cells), jnp.float32), jnp.zeros((4, state.shape[1] * NY), jnp.float32))
    (hydrodynamic_averages, wall_sums), _ = lax.scan(first_pass, initial, (sectioned,) + velocities)
    particle_concentration, mean_flow_first, mean_flow_second, mean_flow_third, pointwise_thermal_level = site_average_arrays(hydrodynamic_averages)

    def second_pass(running, scan_item):
        block_piece, part_x, part_y, part_z = scan_item
        return running + heat_terms(block_piece, part_x, part_y, part_z, mean_flow_first, mean_flow_second, mean_flow_third), None

    thermal_current_triple, _ = lax.scan(second_pass, jnp.zeros((3, cells), jnp.float32), (sectioned,) + velocities)
    wall_density, plate_temp, wall_heat = wall_state(wall_sums, wall_tags, tables)
    averaged_arrays = (particle_concentration, mean_flow_first, mean_flow_second, mean_flow_third, pointwise_thermal_level, thermal_current_triple[0], thermal_current_triple[1], thermal_current_triple[2])

    def update(scan_item):
        block_piece, part_x, part_y, part_z = scan_item
        extended = jnp.concatenate([block_piece[:, -1:], block_piece, block_piece[:, :1]], axis=1)
        return relax(extended, part_x, part_y, part_z, averaged_arrays, wall_density, plate_temp, NZ)

    updated = lax.map(update, (sectioned,) + velocities).reshape(state.shape)
    return updated, wall_heat


def reference(state, velocity_order, wall_tag):
    vel_x, vel_y, vel_z = velocity_parts(velocity_order, NV1)
    tables = wall_tables(NV1)
    current = state
    wall_heat = jnp.zeros(wall_tag.shape, jnp.float32)
    for step_index in range(STEPS):
        current, wall_heat = advance(current, wall_tag, vel_x, vel_y, vel_z, tables)
    return current, wall_heat
```

```python
import math

import jax
import jax.numpy as jnp
import numpy as np
from jax import lax
from jax.experimental import pallas as pl
from jax.experimental.pallas import tpu as pltpu
from jax.sharding import PartitionSpec as P

NV1 = 24
NSLOT = 864
NPAD = 896
CELLS = 1024
COL = 256
SPACING = 12.0 / NV1
TOP = (NV1 - 1) * 0.5 * SPACING
KD = 0.3 / TOP
DT = 0.3 / (8 * TOP)
WEIGHT = SPACING**3 / (2.0 * math.pi) ** 1.5
LOG2E = 1.0 / math.log(2.0)
WALL_T = [[b * (0.7 + 0.3 * level) for level in range(3)] for b in (1.4, 0.7)]
AXES = ("vel", "space")
F32 = jnp.float32
BF16 = jnp.bfloat16


def wall_norms():
    line = (2 * np.arange(NV1) - (NV1 - 1)) * 0.5 * SPACING
    cx, cy, cz = np.meshgrid(line, line, line, indexing="ij")
    sq = cx**2 + cy**2 + cz**2
    mass, energy = [], []
    for side in range(2):
        out = np.maximum(cz if side == 0 else -cz, 0.0) * WEIGHT
        prof = [out * t**-1.5 * np.exp(-sq / (2.0 * t)) for t in WALL_T[side]]
        mass.append([float(p.sum()) for p in prof])
        energy.append([float((p * 0.5 * sq).sum()) for p in prof])
    return mass, energy


MASS, ENERGY = wall_norms()


def device_of(i):
    v, s = divmod(i, 16)
    x, r = divmod(v, 4)
    return x, r >> 1, r & 1, s


def index_of(x, y, core, s):
    return ((x % 4 * 2 + y % 2) * 2 + core % 2) * 16 + s % 16


def permute(value, move):
    return lax.ppermute(value, AXES, [(i, index_of(*move(*device_of(i)))) for i in range(256)])


def downstream(value):
    return permute(value, lambda x, y, c, s: (x, y, c, s - 1 if x < 2 else s + 1))


def reduce_vel(part):
    core = permute(part, lambda x, y, c, s: (x, y, c ^ 1, s))
    near = permute(part, lambda x, y, c, s: (x, y ^ 1, c, s))
    both = permute(part, lambda x, y, c, s: (x, y ^ 1, c ^ 1, s))
    part = (part + core) + (near + both)
    one = permute(part, lambda x, y, c, s: (x + 1, y, c, s))
    three = permute(part, lambda x, y, c, s: (x - 1, y, c, s))
    two = permute(part, lambda x, y, c, s: (x + 2, y, c, s))
    return (part + two) + (one + three)


def upstream_first():
    return (lax.axis_index("vel") >= 8).astype(jnp.int32)


def column_of(forward, i):
    return jnp.where(forward == 1, i, 3 - i)


def spec():
    return pl.BlockSpec(memory_space=pltpu.VMEM)


def smem():
    return pl.BlockSpec(memory_space=pltpu.SMEM)


def params():
    return pltpu.CompilerParams(vmem_limit_bytes=48 * 2**20)


def shape(*dims, dtype=F32):
    return jax.ShapeDtypeStruct(dims, dtype)


def unpack_kernel(dir_ref, in_ref, h_ref, near_ref, far_ref):
    rows = h_ref.shape[0]
    forward = dir_ref[0]
    for i in range(4):
        col = column_of(forward, i)
        for half in range(2):
            part = in_ref[pl.ds(half * 4 + col, rows, stride=8), :]
            h_ref[:, pl.ds(i * COL + half * 128, 128)] = part
            if i == 3:
                near_ref[:, pl.ds(half * 128, 128)] = part
            if i == 2:
                far_ref[:, pl.ds(half * 128, 128)] = part


def unpack(forward, flat):
    rows = 96
    return pl.pallas_call(
        unpack_kernel,
        grid=(NSLOT // rows,),
        in_specs=[smem(), pl.BlockSpec((rows * 8, 128), lambda i: (i, 0))],
        out_specs=[
            pl.BlockSpec((rows, CELLS), lambda i: (i, 0)),
            pl.BlockSpec((rows, COL), lambda i: (i, 0)),
            pl.BlockSpec((rows, COL), lambda i: (i, 0)),
        ],
        out_shape=[shape(NSLOT, CELLS), shape(NSLOT, COL), shape(NSLOT, COL)],
        name="unpack",
    )(forward, flat)


def velocity_kernel(order_ref, left_ref, phi_ref, coef_ref, table):
    order = order_ref[...]
    upper = (order * 43691) >> 20
    kx = (upper * 43691) >> 20
    ky = upper - kx * NV1
    kz = order - upper * NV1
    live = (lax.broadcasted_iota(jnp.int32, (1, NPAD), 1) < NSLOT).astype(F32)

    def coordinate(k):
        return (2 * k - (NV1 - 1)).astype(F32) * (0.5 * SPACING) * live

    cx, cy, cz = coordinate(kx), coordinate(ky), coordinate(kz)
    sq = cx * cx + cy * cy + cz * cz
    zero = jnp.zeros_like(cx)
    down, up = jnp.maximum(-cz, 0.0), jnp.maximum(cz, 0.0)
    phi = [live, cx, cy, cz, cx * cx, cy * cy, cz * cz, cx * cy, cx * cz, cy * cz, cx * sq, cy * sq, cz * sq]
    sums = phi + [down, down * (0.5 * sq), zero] + [zero] * 5 + [up, up * (0.5 * sq), zero]

    def high(a):
        return a.astype(BF16).astype(F32)

    for r, a in enumerate(sums):
        table[pl.ds(r, 1), :] = high(a)
        table[pl.ds(24 + r, 1), :] = a - high(a)
    left_ref[...] = table[pl.ds(0, 48), :].astype(BF16)
    ghost = []
    for side, out in ((0, up), (1, down)):
        ghost += [out * KD * jnp.exp(sq * (-0.5 / t)) for t in WALL_T[side]]
    rows = []
    for _ in range(3):
        rows += [high(a) for a in phi] + [zero] * 3
    for _ in range(2):
        rows += [a - high(a) for a in phi] + [zero] * 3
    rows += [high(a) for a in ghost] + [high(a - high(a)) for a in ghost] + [zero] * 4
    rows += [high(a) for a in ghost] + [zero] * 10
    rows += [jnp.abs(cx), jnp.maximum(cy, 0.0), jnp.maximum(-cy, 0.0), up, down]
    rows += [jnp.abs(cx) + jnp.abs(cy) + jnp.abs(cz)] + [zero] * 10
    for r, a in enumerate(rows):
        table[pl.ds(r, 1), :] = a
    turned = table[...].T.astype(BF16)
    phi_ref[...] = turned[:NSLOT]
    row = lax.broadcasted_iota(jnp.int32, (128, 768), 0)
    lane = lax.broadcasted_iota(jnp.int32, (128, 768), 1)
    kind, z = lane >> 7, lane & 7
    drop = ((kind == 3) & (z == 0)) | ((kind == 4) & (z == 7))
    pick = ((row == 112 + kind) & jnp.logical_not(drop)).astype(F32).astype(BF16)
    coef_ref[...] = jnp.dot(turned, pick, preferred_element_type=F32)[:NSLOT] * KD


def velocities(order):
    return pl.pallas_call(
        velocity_kernel,
        in_specs=[spec()],
        out_specs=[spec()] * 3,
        out_shape=[shape(48, NPAD, dtype=BF16), shape(NSLOT, 128, dtype=BF16), shape(NSLOT, 768)],
        scratch_shapes=[pltpu.VMEM((128, NPAD), F32)],
        compiler_params=params(),
        name="velocities",
    )(order)


def clear_tail(high_ref, low_ref):
    tail = jnp.zeros((NPAD - NSLOT, high_ref.shape[1]), BF16)
    high_ref[pl.ds(NSLOT, NPAD - NSLOT), :] = tail
    low_ref[pl.ds(NSLOT, NPAD - NSLOT), :] = tail


def put_moments(forward, left_ref, high_ref, low_ref, out_ref):
    left = left_ref[...]
    sub = lax.broadcasted_iota(jnp.int32, (8, 128), 0)
    lane = lax.broadcasted_iota(jnp.int32, (8, 128), 1)
    top = (sub >= 5) & ((lane & 7) >= 4)
    for i in range(4):
        cols = pl.ds(i * COL, COL)
        first = jnp.dot(left, high_ref[:, cols], preferred_element_type=F32)
        second = jnp.dot(left, low_ref[:, cols], preferred_element_type=F32)
        total = first + second
        total = total[:24] + total[24:]
        col = column_of(forward, i)
        for half in range(2):
            part = total[:, half * 128 : half * 128 + 128]
            mid = jnp.where(top, part[16:24], part[8:16])
            out_ref[pl.ds(col * 2 + half, 8, stride=8), :] = part[0:8]
            out_ref[pl.ds(64 + col * 2 + half, 8, stride=8), :] = mid


def split_into(value, rows, cols, high_ref, low_ref):
    high = value.astype(BF16)
    high_ref[rows, cols] = high
    low_ref[rows, cols] = (value - high.astype(F32)).astype(BF16)


def moment_kernel(dir_ref, h_ref, left_ref, out_ref, high_ref, low_ref):
    clear_tail(high_ref, low_ref)

    def body(k, carry):
        rows = pl.ds(pl.multiple_of(k * 48, 16), 48)
        for b in range(8):
            cols = pl.ds(b * 128, 128)
            split_into(h_ref[rows, cols], rows, cols, high_ref, low_ref)
        return carry

    lax.fori_loop(0, NSLOT // 48, body, 0)
    put_moments(dir_ref[0], left_ref, high_ref, low_ref, out_ref)


def moments(forward, h, left):
    return pl.pallas_call(
        moment_kernel,
        in_specs=[smem(), spec(), spec()],
        out_specs=spec(),
        out_shape=shape(128, 128),
        scratch_shapes=[pltpu.VMEM((NPAD, CELLS), BF16)] * 2,
        compiler_params=params(),
        name="moments",
    )(forward, h, left)


def field_kernel(columns, dir_ref, m_ref, tag_ref, right_ref, keep_ref, heat_ref, table):
    m = [m_ref[pl.ds(f * 8, 8), :] * WEIGHT for f in range(15)]
    rho = m[0]
    inv = 1.0 / rho
    u = [a * inv for a in m[1:4]]
    energy = m[4] + m[5] + m[6]
    usq = u[0] * u[0] + u[1] * u[1] + u[2] * u[2]
    temp = (energy * inv - usq) * (1.0 / 3.0)
    stress = [[m[4], m[7], m[8]], [m[7], m[5], m[9]], [m[8], m[9], m[6]]]
    q = []
    for i in range(3):
        pu = stress[i][0] * u[0] + stress[i][1] * u[1] + stress[i][2] * u[2]
        q.append(0.5 * (m[10 + i] - 2.0 * pu - u[i] * energy + 2.0 * rho * usq * u[i]))
    log_t = jnp.log(temp)
    inv_t = 1.0 / temp
    rate = (DT / 0.05) * rho * jnp.exp(0.19 * log_t)
    amp = rate * rho * jnp.exp(-1.5 * log_t)
    half = (0.5 * LOG2E) * inv_t
    zero = jnp.zeros_like(rho)
    expo = [-half * usq] + [2.0 * half * a for a in u] + [-half] * 3 + [zero] * 9
    scale = inv * inv_t * inv_t * (1.0 / 15.0)
    a = [b * scale for b in q]
    s0 = u[0] * a[0] + u[1] * a[1] + u[2] * a[2]
    s1 = usq * inv_t - 5.0
    poly = [amp * (1.0 - s0 * s1)]
    poly += [amp * (a[i] * s1 + 2.0 * s0 * u[i] * inv_t) for i in range(3)]
    front = amp * inv_t
    poly += [-front * (2.0 * a[i] * u[i] + s0) for i in range(3)]
    poly += [-2.0 * front * (a[i] * u[j] + a[j] * u[i]) for i, j in ((0, 1), (0, 2), (1, 2))]
    poly += [front * a[i] for i in range(3)] + [zero] * 3
    z = lax.broadcasted_iota(jnp.int32, (8, 128), 1) & 7
    tag = tag_ref[...]
    density, heat = zero, zero
    walls = []
    for side, at in ((0, 0), (1, 7)):
        for level in range(3):
            here = (z == at) & (tag == level)
            n = jnp.where(here, m[13] * (1.0 / MASS[side][level]), 0.0)
            heat = jnp.where(here, n * ENERGY[side][level] - m[14], heat)
            walls.append(n * WALL_T[side][level] ** -1.5)
    heat_ref[...] = heat
    for r, c in enumerate(expo + poly + walls + [zero] * 10):
        table[pl.ds(r * 8, 8), :] = c
    keep = 1.0 - rate
    table[pl.ds(384, 8), :] = keep
    forward = dir_ref[0]
    n = len(columns)
    right_ref[...] = jnp.zeros(right_ref.shape, BF16)

    def pieces(value, count):
        out = []
        for _ in range(count):
            piece = value.astype(BF16)
            out.append(piece)
            value = value - piece.astype(F32)
        return out

    for k, i in enumerate(columns):
        col = column_of(forward, i)
        for hf in range(2):
            j = col * 2 + hf
            at = k * COL + hf * 128
            keep_ref[pl.ds(k * 2 + hf, 1), :] = table[pl.ds(384 + j, 1), :]
            for kind in range(2):
                lanes = pl.ds(kind * n * COL + at, 128)
                first, second, third = pieces(table[pl.ds(kind * 128 + j, 16, stride=8), :], 3)
                for g, piece in enumerate((first, second, third, first, second)):
                    right_ref[pl.ds(g * 16, 16), lanes] = piece
            wall = table[pl.ds(256 + j, 16, stride=8), :]
            twice = table[pl.ds(256 + j, 6, stride=8), :]
            twice = jnp.concatenate([twice, twice, jnp.zeros((4, 128), F32)], axis=0)
            lanes = pl.ds(2 * n * COL + at, 128)
            right_ref[pl.ds(80, 16), lanes] = pieces(twice, 1)[0]
            right_ref[pl.ds(96, 16), lanes] = pieces(wall, 2)[1]


def fields(forward, m, tags, columns):
    n = len(columns)

    def kernel(*refs):
        field_kernel(columns, *refs)

    return pl.pallas_call(
        kernel,
        in_specs=[smem(), spec(), spec()],
        out_specs=[spec()] * 3,
        out_shape=[shape(128, 3 * n * COL, dtype=BF16), shape(2 * n, 128), shape(8, 128)],
        scratch_shapes=[pltpu.VMEM((392, 128), F32)],
        compiler_params=params(),
        name="fields",
    )(forward, m, tags)


def products(n, phi_ref, right_ref, prod):
    phi = phi_ref[...]
    for k in range(3 * n):
        cols = pl.ds(k * COL, COL)
        prod[:, cols] = jnp.dot(phi, right_ref[:, cols], preferred_element_type=F32)


def updated(n, i, rows, coefs, h, upwind, keep, prod):
    cx, cyp, cym, czp, czm, spill = coefs
    lane = lax.broadcasted_iota(jnp.int32, (1, 128), 1)
    plus = [pltpu.roll(a, 8, 1) for a in h]
    minus = [pltpu.roll(a, 120, 1) for a in h]
    out = []
    for hf in range(2):
        at = i * COL + hf * 128
        before = jnp.where(lane < 8, plus[1 - hf], plus[hf])
        after = jnp.where(lane >= 120, minus[1 - hf], minus[hf])
        expo = prod[rows, pl.ds(at, 128)]
        poly = prod[rows, pl.ds(n * COL + at, 128)]
        ghost = prod[rows, pl.ds(2 * n * COL + at, 128)]
        new = jnp.exp2(expo) * poly + ghost
        new = new + h[hf] * (keep[2 * i + hf] - spill)
        new = new + (cyp * before + cym * after)
        new = new + (czp * pltpu.roll(h[hf], 1, 1) + czm * pltpu.roll(h[hf], 127, 1))
        if upwind is not None:
            new = new + cx * upwind[hf]
        out.append(new)
    return out


def read_coefs(coef_ref, rows):
    return [coef_ref[rows, pl.ds(c * 128, 128)] for c in range(6)]


def first_kernel(dir_ref, h_ref, halo_ref, right_ref, keep_ref, phi_ref, coef_ref, left_ref, out_ref, m_ref, prod, high_ref, low_ref):
    clear_tail(high_ref, low_ref)
    products(4, phi_ref, right_ref, prod)
    step = 16

    def body(k, carry):
        rows = pl.ds(pl.multiple_of(k * step, step), step)
        coefs = read_coefs(coef_ref, rows)
        keep = [keep_ref[pl.ds(b, 1), :] for b in range(8)]
        upwind = [halo_ref[rows, pl.ds(hf * 128, 128)] for hf in range(2)]
        for i in range(4):
            h = [h_ref[rows, pl.ds(i * COL + hf * 128, 128)] for hf in range(2)]
            new = updated(4, i, rows, coefs, h, upwind, keep, prod)
            for hf in range(2):
                cols = pl.ds(i * COL + hf * 128, 128)
                out_ref[rows, cols] = new[hf]
                split_into(new[hf], rows, cols, high_ref, low_ref)
            upwind = h
        return carry

    lax.fori_loop(0, NSLOT // step, body, 0)
    put_moments(dir_ref[0], left_ref, high_ref, low_ref, m_ref)


def first_step(forward, h, halo, right, keep, phi, coef, left):
    return pl.pallas_call(
        first_kernel,
        in_specs=[smem()] + [spec()] * 7,
        out_specs=[spec()] * 2,
        out_shape=[shape(NSLOT, CELLS), shape(128, 128)],
        scratch_shapes=[pltpu.VMEM((NSLOT, 3 * CELLS), F32)] + [pltpu.VMEM((NPAD, CELLS), BF16)] * 2,
        compiler_params=params(),
        name="first_step",
    )(forward, h, halo, right, keep, phi, coef, left)


def edge_kernel(halo_ref, right_ref, keep_ref, phi_ref, coef_ref, out_ref, prod):
    products(1, phi_ref, right_ref, prod)
    step = 16

    def body(k, carry):
        rows = pl.ds(pl.multiple_of(k * step, step), step)
        coefs = read_coefs(coef_ref, rows)
        keep = [keep_ref[pl.ds(b, 1), :] for b in range(2)]
        h = [halo_ref[rows, pl.ds(hf * 128, 128)] for hf in range(2)]
        new = updated(1, 0, rows, coefs, h, None, keep, prod)
        for hf in range(2):
            out_ref[rows, pl.ds(hf * 128, 128)] = new[hf]
        return carry

    lax.fori_loop(0, NSLOT // step, body, 0)


def edge_step(halo, right, keep, phi, coef):
    return pl.pallas_call(
        edge_kernel,
        in_specs=[spec()] * 5,
        out_specs=spec(),
        out_shape=shape(NSLOT, COL),
        scratch_shapes=[pltpu.VMEM((NSLOT, 3 * COL), F32)],
        compiler_params=params(),
        name="edge_step",
    )(halo, right, keep, phi, coef)


def last_kernel(dir_ref, h_ref, edge_ref, far_ref, right_ref, keep_ref, phi_ref, coef_ref, out_ref, prod):
    products(4, phi_ref, right_ref, prod)
    step = 16
    forward = dir_ref[0]

    def body(k, carry):
        rows = pl.ds(pl.multiple_of(k * step, step), step)
        coefs = read_coefs(coef_ref, rows)
        keep = [keep_ref[pl.ds(b, 1), :] for b in range(8)]
        upwind = [
            edge_ref[rows, pl.ds(hf * 128, 128)] + coefs[0] * far_ref[rows, pl.ds(hf * 128, 128)] for hf in range(2)
        ]
        for i in range(4):
            h = [h_ref[rows, pl.ds(i * COL + hf * 128, 128)] for hf in range(2)]
            new = updated(4, i, rows, coefs, h, upwind, keep, prod)
            for hf in range(2):
                out_ref[pl.ds(k * (8 * step) + hf * 4 + column_of(forward, i), step, stride=8), :] = new[hf]
            upwind = h
        return carry

    lax.fori_loop(0, NSLOT // step, body, 0)


def last_step(forward, h, edge, far, right, keep, phi, coef):
    return pl.pallas_call(
        last_kernel,
        in_specs=[smem()] + [spec()] * 7,
        out_specs=spec(),
        out_shape=shape(NSLOT * 8, 128),
        scratch_shapes=[pltpu.VMEM((NSLOT, 3 * CELLS), F32)],
        compiler_params=params(),
        name="last_step",
    )(forward, h, edge, far, right, keep, phi, coef)


def body(state, velocity_order, wall_tag):
    forward = upstream_first()
    flag = forward.reshape(1)
    flat = state.reshape(NSLOT, 4, 2, 128).transpose(0, 2, 1, 3).reshape(NSLOT * 8, 128)
    h0, near, far = unpack(flag, flat)
    halo = downstream(near)
    far_halo = downstream(far)
    left, phi, coef = velocities(jnp.pad(velocity_order, (0, NPAD - NSLOT)).reshape(1, NPAD))

    s = lax.axis_index("space")
    spread = jnp.repeat(jnp.transpose(wall_tag, (0, 2, 1)), 4, axis=2).reshape(128, 128)
    tags = lax.dynamic_slice_in_dim(spread, s * 8, 8, 0)
    up = (s + jnp.where(forward == 1, 15, 1)) % 16
    tags_up = lax.dynamic_slice_in_dim(spread, up * 8, 8, 0)

    m1 = reduce_vel(moments(flag, h0, left))
    m_up = downstream(m1)
    right, keep, _ = fields(flag, m1, tags, (0, 1, 2, 3))
    h1, part = first_step(flag, h0, halo, right, keep, phi, coef, left)
    m2 = reduce_vel(part)
    right_up, keep_up, _ = fields(flag, m_up, tags_up, (3,))
    edge = edge_step(halo, right_up, keep_up, phi, coef)
    right, keep, heat = fields(flag, m2, tags, (0, 1, 2, 3))
    out = last_step(flag, h1, edge, far_halo, right, keep, phi, coef)
    state_next = out.reshape(NSLOT, 2, 4, 128).transpose(0, 2, 1, 3).reshape(NSLOT, 4, 256)
    heat = heat.reshape(4, 32, 8)
    wall_heat = jnp.stack([heat[:, :, 0], heat[:, :, 7]], axis=1)
    return state_next, wall_heat


def solution(mesh):
    return jax.shard_map(
        body,
        mesh=mesh,
        in_specs=(P("vel", "space", None), P("vel"), P()),
        out_specs=(P("vel", "space", None), P("space", None, None)),
        check_vma=False,
    )
```

```python
import math

import jax
import jax.numpy as jnp
import numpy as np
from jax import lax
from jax.experimental import pallas as pl
from jax.experimental.pallas import tpu as pltpu
from jax.sharding import PartitionSpec as P

NV1 = 24
NSLOT = 864
NPAD = 896
CELLS = 1024
COL = 256
SPACING = 12.0 / NV1
TOP = (NV1 - 1) * 0.5 * SPACING
KD = 0.3 / TOP
DT = 0.3 / (8 * TOP)
WEIGHT = SPACING**3 / (2.0 * math.pi) ** 1.5
LOG2E = 1.0 / math.log(2.0)
WALL_T = [[b * (0.7 + 0.3 * level) for level in range(3)] for b in (1.4, 0.7)]
AXES = ("vel", "space")
F32 = jnp.float32
BF16 = jnp.bfloat16


def wall_norms():
    line = (2 * np.arange(NV1) - (NV1 - 1)) * 0.5 * SPACING
    cx, cy, cz = np.meshgrid(line, line, line, indexing="ij")
    sq = cx**2 + cy**2 + cz**2
    mass, energy = [], []
    for side in range(2):
        out = np.maximum(cz if side == 0 else -cz, 0.0) * WEIGHT
        prof = [out * t**-1.5 * np.exp(-sq / (2.0 * t)) for t in WALL_T[side]]
        mass.append([float(p.sum()) for p in prof])
        energy.append([float((p * 0.5 * sq).sum()) for p in prof])
    return mass, energy


MASS, ENERGY = wall_norms()


def device_of(i):
    v, s = divmod(i, 16)
    x, r = divmod(v, 4)
    return x, r >> 1, r & 1, s


def index_of(x, y, core, s):
    return ((x % 4 * 2 + y % 2) * 2 + core % 2) * 16 + s % 16


def permute(value, move):
    return lax.ppermute(value, AXES, [(i, index_of(*move(*device_of(i)))) for i in range(256)])


def downstream(value):
    return permute(value, lambda x, y, c, s: (x, y, c, s - 1 if x < 2 else s + 1))


def over_near(part):
    return part + permute(part, lambda x, y, c, s: (x, y ^ 1, c, s))


def over_rest(part):
    part = part + permute(part, lambda x, y, c, s: (x, y, c ^ 1, s))
    one = permute(part, lambda x, y, c, s: (x + 1, y, c, s))
    three = permute(part, lambda x, y, c, s: (x - 1, y, c, s))
    two = permute(part, lambda x, y, c, s: (x + 2, y, c, s))
    return (part + two) + (one + three)


def upstream_first():
    return (lax.axis_index("vel") >= 8).astype(jnp.int32)


def column_of(forward, i):
    return jnp.where(forward == 1, i, 3 - i)


def spec():
    return pl.BlockSpec(memory_space=pltpu.VMEM)


def anywhere():
    return pl.BlockSpec(memory_space=pl.ANY)


def smem():
    return pl.BlockSpec(memory_space=pltpu.SMEM)


def params(mib=8):
    return pltpu.CompilerParams(vmem_limit_bytes=mib * 2**20)


def shape(*dims, dtype=F32):
    return jax.ShapeDtypeStruct(dims, dtype)


def fetch(sems, *pairs):
    copies = [pltpu.make_async_copy(src, dst, sems.at[k]) for k, (src, dst) in enumerate(pairs)]
    for copy in copies:
        copy.start()
    return copies


def high(a):
    return a.astype(BF16).astype(F32)


def velocity_rows(order_ref, padded):
    padded[...] = jnp.zeros((1, NPAD), jnp.int32)
    padded[:, pl.ds(0, NSLOT)] = order_ref[...].reshape(1, NSLOT)
    order = padded[...]
    upper = (order * 43691) >> 20
    kx = (upper * 43691) >> 20
    ky = upper - kx * NV1
    kz = order - upper * NV1
    live = (lax.broadcasted_iota(jnp.int32, (1, NPAD), 1) < NSLOT).astype(F32)

    def coordinate(k):
        return (2 * k - (NV1 - 1)).astype(F32) * (0.5 * SPACING) * live

    cx, cy, cz = coordinate(kx), coordinate(ky), coordinate(kz)
    sq = cx * cx + cy * cy + cz * cz
    phi = [live, cx, cy, cz, cx * cx, cy * cy, cz * cz, cx * cy, cx * cz, cy * cz, cx * sq, cy * sq, cz * sq]
    return cx, cy, cz, sq, phi


def put_left(order_ref, padded, table, left_ref):
    _, _, cz, sq, phi = velocity_rows(order_ref, padded)
    zero = jnp.zeros_like(cz)
    down, up = jnp.maximum(-cz, 0.0), jnp.maximum(cz, 0.0)
    sums = phi + [down, down * (0.5 * sq), zero] + [zero] * 5 + [up, up * (0.5 * sq), zero]
    for r, a in enumerate(sums):
        table[pl.ds(r, 1), :] = high(a)
        table[pl.ds(24 + r, 1), :] = a - high(a)
    left_ref[...] = table[...].astype(BF16)


def velocity_kernel(order_ref, phi_ref, coef_ref, table, padded):
    cx, cy, cz, sq, phi = velocity_rows(order_ref, padded)
    zero = jnp.zeros_like(cx)
    down, up = jnp.maximum(-cz, 0.0), jnp.maximum(cz, 0.0)
    ghost = []
    for side, out in ((0, up), (1, down)):
        ghost += [out * KD * jnp.exp(sq * (-0.5 / t)) for t in WALL_T[side]]
    rows = []
    for _ in range(3):
        rows += [high(a) for a in phi] + [zero] * 3
    for _ in range(2):
        rows += [a - high(a) for a in phi] + [zero] * 3
    rows += [high(a) for a in ghost] + [high(a - high(a)) for a in ghost] + [zero] * 4
    rows += [high(a) for a in ghost] + [zero] * 10
    rows += [jnp.abs(cx), jnp.maximum(cy, 0.0), jnp.maximum(-cy, 0.0), up, down]
    rows += [jnp.abs(cx) + jnp.abs(cy) + jnp.abs(cz)] + [zero] * 10
    for r, a in enumerate(rows):
        table[pl.ds(r, 1), :] = a
    turned = table[...].T.astype(BF16)
    phi_ref[...] = turned[:NSLOT]
    row = lax.broadcasted_iota(jnp.int32, (128, 768), 0)
    lane = lax.broadcasted_iota(jnp.int32, (128, 768), 1)
    kind, z = lane >> 7, lane & 7
    drop = ((kind == 3) & (z == 0)) | ((kind == 4) & (z == 7))
    pick = ((row == 112 + kind) & jnp.logical_not(drop)).astype(F32).astype(BF16)
    coef_ref[...] = jnp.dot(turned, pick, preferred_element_type=F32)[:NSLOT] * KD


def velocities(order):
    return pl.pallas_call(
        velocity_kernel,
        in_specs=[spec()],
        out_specs=[spec()] * 2,
        out_shape=[shape(NSLOT, 128, dtype=BF16), shape(NSLOT, 768)],
        scratch_shapes=[pltpu.VMEM((128, NPAD), F32), pltpu.VMEM((1, NPAD), jnp.int32)],
        compiler_params=params(),
        name="velocities",
    )(order)


def clear_tail(high_ref, low_ref):
    tail = jnp.zeros((NPAD - NSLOT, high_ref.shape[1]), BF16)
    high_ref[pl.ds(NSLOT, NPAD - NSLOT), :] = tail
    low_ref[pl.ds(NSLOT, NPAD - NSLOT), :] = tail


def sums_of(left, high, low):
    total = jnp.dot(left, high, preferred_element_type=F32) + jnp.dot(left, low, preferred_element_type=F32)
    total = total[:24] + total[24:]
    sub = lax.broadcasted_iota(jnp.int32, (8, 128), 0)
    lane = lax.broadcasted_iota(jnp.int32, (8, 128), 1)
    top = (sub >= 5) & ((lane & 7) >= 4)
    out = []
    for half in range(2):
        part = total[:, half * 128 : half * 128 + 128]
        out.append((part[0:8], jnp.where(top, part[16:24], part[8:16])))
    return out


def put_moments(forward, left_ref, high_ref, low_ref, out_ref):
    left = left_ref[...]
    for i in range(4):
        cols = pl.ds(i * COL, COL)
        row = column_of(forward, i) * 2
        for half, (low, mid) in enumerate(sums_of(left, high_ref[:, cols], low_ref[:, cols])):
            out_ref[pl.ds(row + half, 8, stride=8), :] = low
            out_ref[pl.ds(64 + row + half, 8, stride=8), :] = mid


def split_into(value, rows, cols, high_ref, low_ref):
    high = value.astype(BF16)
    high_ref[rows, cols] = high
    low_ref[rows, cols] = (value - high.astype(F32)).astype(BF16)


PARTS = 3


def unpack_kernel(dir_ref, in_ref, order_ref, near_ref, m_ref, left_ref, whole, high_ref, low_ref, table, padded, sems):
    forward = dir_ref[0]
    size = NSLOT // PARTS
    spans = [pl.ds(p * size * 8, size * 8) for p in range(PARTS)]
    copies = fetch(sems, *[(in_ref.at[a], whole.at[a]) for a in spans])
    put_left(order_ref, padded, table, left_ref)
    clear_tail(high_ref, low_ref)
    step = 96

    for p in range(PARTS):
        copies[p].wait()

        def body(k, carry):
            first = pl.multiple_of(p * size + k * step, 16)
            rows = pl.ds(first, step)
            for i in range(4):
                for half in range(2):
                    start = first * 8 + half * 4 + column_of(forward, i)
                    part = whole[pl.ds(start, step, stride=8), :]
                    if i == 3:
                        near_ref[rows, pl.ds(half * 128, 128)] = part
                    split_into(part, rows, pl.ds(i * COL + half * 128, 128), high_ref, low_ref)
            return carry

        lax.fori_loop(0, size // step, body, 0)
    put_moments(forward, left_ref, high_ref, low_ref, m_ref)


def unpack(forward, flat, order):
    return pl.pallas_call(
        unpack_kernel,
        in_specs=[smem(), anywhere(), spec()],
        out_specs=[spec()] * 3,
        out_shape=[shape(NSLOT, COL), shape(128, 128), shape(48, NPAD, dtype=BF16)],
        scratch_shapes=[
            pltpu.VMEM((NSLOT * 8, 128), F32),
            pltpu.VMEM((NPAD, CELLS), BF16),
            pltpu.VMEM((NPAD, CELLS), BF16),
            pltpu.VMEM((48, NPAD), F32),
            pltpu.VMEM((1, NPAD), jnp.int32),
            pltpu.SemaphoreType.DMA((PARTS,)),
        ],
        compiler_params=params(16),
        name="unpack",
    )(forward, flat, order)


def tag_kernel(at_ref, tag_ref, out_ref):
    row = lax.broadcasted_iota(jnp.int32, (8, 64), 0)
    x = lax.broadcasted_iota(jnp.int32, (8, 64), 1)
    strip = (x == at_ref[0] * 4 + (row >> 1)).astype(F32).astype(BF16)
    picked = lax.dot_general(
        strip, tag_ref[...].astype(F32).astype(BF16), (((1,), (1,)), ((), ())), preferred_element_type=F32
    )
    row = lax.broadcasted_iota(jnp.int32, (64, COL), 0)
    lane = lax.broadcasted_iota(jnp.int32, (64, COL), 1)
    spread = row == ((lane >> 2) & 1) * 32 + (lane >> 3)
    spread = jnp.dot(picked.astype(BF16), spread.astype(F32).astype(BF16), preferred_element_type=F32)
    odd = (lax.broadcasted_iota(jnp.int32, (8, 128), 0) & 1) == 1
    out_ref[...] = jnp.where(odd, spread[:, 128:], spread[:, :128]).astype(jnp.int32)


def strip_tags(at, tags):
    return pl.pallas_call(
        tag_kernel,
        in_specs=[smem(), spec()],
        out_specs=spec(),
        out_shape=shape(8, 128, dtype=jnp.int32),
        compiler_params=params(),
        name="strip_tags",
    )(at, tags)


def put_fields(forward, m_ref, tag_ref, right_ref, keep_ref, table):
    m = [m_ref[pl.ds(f * 8, 8), :] * WEIGHT for f in range(15)]
    rho = m[0]
    inv = 1.0 / rho
    u = [a * inv for a in m[1:4]]
    energy = m[4] + m[5] + m[6]
    usq = u[0] * u[0] + u[1] * u[1] + u[2] * u[2]
    temp = (energy * inv - usq) * (1.0 / 3.0)
    stress = [[m[4], m[7], m[8]], [m[7], m[5], m[9]], [m[8], m[9], m[6]]]
    q = []
    for i in range(3):
        pu = stress[i][0] * u[0] + stress[i][1] * u[1] + stress[i][2] * u[2]
        q.append(0.5 * (m[10 + i] - 2.0 * pu - u[i] * energy + 2.0 * rho * usq * u[i]))
    log_t = jnp.log(temp)
    inv_t = 1.0 / temp
    rate = (DT / 0.05) * rho * jnp.exp(0.19 * log_t)
    amp = rate * rho * jnp.exp(-1.5 * log_t)
    half = (0.5 * LOG2E) * inv_t
    zero = jnp.zeros_like(rho)
    expo = [-half * usq] + [2.0 * half * a for a in u] + [-half] * 3 + [zero] * 9
    scale = inv * inv_t * inv_t * (1.0 / 15.0)
    a = [b * scale for b in q]
    s0 = u[0] * a[0] + u[1] * a[1] + u[2] * a[2]
    s1 = usq * inv_t - 5.0
    poly = [amp * (1.0 - s0 * s1)]
    poly += [amp * (a[i] * s1 + 2.0 * s0 * u[i] * inv_t) for i in range(3)]
    front = amp * inv_t
    poly += [-front * (2.0 * a[i] * u[i] + s0) for i in range(3)]
    poly += [-2.0 * front * (a[i] * u[j] + a[j] * u[i]) for i, j in ((0, 1), (0, 2), (1, 2))]
    poly += [front * a[i] for i in range(3)] + [zero] * 3
    z = lax.broadcasted_iota(jnp.int32, (8, 128), 1) & 7
    tag = tag_ref[...]
    density, heat = zero, zero
    walls = []
    for side, at in ((0, 0), (1, 7)):
        for level in range(3):
            here = (z == at) & (tag == level)
            n = jnp.where(here, m[13] * (1.0 / MASS[side][level]), 0.0)
            heat = jnp.where(here, n * ENERGY[side][level] - m[14], heat)
            walls.append(n * WALL_T[side][level] ** -1.5)
    for r, c in enumerate(expo + poly + walls + [zero] * 10):
        table[pl.ds(r * 8, 8), :] = c
    keep = 1.0 - rate
    table[pl.ds(384, 8), :] = keep
    n = 4
    right_ref[...] = jnp.zeros(right_ref.shape, BF16)

    def pieces(value, count):
        out = []
        for _ in range(count):
            piece = value.astype(BF16)
            out.append(piece)
            value = value - piece.astype(F32)
        return out

    for k in range(n):
        col = column_of(forward, k)
        for hf in range(2):
            j = col * 2 + hf
            at = k * COL + hf * 128
            keep_ref[pl.ds(k * 2 + hf, 1), :] = table[pl.ds(384 + j, 1), :]
            for kind in range(2):
                lanes = pl.ds(kind * n * COL + at, 128)
                first, second, third = pieces(table[pl.ds(kind * 128 + j, 16, stride=8), :], 3)
                for g, piece in enumerate((first, second, third, first, second)):
                    right_ref[pl.ds(g * 16, 16), lanes] = piece
            wall = table[pl.ds(256 + j, 16, stride=8), :]
            twice = table[pl.ds(256 + j, 6, stride=8), :]
            twice = jnp.concatenate([twice, twice, jnp.zeros((4, 128), F32)], axis=0)
            lanes = pl.ds(2 * n * COL + at, 128)
            right_ref[pl.ds(80, 16), lanes] = pieces(twice, 1)[0]
            right_ref[pl.ds(96, 16), lanes] = pieces(wall, 2)[1]
    return heat


def field_scratch():
    return [pltpu.VMEM((128, 3 * CELLS), BF16), pltpu.VMEM((8, 128), F32), pltpu.VMEM((392, 128), F32)]


def put_heat(heat, table, out_ref):
    lane = lax.broadcasted_iota(jnp.int32, (128, 64), 0)
    to = lax.broadcasted_iota(jnp.int32, (128, 64), 1)
    pick = (lane == (to & 15) * 8 + 7 * (to >> 5)).astype(F32).astype(BF16)
    total = jnp.zeros((8, 64), F32)
    for _ in range(3):
        piece = heat.astype(BF16)
        total = total + jnp.dot(piece, pick, preferred_element_type=F32)
        heat = heat - piece.astype(F32)
    odd = lax.broadcasted_iota(jnp.int32, (8, 64), 0) & 1
    half = (lax.broadcasted_iota(jnp.int32, (8, 64), 1) >> 4) & 1
    total = jnp.where(odd == half, total, 0.0)
    table[pl.ds(0, 8), pl.ds(0, 64)] = total
    for x in range(4):
        for side in range(2):
            lanes = pl.ds(side * 32, 32)
            out_ref[x, pl.ds(side, 1), :] = table[pl.ds(2 * x, 1), lanes] + table[pl.ds(2 * x + 1, 1), lanes]


def products(n, phi_ref, right_ref, prod):
    phi = phi_ref[...]
    for k in range(3 * n):
        cols = pl.ds(k * COL, COL)
        prod[:, cols] = jnp.dot(phi, right_ref[:, cols], preferred_element_type=F32)


def updated(n, i, rows, coefs, h, upwind, keep, prod):
    cx, cyp, cym, czp, czm, spill = coefs
    lane = lax.broadcasted_iota(jnp.int32, (1, 128), 1)
    plus = [pltpu.roll(a, 8, 1) for a in h]
    minus = [pltpu.roll(a, 120, 1) for a in h]
    out = []
    for hf in range(2):
        at = i * COL + hf * 128
        before = jnp.where(lane < 8, plus[1 - hf], plus[hf])
        after = jnp.where(lane >= 120, minus[1 - hf], minus[hf])
        expo = prod[rows, pl.ds(at, 128)]
        poly = prod[rows, pl.ds(n * COL + at, 128)]
        ghost = prod[rows, pl.ds(2 * n * COL + at, 128)]
        new = jnp.exp2(expo) * poly + ghost
        new = new + h[hf] * (keep[2 * i + hf] - spill)
        new = new + (cyp * before + cym * after)
        new = new + (czp * pltpu.roll(h[hf], 1, 1) + czm * pltpu.roll(h[hf], 127, 1))
        if upwind is not None:
            new = new + cx * upwind[hf]
        out.append(new)
    return out


def read_coefs(coef_ref, rows):
    return [coef_ref[rows, pl.ds(c * 128, 128)] for c in range(6)]


def sweep(column, coef_ref, keep_ref, prod, put):
    step = 32

    def body(k, carry):
        first = pl.multiple_of(k * step, step)
        rows = pl.ds(first, step)
        coefs = read_coefs(coef_ref, rows)
        keep = [keep_ref[pl.ds(b, 1), :] for b in range(8)]
        upwind = None
        for i in range(4):
            h = [column(i, hf, first, step) for hf in range(2)]
            new = updated(4, i, rows, coefs, h, upwind, keep, prod)
            for hf in range(2):
                put(i, hf, first, step, new[hf])
            upwind = h
        return carry

    lax.fori_loop(0, NSLOT // step, body, 0)


def first_kernel(
    dir_ref, in_ref, m0_ref, tag_ref, phi_ref, coef_ref, left_ref, c0_ref, rest_ref, edge_ref, m_ref,
    right, keep, table, prod, whole, coef, high_ref, low_ref, sems,
):
    forward = dir_ref[0]
    copies = fetch(sems, (in_ref, whole), (coef_ref, coef))
    clear_tail(high_ref, low_ref)
    put_fields(forward, m0_ref, tag_ref, right, keep, table)
    products(4, phi_ref, right, prod)
    for copy in copies:
        copy.wait()

    def column(i, hf, first, step):
        return whole[pl.ds(first * 8 + hf * 4 + column_of(forward, i), step, stride=8), :]

    def put(i, hf, first, step, new):
        rows = pl.ds(first, step)
        side = pl.ds(hf * 128, 128)
        if i == 0:
            c0_ref[rows, side] = new
        else:
            rest_ref[rows, pl.ds((i - 1) * COL + hf * 128, 128)] = new
        if i == 3:
            edge_ref[rows, side] = new
        split_into(new, rows, pl.ds(i * COL + hf * 128, 128), high_ref, low_ref)

    sweep(column, coef, keep, prod, put)
    put_moments(forward, left_ref, high_ref, low_ref, m_ref)


def first_step(forward, flat, m, tags, phi, coef, left):
    return pl.pallas_call(
        first_kernel,
        in_specs=[smem(), anywhere(), spec(), spec(), spec(), anywhere(), spec()],
        out_specs=[spec()] * 4,
        out_shape=[shape(NSLOT, COL), shape(NSLOT, 3 * COL), shape(NSLOT, COL), shape(128, 128)],
        scratch_shapes=field_scratch()
        + [
            pltpu.VMEM((NSLOT, 3 * CELLS), F32),
            pltpu.VMEM((NSLOT * 8, 128), F32),
            pltpu.VMEM((NSLOT, 768), F32),
            pltpu.VMEM((NPAD, CELLS), BF16),
            pltpu.VMEM((NPAD, CELLS), BF16),
            pltpu.SemaphoreType.DMA((2,)),
        ],
        compiler_params=params(32),
        name="first_step",
    )(forward, flat, m, tags, phi, coef, left)


def inflow_kernel(
    dir_ref, c0_any, halo_any, coef_any, left_any, m_ref, c1_ref, out_ref, c0, halo, coef, left, high_ref, low_ref, sems
):
    copies = fetch(sems, (halo_any, halo), (c0_any, c0), (coef_any.at[:, pl.ds(0, 128)], coef), (left_any, left))
    clear_tail(high_ref, low_ref)
    out_ref[...] = m_ref[...]
    for copy in copies:
        copy.wait()
    step = 48

    def body(k, carry):
        rows = pl.ds(pl.multiple_of(k * step, 16), step)
        cx = coef[rows, :]
        for half in range(2):
            cols = pl.ds(half * 128, 128)
            share = cx * halo[rows, cols]
            c1_ref[rows, cols] = c0[rows, cols] + share
            split_into(share, rows, cols, high_ref, low_ref)
        return carry

    lax.fori_loop(0, NSLOT // step, body, 0)
    row = column_of(dir_ref[0], 0) * 2
    for half, parts in enumerate(sums_of(left[...], high_ref[...], low_ref[...])):
        for k, part in enumerate(parts):
            at = pl.ds(64 * k + row + half, 8, stride=8)
            out_ref[at, :] = m_ref[at, :] + part


def inflow(forward, c0, halo, coef, left, m):
    return pl.pallas_call(
        inflow_kernel,
        in_specs=[smem()] + [anywhere()] * 4 + [spec()],
        out_specs=[spec()] * 2,
        out_shape=[shape(NSLOT, COL), shape(128, 128)],
        scratch_shapes=[
            pltpu.VMEM((NSLOT, COL), F32),
            pltpu.VMEM((NSLOT, COL), F32),
            pltpu.VMEM((NSLOT, 128), F32),
            pltpu.VMEM((48, NPAD), BF16),
            pltpu.VMEM((NPAD, COL), BF16),
            pltpu.VMEM((NPAD, COL), BF16),
            pltpu.SemaphoreType.DMA((4,)),
        ],
        compiler_params=params(),
        name="inflow",
    )(forward, c0, halo, coef, left, m)


def second_kernel(
    dir_ref, c1_any, rest_any, m0_ref, tag_ref, phi_ref, coef_any, out_ref, heat_ref,
    right, keep, table, prod, c1, rest, coef, sems,
):
    forward = dir_ref[0]
    copies = fetch(sems, (c1_any, c1), (rest_any, rest), (coef_any, coef))
    heat = put_fields(forward, m0_ref, tag_ref, right, keep, table)
    put_heat(heat, table, heat_ref)
    products(4, phi_ref, right, prod)
    for copy in copies:
        copy.wait()

    def column(i, hf, first, step):
        if i == 0:
            return c1[pl.ds(first, step), pl.ds(hf * 128, 128)]
        return rest[pl.ds(first, step), pl.ds((i - 1) * COL + hf * 128, 128)]

    def put(i, hf, first, step, new):
        out_ref[pl.ds(first * 8 + hf * 4 + column_of(forward, i), step, stride=8), :] = new

    sweep(column, coef, keep, prod, put)


def second_step(forward, c1, rest, m, tags, phi, coef):
    return pl.pallas_call(
        second_kernel,
        in_specs=[smem(), anywhere(), anywhere(), spec(), spec(), spec(), anywhere()],
        out_specs=[spec()] * 2,
        out_shape=[shape(NSLOT * 8, 128), shape(4, 2, 32)],
        scratch_shapes=field_scratch()
        + [
            pltpu.VMEM((NSLOT, 3 * CELLS), F32),
            pltpu.VMEM((NSLOT, COL), F32),
            pltpu.VMEM((NSLOT, 3 * COL), F32),
            pltpu.VMEM((NSLOT, 768), F32),
            pltpu.SemaphoreType.DMA((3,)),
        ],
        compiler_params=params(32),
        name="second_step",
    )(forward, c1, rest, m, tags, phi, coef)


def last_kernel(dir_ref, h_ref, halo_ref, cx_ref, out_ref):
    step = halo_ref.shape[0]
    col = column_of(dir_ref[0], 0)
    out_ref[...] = h_ref[...]
    cx = cx_ref[...]
    for half in range(2):
        at = pl.ds(half * 4 + col, step, stride=8)
        out_ref[at, :] = h_ref[at, :] + cx * halo_ref[:, pl.ds(half * 128, 128)]


def last(forward, h, halo, coef):
    step = 144
    return pl.pallas_call(
        last_kernel,
        grid=(NSLOT // step,),
        in_specs=[
            smem(),
            pl.BlockSpec((step * 8, 128), lambda i: (i, 0)),
            pl.BlockSpec((step, COL), lambda i: (i, 0)),
            pl.BlockSpec((step, 128), lambda i: (i, 0)),
        ],
        out_specs=pl.BlockSpec((step * 8, 128), lambda i: (i, 0)),
        out_shape=shape(NSLOT * 8, 128),
        compiler_params=params(),
        name="last",
    )(forward, h, halo, coef)


def body(state, velocity_order, wall_tag):
    forward = upstream_first().reshape(1)
    at = lax.axis_index("space").astype(jnp.int32).reshape(1)
    flat = state.reshape(NSLOT, 4, 2, 128).transpose(0, 2, 1, 3).reshape(NSLOT * 8, 128)
    near, m1, left = unpack(forward, flat, velocity_order)
    m1 = over_near(m1)
    near, m1 = lax.optimization_barrier((near, m1))
    halo = downstream(near)
    phi, coef = velocities(velocity_order)
    tags = strip_tags(at, jnp.transpose(wall_tag, (1, 2, 0)).reshape(64, 64))
    m1 = over_rest(m1)
    c0, rest, edge, m2 = first_step(forward, flat, m1, tags, phi, coef, left)
    c1, m2 = inflow(forward, c0, halo, coef, left, m2)
    m2 = over_near(m2)
    edge, m2 = lax.optimization_barrier((edge, m2))
    halo = downstream(edge)
    m2 = over_rest(m2)
    out, wall_heat = second_step(forward, c1, rest, m2, tags, phi, coef)
    out = last(forward, out, halo, coef)
    state_next = out.reshape(NSLOT, 2, 4, 128).transpose(0, 2, 1, 3).reshape(NSLOT, 4, 256)
    return state_next, wall_heat


def solution(mesh):
    return jax.shard_map(
        body,
        mesh=mesh,
        in_specs=(P("vel", "space", None), P("vel"), P()),
        out_specs=(P("vel", "space", None), P("space", None, None)),
        check_vma=False,
    )
```

```python
import math

import jax
import jax.numpy as jnp
import numpy as np
from jax import lax
from jax.experimental import pallas as pl
from jax.experimental.pallas import tpu as pltpu
from jax.sharding import PartitionSpec as P

NV1 = 24
NSLOT = 864
NPAD = 896
CELLS = 1024
COL = 256
SPACING = 12.0 / NV1
TOP = (NV1 - 1) * 0.5 * SPACING
KD = 0.3 / TOP
DT = 0.3 / (8 * TOP)
WEIGHT = SPACING**3 / (2.0 * math.pi) ** 1.5
LOG2E = 1.0 / math.log(2.0)
WALL_T = [[b * (0.7 + 0.3 * level) for level in range(3)] for b in (1.4, 0.7)]
AXES = ("vel", "space")
F32 = jnp.float32
BF16 = jnp.bfloat16


def wall_norms():
    line = (2 * np.arange(NV1) - (NV1 - 1)) * 0.5 * SPACING
    cx, cy, cz = np.meshgrid(line, line, line, indexing="ij")
    sq = cx**2 + cy**2 + cz**2
    mass, energy = [], []
    for side in range(2):
        out = np.maximum(cz if side == 0 else -cz, 0.0) * WEIGHT
        prof = [out * t**-1.5 * np.exp(-sq / (2.0 * t)) for t in WALL_T[side]]
        mass.append([float(p.sum()) for p in prof])
        energy.append([float((p * 0.5 * sq).sum()) for p in prof])
    return mass, energy


MASS, ENERGY = wall_norms()


def device_of(i):
    v, s = divmod(i, 16)
    x, r = divmod(v, 4)
    return x, r >> 1, r & 1, s


def index_of(x, y, core, s):
    return ((x % 4 * 2 + y % 2) * 2 + core % 2) * 16 + s % 16


def permute(value, move):
    return lax.ppermute(value, AXES, [(i, index_of(*move(*device_of(i)))) for i in range(256)])


def downstream(value):
    return permute(value, lambda x, y, c, s: (x, y, c, s - 1 if x < 2 else s + 1))


def over_y(part):
    return part + permute(part, lambda x, y, c, s: (x, y ^ 1, c, s))


def over_x(part):
    return part + permute(part, lambda x, y, c, s: (x ^ 1, y, c, s))


def over_rest(part):
    part = part + permute(part, lambda x, y, c, s: (x ^ 2, y, c, s))
    return part + permute(part, lambda x, y, c, s: (x, y, c ^ 1, s))


def hold(token, *values):
    def kernel(*refs):
        del refs

    place = pl.BlockSpec(memory_space=pl.ANY)
    return pl.pallas_call(
        kernel,
        in_specs=[spec()] + [place] * len(values),
        out_specs=[place] * len(values),
        out_shape=[shape(*v.shape) for v in values],
        input_output_aliases={k + 1: k for k in range(len(values))},
        cost_estimate=cost(HOLD_COST),
        name="hold",
    )(token, *values)


def upstream_first():
    return (lax.axis_index("vel") >= 8).astype(jnp.int32)


def column_of(forward, i):
    return jnp.where(forward == 1, i, 3 - i)


def spec():
    return pl.BlockSpec(memory_space=pltpu.VMEM)


def anywhere():
    return pl.BlockSpec(memory_space=pltpu.HBM)


def smem():
    return pl.BlockSpec(memory_space=pltpu.SMEM)


def params(mib=63.5):
    return pltpu.CompilerParams(vmem_limit_bytes=int(mib * 2**20))


def cost(us):
    return pl.CostEstimate(flops=int(us * 1.15e9), bytes_accessed=10_000, transcendentals=0)


def shape(*dims, dtype=F32):
    return jax.ShapeDtypeStruct(dims, dtype)


def settle(copies):
    for copy in copies:
        copy.wait()


def fetch(sems, *pairs):
    copies = [pltpu.make_async_copy(src, dst, sems.at[k]) for k, (src, dst) in enumerate(pairs)]
    for copy in copies:
        copy.start()
    return copies


def high(a):
    return a.astype(BF16).astype(F32)


def velocity_rows(order_ref, padded):
    padded[...] = jnp.zeros((1, NPAD), jnp.int32)
    padded[:, pl.ds(0, NSLOT)] = order_ref[...].reshape(1, NSLOT)
    order = padded[...]
    upper = (order * 43691) >> 20
    kx = (upper * 43691) >> 20
    ky = upper - kx * NV1
    kz = order - upper * NV1
    live = (lax.broadcasted_iota(jnp.int32, (1, NPAD), 1) < NSLOT).astype(F32)

    def coordinate(k):
        return (2 * k - (NV1 - 1)).astype(F32) * (0.5 * SPACING) * live

    cx, cy, cz = coordinate(kx), coordinate(ky), coordinate(kz)
    sq = cx * cx + cy * cy + cz * cz
    phi = [live, cx, cy, cz, cx * cx, cy * cy, cz * cz, cx * cy, cx * cz, cy * cz, cx * sq, cy * sq, cz * sq]
    return cx, cy, cz, sq, phi


def put_left(order_ref, padded, table, left_ref):
    _, _, cz, sq, phi = velocity_rows(order_ref, padded)
    zero = jnp.zeros_like(cz)
    down, up = jnp.maximum(-cz, 0.0), jnp.maximum(cz, 0.0)
    sums = phi + [down, down * (0.5 * sq), zero] + [zero] * 5 + [up, up * (0.5 * sq), zero]
    for r, a in enumerate(sums):
        table[pl.ds(r, 1), :] = high(a)
        table[pl.ds(24 + r, 1), :] = a - high(a)
    left_ref[...] = table[pl.ds(0, 48), :].astype(BF16)


def put_phi(order_ref, padded, table, phi_ref):
    cx, cy, cz, sq, phi = velocity_rows(order_ref, padded)
    zero = jnp.zeros_like(cx)
    down, up = jnp.maximum(-cz, 0.0), jnp.maximum(cz, 0.0)
    ghost = []
    for side, out in ((0, up), (1, down)):
        ghost += [out * KD * jnp.exp(sq * (-0.5 / t)) for t in WALL_T[side]]
    rows = []
    for _ in range(3):
        rows += [high(a) for a in phi] + [zero] * 3
    for _ in range(2):
        rows += [a - high(a) for a in phi] + [zero] * 3
    rows += [high(a) for a in ghost] + [high(a - high(a)) for a in ghost] + [zero] * 4
    rows += [high(a) for a in ghost] + [zero] * 10
    rows += [jnp.abs(cx), jnp.maximum(cy, 0.0), jnp.maximum(-cy, 0.0), up, down]
    rows += [jnp.abs(cx) + jnp.abs(cy) + jnp.abs(cz)] + [zero] * 10
    for r, a in enumerate(rows):
        table[pl.ds(r, 1), :] = a
    turned = table[...].T.astype(BF16)
    phi_ref[...] = turned[:NSLOT]


def coefs_of(phi, kinds):
    row = lax.broadcasted_iota(jnp.int32, (128, 128 * kinds), 0)
    lane = lax.broadcasted_iota(jnp.int32, (128, 128 * kinds), 1)
    kind, z = lane >> 7, lane & 7
    drop = ((kind == 3) & (z == 0)) | ((kind == 4) & (z == 7))
    pick = ((row == 112 + kind) & jnp.logical_not(drop)).astype(F32).astype(BF16)
    return jnp.dot(phi, pick, preferred_element_type=F32) * KD


def clear_tail(high_ref, low_ref):
    tail = jnp.zeros((NPAD - NSLOT, high_ref.shape[1]), BF16)
    high_ref[pl.ds(NSLOT, NPAD - NSLOT), :] = tail
    low_ref[pl.ds(NSLOT, NPAD - NSLOT), :] = tail


def sums_of(left, high, low):
    total = jnp.dot(left, high, preferred_element_type=F32) + jnp.dot(left, low, preferred_element_type=F32)
    total = total[:24] + total[24:]
    sub = lax.broadcasted_iota(jnp.int32, (8, 128), 0)
    lane = lax.broadcasted_iota(jnp.int32, (8, 128), 1)
    top = (sub >= 5) & ((lane & 7) >= 4)
    out = []
    for half in range(2):
        part = total[:, half * 128 : half * 128 + 128]
        out.append((part[0:8], jnp.where(top, part[16:24], part[8:16])))
    return out


def put_moments(forward, left_ref, high_ref, low_ref, out_ref):
    left = left_ref[...]
    for i in range(4):
        cols = pl.ds(i * COL, COL)
        row = column_of(forward, i) * 2
        for half, (low, mid) in enumerate(sums_of(left, high_ref[:, cols], low_ref[:, cols])):
            out_ref[pl.ds(row + half, 8, stride=8), :] = low
            out_ref[pl.ds(64 + row + half, 8, stride=8), :] = mid


def split_into(value, rows, cols, high_ref, low_ref):
    high = value.astype(BF16)
    high_ref[rows, cols] = high
    low_ref[rows, cols] = (value - high.astype(F32)).astype(BF16)


PARTS = 3
FIRST_COST, SECOND_COST, HOLD_COST = 6, 2, 3


def column_rows(ref, col):
    return ref.reshape(NSLOT * 2, 4, 128).at[:, col, :]


def unpack_kernel(
    dir_ref, in_ref, order_ref, near_any, m_ref, left_any, phi_any,
    left_ref, phi_ref, whole, high_ref, low_ref, table, padded, sems, out_sems,
):
    forward = dir_ref[0]
    size = NSLOT // PARTS
    spans = [pl.ds(p * size * 8, size * 8) for p in range(PARTS)]
    copies = fetch(sems, *[(in_ref.at[a], whole.at[a]) for a in spans])
    put_phi(order_ref, padded, table, phi_ref)
    put_left(order_ref, padded, table, left_ref)
    clear_tail(high_ref, low_ref)
    step = 96

    for p in range(PARTS):
        copies[p].wait()

        def body(k, carry):
            first = pl.multiple_of(p * size + k * step, 16)
            rows = pl.ds(first, step)
            for i in range(4):
                for half in range(2):
                    start = first * 8 + half * 4 + column_of(forward, i)
                    part = whole[pl.ds(start, step, stride=8), :]
                    split_into(part, rows, pl.ds(i * COL + half * 128, 128), high_ref, low_ref)
            return carry

        lax.fori_loop(0, size // step, body, 0)
    near = column_rows(whole, column_of(forward, 3))
    outs = fetch(out_sems, (near, near_any), (left_ref, left_any), (phi_ref, phi_any))
    put_moments(forward, left_ref, high_ref, low_ref, m_ref)
    settle(outs)


def unpack(forward, flat, order):
    return pl.pallas_call(
        unpack_kernel,
        in_specs=[smem(), anywhere(), spec()],
        out_specs=[anywhere(), spec(), anywhere(), anywhere()],
        out_shape=[
            shape(NSLOT * 2, 128), shape(128, 128), shape(48, NPAD, dtype=BF16), shape(NSLOT, 128, dtype=BF16)
        ],
        scratch_shapes=[
            pltpu.VMEM((48, NPAD), BF16),
            pltpu.VMEM((NSLOT, 128), BF16),
            pltpu.VMEM((NSLOT * 8, 128), F32),
            pltpu.VMEM((NPAD, CELLS), BF16),
            pltpu.VMEM((NPAD, CELLS), BF16),
            pltpu.VMEM((128, NPAD), F32),
            pltpu.VMEM((1, NPAD), jnp.int32),
            pltpu.SemaphoreType.DMA((PARTS,)),
            pltpu.SemaphoreType.DMA((3,)),
        ],
        compiler_params=params(),
        name="unpack",
    )(forward, flat, order)


def tag_kernel(at_ref, tag_ref, out_ref):
    row = lax.broadcasted_iota(jnp.int32, (8, 64), 0)
    x = lax.broadcasted_iota(jnp.int32, (8, 64), 1)
    strip = (x == at_ref[0] * 4 + (row >> 1)).astype(F32).astype(BF16)
    picked = lax.dot_general(
        strip, tag_ref[...].astype(F32).astype(BF16), (((1,), (1,)), ((), ())), preferred_element_type=F32
    )
    row = lax.broadcasted_iota(jnp.int32, (64, COL), 0)
    lane = lax.broadcasted_iota(jnp.int32, (64, COL), 1)
    spread = row == ((lane >> 2) & 1) * 32 + (lane >> 3)
    spread = jnp.dot(picked.astype(BF16), spread.astype(F32).astype(BF16), preferred_element_type=F32)
    odd = (lax.broadcasted_iota(jnp.int32, (8, 128), 0) & 1) == 1
    out_ref[...] = jnp.where(odd, spread[:, 128:], spread[:, :128]).astype(jnp.int32)


def strip_tags(at, tags):
    return pl.pallas_call(
        tag_kernel,
        in_specs=[smem(), spec()],
        out_specs=spec(),
        out_shape=shape(8, 128, dtype=jnp.int32),
        compiler_params=params(),
        name="strip_tags",
    )(at, tags)


def put_fields(forward, m_ref, tag_ref, right_ref, keep_ref, table):
    m = [m_ref[pl.ds(f * 8, 8), :] * WEIGHT for f in range(15)]
    rho = m[0]
    inv = 1.0 / rho
    u = [a * inv for a in m[1:4]]
    energy = m[4] + m[5] + m[6]
    usq = u[0] * u[0] + u[1] * u[1] + u[2] * u[2]
    temp = (energy * inv - usq) * (1.0 / 3.0)
    stress = [[m[4], m[7], m[8]], [m[7], m[5], m[9]], [m[8], m[9], m[6]]]
    q = []
    for i in range(3):
        pu = stress[i][0] * u[0] + stress[i][1] * u[1] + stress[i][2] * u[2]
        q.append(0.5 * (m[10 + i] - 2.0 * pu - u[i] * energy + 2.0 * rho * usq * u[i]))
    log_t = jnp.log(temp)
    inv_t = 1.0 / temp
    rate = (DT / 0.05) * rho * jnp.exp(0.19 * log_t)
    amp = rate * rho * jnp.exp(-1.5 * log_t)
    half = (0.5 * LOG2E) * inv_t
    zero = jnp.zeros_like(rho)
    expo = [-half * usq] + [2.0 * half * a for a in u] + [-half] * 3 + [zero] * 9
    scale = inv * inv_t * inv_t * (1.0 / 15.0)
    a = [b * scale for b in q]
    s0 = u[0] * a[0] + u[1] * a[1] + u[2] * a[2]
    s1 = usq * inv_t - 5.0
    poly = [amp * (1.0 - s0 * s1)]
    poly += [amp * (a[i] * s1 + 2.0 * s0 * u[i] * inv_t) for i in range(3)]
    front = amp * inv_t
    poly += [-front * (2.0 * a[i] * u[i] + s0) for i in range(3)]
    poly += [-2.0 * front * (a[i] * u[j] + a[j] * u[i]) for i, j in ((0, 1), (0, 2), (1, 2))]
    poly += [front * a[i] for i in range(3)] + [zero] * 3
    z = lax.broadcasted_iota(jnp.int32, (8, 128), 1) & 7
    tag = tag_ref[...]
    density, heat = zero, zero
    walls = []
    for side, at in ((0, 0), (1, 7)):
        for level in range(3):
            here = (z == at) & (tag == level)
            n = jnp.where(here, m[13] * (1.0 / MASS[side][level]), 0.0)
            heat = jnp.where(here, n * ENERGY[side][level] - m[14], heat)
            walls.append(n * WALL_T[side][level] ** -1.5)
    for r, c in enumerate(expo + poly + walls + [zero] * 10):
        table[pl.ds(r * 8, 8), :] = c
    keep = 1.0 - rate
    table[pl.ds(384, 8), :] = keep
    n = 4
    right_ref[...] = jnp.zeros(right_ref.shape, BF16)

    def pieces(value, count):
        out = []
        for _ in range(count):
            piece = value.astype(BF16)
            out.append(piece)
            value = value - piece.astype(F32)
        return out

    for k in range(n):
        col = column_of(forward, k)
        for hf in range(2):
            j = col * 2 + hf
            at = k * COL + hf * 128
            keep_ref[pl.ds(k * 2 + hf, 1), :] = table[pl.ds(384 + j, 1), :]
            for kind in range(2):
                lanes = pl.ds(kind * n * COL + at, 128)
                first, second, third = pieces(table[pl.ds(kind * 128 + j, 16, stride=8), :], 3)
                for g, piece in enumerate((first, second, third, first, second)):
                    right_ref[pl.ds(g * 16, 16), lanes] = piece
            wall = table[pl.ds(256 + j, 16, stride=8), :]
            twice = table[pl.ds(256 + j, 6, stride=8), :]
            twice = jnp.concatenate([twice, twice, jnp.zeros((4, 128), F32)], axis=0)
            lanes = pl.ds(2 * n * COL + at, 128)
            right_ref[pl.ds(80, 16), lanes] = pieces(twice, 1)[0]
            right_ref[pl.ds(96, 16), lanes] = pieces(wall, 2)[1]
    return heat


def field_scratch():
    return [pltpu.VMEM((128, 3 * CELLS), BF16), pltpu.VMEM((8, 128), F32), pltpu.VMEM((392, 128), F32)]


def put_heat(heat, table, out_ref):
    lane = lax.broadcasted_iota(jnp.int32, (128, 64), 0)
    to = lax.broadcasted_iota(jnp.int32, (128, 64), 1)
    pick = (lane == (to & 15) * 8 + 7 * (to >> 5)).astype(F32).astype(BF16)
    total = jnp.zeros((8, 64), F32)
    for _ in range(3):
        piece = heat.astype(BF16)
        total = total + jnp.dot(piece, pick, preferred_element_type=F32)
        heat = heat - piece.astype(F32)
    odd = lax.broadcasted_iota(jnp.int32, (8, 64), 0) & 1
    half = (lax.broadcasted_iota(jnp.int32, (8, 64), 1) >> 4) & 1
    total = jnp.where(odd == half, total, 0.0)
    table[pl.ds(0, 8), pl.ds(0, 64)] = total
    for x in range(4):
        for side in range(2):
            lanes = pl.ds(side * 32, 32)
            out_ref[x, pl.ds(side, 1), :] = table[pl.ds(2 * x, 1), lanes] + table[pl.ds(2 * x + 1, 1), lanes]


def products(n, phi_ref, right_ref, prod):
    phi = phi_ref[...]
    for k in range(3 * n):
        cols = pl.ds(k * COL, COL)
        prod[:, cols] = jnp.dot(phi, right_ref[:, cols], preferred_element_type=F32)


def updated(n, i, rows, coefs, h, upwind, keep, prod):
    cx, cyp, cym, czp, czm, spill = coefs
    lane = lax.broadcasted_iota(jnp.int32, (1, 128), 1)
    plus = [pltpu.roll(a, 8, 1) for a in h]
    minus = [pltpu.roll(a, 120, 1) for a in h]
    out = []
    for hf in range(2):
        at = i * COL + hf * 128
        before = jnp.where(lane < 8, plus[1 - hf], plus[hf])
        after = jnp.where(lane >= 120, minus[1 - hf], minus[hf])
        expo = prod[rows, pl.ds(at, 128)]
        poly = prod[rows, pl.ds(n * COL + at, 128)]
        ghost = prod[rows, pl.ds(2 * n * COL + at, 128)]
        new = jnp.exp2(expo) * poly + ghost
        new = new + h[hf] * (keep[2 * i + hf] - spill)
        new = new + (cyp * before + cym * after)
        new = new + (czp * pltpu.roll(h[hf], 1, 1) + czm * pltpu.roll(h[hf], 127, 1))
        if upwind is not None:
            new = new + cx * upwind[hf]
        out.append(new)
    return out


def read_coefs(coef_ref, rows):
    return [coef_ref[rows, pl.ds(c * 128, 128)] for c in range(6)]


def sweep(column, coef_ref, keep_ref, prod, put, start=0, stop=NSLOT):
    step = 32

    def body(k, carry):
        first = pl.multiple_of(k * step, step)
        rows = pl.ds(first, step)
        coefs = read_coefs(coef_ref, rows)
        keep = [keep_ref[pl.ds(b, 1), :] for b in range(8)]
        upwind = None
        for i in range(4):
            h = [column(i, hf, first, step) for hf in range(2)]
            new = updated(4, i, rows, coefs, h, upwind, keep, prod)
            for hf in range(2):
                put(i, hf, first, step, new[hf])
            upwind = h
        return carry

    lax.fori_loop(start // step, stop // step, body, 0)


def first_kernel(
    dir_ref, in_ref, m0_ref, tag_ref, phi_ref, left_ref, h1_any, edge_any, m_ref,
    right, keep, table, prod, whole, phi, coef, left, h1, edge, high_ref, low_ref, sems, out_sems,
):
    forward = dir_ref[0]
    copies = fetch(sems, (phi_ref, phi), (in_ref, whole), (left_ref, left))
    clear_tail(high_ref, low_ref)
    put_fields(forward, m0_ref, tag_ref, right, keep, table)
    copies[0].wait()
    products(4, phi, right, prod)
    coef[...] = coefs_of(phi[...], 6)
    settle(copies[1:])

    def column(i, hf, first, step):
        return whole[pl.ds(first * 8 + hf * 4 + column_of(forward, i), step, stride=8), :]

    def put(i, hf, first, step, new):
        rows = pl.ds(first, step)
        cols = pl.ds(i * COL + hf * 128, 128)
        h1[rows, cols] = new
        if i == 3:
            edge[pl.ds(first * 2 + hf, step, stride=2), :] = new
        split_into(new, rows, cols, high_ref, low_ref)

    size = NSLOT // PARTS
    outs = []
    for p in range(PARTS):
        sweep(column, coef, keep, prod, put, p * size, p * size + size)
        rows = pl.ds(p * size, size)
        outs.append(pltpu.make_async_copy(h1.at[rows], h1_any.at[rows], out_sems.at[p]))
        outs[-1].start()
    outs.append(pltpu.make_async_copy(edge, edge_any, out_sems.at[PARTS]))
    outs[-1].start()
    put_moments(forward, left, high_ref, low_ref, m_ref)
    settle(outs)


def first_step(forward, flat, m, tags, phi, left):
    return pl.pallas_call(
        first_kernel,
        in_specs=[smem(), anywhere(), spec(), spec(), anywhere(), anywhere()],
        out_specs=[anywhere(), anywhere(), spec()],
        out_shape=[shape(NSLOT, CELLS), shape(NSLOT * 2, 128), shape(128, 128)],
        scratch_shapes=field_scratch()
        + [
            pltpu.VMEM((NSLOT, 3 * CELLS), F32),
            pltpu.VMEM((NSLOT * 8, 128), F32),
            pltpu.VMEM((NSLOT, 128), BF16),
            pltpu.VMEM((NSLOT, 768), F32),
            pltpu.VMEM((48, NPAD), BF16),
            pltpu.VMEM((NSLOT, CELLS), F32),
            pltpu.VMEM((NSLOT * 2, 128), F32),
            pltpu.VMEM((NPAD, CELLS), BF16),
            pltpu.VMEM((NPAD, CELLS), BF16),
            pltpu.SemaphoreType.DMA((3,)),
            pltpu.SemaphoreType.DMA((PARTS + 1,)),
        ],
        compiler_params=params(),
        cost_estimate=cost(FIRST_COST),
        name="first_step",
    )(forward, flat, m, tags, phi, left)


def inflow_kernel(dir_ref, halo_any, phi_any, left_any, m_ref, out_ref, halo, phi, left, high_ref, low_ref, sems):
    copies = fetch(sems, (phi_any, phi), (halo_any, halo), (left_any, left))
    clear_tail(high_ref, low_ref)
    out_ref[...] = m_ref[...]
    copies[0].wait()
    cx = coefs_of(phi[...], 1)
    settle(copies[1:])
    for half in range(2):
        share = cx * halo[pl.ds(half, NSLOT, stride=2), :]
        split_into(share, pl.ds(0, NSLOT), pl.ds(half * 128, 128), high_ref, low_ref)
    row = column_of(dir_ref[0], 0) * 2
    for half, parts in enumerate(sums_of(left[...], high_ref[...], low_ref[...])):
        for k, part in enumerate(parts):
            at = pl.ds(64 * k + row + half, 8, stride=8)
            out_ref[at, :] = m_ref[at, :] + part


def inflow(forward, halo, phi, left, m):
    return pl.pallas_call(
        inflow_kernel,
        in_specs=[smem()] + [anywhere()] * 3 + [spec()],
        out_specs=spec(),
        out_shape=shape(128, 128),
        scratch_shapes=[
            pltpu.VMEM((NSLOT * 2, 128), F32),
            pltpu.VMEM((NSLOT, 128), BF16),
            pltpu.VMEM((48, NPAD), BF16),
            pltpu.VMEM((NPAD, COL), BF16),
            pltpu.VMEM((NPAD, COL), BF16),
            pltpu.SemaphoreType.DMA((3,)),
        ],
        compiler_params=params(),
        name="inflow",
    )(forward, halo, phi, left, m)


def second_kernel(
    dir_ref, h_any, halo_any, m0_ref, tag_ref, phi_any, out_any, pre_any, heat_ref,
    right, keep, table, prod, h, halo, phi, coef, out_ref, pre_ref, sems, out_sems,
):
    forward = dir_ref[0]
    copies = fetch(sems, (phi_any, phi), (h_any, h), (halo_any, halo))
    heat = put_fields(forward, m0_ref, tag_ref, right, keep, table)
    put_heat(heat, table, heat_ref)
    copies[0].wait()
    products(4, phi, right, prod)
    coef[...] = coefs_of(phi[...], 6)
    settle(copies[1:])

    def column(i, hf, first, step):
        rows = pl.ds(first, step)
        state = h[rows, pl.ds(i * COL + hf * 128, 128)]
        if i == 0:
            state = state + coef[rows, pl.ds(0, 128)] * halo[pl.ds(first * 2 + hf, step, stride=2), :]
        return state

    def put(i, hf, first, step, new):
        out_ref[pl.ds(first * 8 + hf * 4 + column_of(forward, i), step, stride=8), :] = new
        if i == 0:
            pre_ref[pl.ds(first * 2 + hf, step, stride=2), :] = new

    size = NSLOT // PARTS
    outs = []
    for p in range(PARTS):
        sweep(column, coef, keep, prod, put, p * size, p * size + size)
        rows = pl.ds(p * size * 8, size * 8)
        outs.append(pltpu.make_async_copy(out_ref.at[rows], out_any.at[rows], out_sems.at[p]))
        outs[-1].start()
    outs.append(pltpu.make_async_copy(pre_ref, pre_any, out_sems.at[PARTS]))
    outs[-1].start()
    settle(outs)


def second_step(forward, h, halo, m, tags, phi):
    return pl.pallas_call(
        second_kernel,
        in_specs=[smem(), anywhere(), anywhere(), spec(), spec(), anywhere()],
        out_specs=[anywhere(), anywhere(), spec()],
        out_shape=[shape(NSLOT * 8, 128), shape(NSLOT * 2, 128), shape(4, 2, 32)],
        scratch_shapes=field_scratch()
        + [
            pltpu.VMEM((NSLOT, 3 * CELLS), F32),
            pltpu.VMEM((NSLOT, CELLS), F32),
            pltpu.VMEM((NSLOT * 2, 128), F32),
            pltpu.VMEM((NSLOT, 128), BF16),
            pltpu.VMEM((NSLOT, 768), F32),
            pltpu.VMEM((NSLOT * 8, 128), F32),
            pltpu.VMEM((NSLOT * 2, 128), F32),
            pltpu.SemaphoreType.DMA((3,)),
            pltpu.SemaphoreType.DMA((PARTS + 1,)),
        ],
        compiler_params=params(),
        cost_estimate=cost(SECOND_COST),
        name="second_step",
    )(forward, h, halo, m, tags, phi)


def last_kernel(dir_ref, h_any, pre_any, halo_any, phi_any, out_any, pre, halo, phi, sems, out_sems):
    del h_any
    copies = fetch(sems, (phi_any, phi), (pre_any, pre), (halo_any, halo))
    copies[0].wait()
    cx = coefs_of(phi[...], 1)
    settle(copies[1:])
    for half in range(2):
        at = pl.ds(half, NSLOT, stride=2)
        pre[at, :] = pre[at, :] + cx * halo[at, :]
    settle(fetch(out_sems, (pre, column_rows(out_any, column_of(dir_ref[0], 0)))))


def last(forward, h, pre, halo, phi):
    return pl.pallas_call(
        last_kernel,
        in_specs=[smem()] + [anywhere()] * 4,
        out_specs=anywhere(),
        out_shape=shape(NSLOT * 8, 128),
        input_output_aliases={1: 0},
        scratch_shapes=[
            pltpu.VMEM((NSLOT * 2, 128), F32),
            pltpu.VMEM((NSLOT * 2, 128), F32),
            pltpu.VMEM((NSLOT, 128), BF16),
            pltpu.SemaphoreType.DMA((3,)),
            pltpu.SemaphoreType.DMA((1,)),
        ],
        compiler_params=params(),
        name="last",
    )(forward, h, pre, halo, phi)


def body(state, velocity_order, wall_tag):
    forward = upstream_first().reshape(1)
    at = lax.axis_index("space").astype(jnp.int32).reshape(1)
    flat = state.reshape(NSLOT, 4, 2, 128).transpose(0, 2, 1, 3).reshape(NSLOT * 8, 128)
    near, m, left, phi = unpack(forward, flat, velocity_order)
    m = over_y(m)
    (near,) = hold(m, near)
    near = downstream(near)
    tags = strip_tags(at, jnp.transpose(wall_tag, (1, 2, 0)).reshape(64, 64))
    m = over_rest(over_x(m))
    h1, edge, m = first_step(forward, flat, m, tags, phi, left)
    m = over_x(over_y(inflow(forward, near, phi, left, m)))
    (edge,) = hold(m, edge)
    edge = downstream(edge)
    m = over_rest(m)
    out, pre, wall_heat = second_step(forward, h1, near, m, tags, phi)
    out = last(forward, out, pre, edge, phi)
    state_next = out.reshape(NSLOT, 2, 4, 128).transpose(0, 2, 1, 3).reshape(NSLOT, 4, 256)
    return state_next, wall_heat


def solution(mesh):
    return jax.shard_map(
        body,
        mesh=mesh,
        in_specs=(P("vel", "space", None), P("vel"), P()),
        out_specs=(P("vel", "space", None), P("space", None, None)),
        check_vma=False,
    )
```

```python
import math

import jax
import jax.numpy as jnp
import numpy as np
from jax import lax
from jax.experimental import pallas as pl
from jax.experimental.pallas import tpu as pltpu
from jax.sharding import PartitionSpec as P

NV1 = 24
NSLOT = 864
NPAD = 896
CELLS = 1024
COL = 256
SPACING = 12.0 / NV1
TOP = (NV1 - 1) * 0.5 * SPACING
KD = 0.3 / TOP
DT = 0.3 / (8 * TOP)
WEIGHT = SPACING**3 / (2.0 * math.pi) ** 1.5
LOG2E = 1.0 / math.log(2.0)
WALL_T = [[b * (0.7 + 0.3 * level) for level in range(3)] for b in (1.4, 0.7)]
AXES = ("vel", "space")
F32 = jnp.float32
BF16 = jnp.bfloat16


def wall_norms():
    line = (2 * np.arange(NV1) - (NV1 - 1)) * 0.5 * SPACING
    cx, cy, cz = np.meshgrid(line, line, line, indexing="ij")
    sq = cx**2 + cy**2 + cz**2
    mass, energy = [], []
    for side in range(2):
        out = np.maximum(cz if side == 0 else -cz, 0.0) * WEIGHT
        prof = [out * t**-1.5 * np.exp(-sq / (2.0 * t)) for t in WALL_T[side]]
        mass.append([float(p.sum()) for p in prof])
        energy.append([float((p * 0.5 * sq).sum()) for p in prof])
    return mass, energy


MASS, ENERGY = wall_norms()


def device_of(i):
    v, s = divmod(i, 16)
    x, r = divmod(v, 4)
    return x, r >> 1, r & 1, s


def index_of(x, y, core, s):
    return ((x % 4 * 2 + y % 2) * 2 + core % 2) * 16 + s % 16


def permute(value, move):
    return lax.ppermute(value, AXES, [(i, index_of(*move(*device_of(i)))) for i in range(256)])


def downstream(value):
    return permute(value, lambda x, y, c, s: (x, y, c, s - 1 if x < 2 else s + 1))


def over_y(part):
    return part + permute(part, lambda x, y, c, s: (x, y ^ 1, c, s))


def over_x(part):
    return part + permute(part, lambda x, y, c, s: (x ^ 1, y, c, s))


def over_rest(part, *work):
    part = part + permute(part, lambda x, y, c, s: (x ^ 2, y, c, s))
    part, *work = lax.optimization_barrier((part, *work))
    return part + permute(part, lambda x, y, c, s: (x, y, c ^ 1, s)), work


def hold(token, *values):
    def kernel(*refs):
        del refs

    place = pl.BlockSpec(memory_space=pl.ANY)
    return pl.pallas_call(
        kernel,
        in_specs=[spec()] + [place] * len(values),
        out_specs=[place] * len(values),
        out_shape=[shape(*v.shape) for v in values],
        input_output_aliases={k + 1: k for k in range(len(values))},
        compiler_params=params(53),
        cost_estimate=cost(HOLD_COST),
        name="hold",
    )(token, *values)


def upstream_first():
    return (lax.axis_index("vel") >= 8).astype(jnp.int32)


def column_of(forward, i):
    return jnp.where(forward == 1, i, 3 - i)


def spec():
    return pl.BlockSpec(memory_space=pltpu.VMEM)


def anywhere():
    return pl.BlockSpec(memory_space=pltpu.HBM)


def smem():
    return pl.BlockSpec(memory_space=pltpu.SMEM)


def params(mib=63.5):
    return pltpu.CompilerParams(vmem_limit_bytes=int(mib * 2**20))


def cost(us):
    return pl.CostEstimate(flops=int(us * 1.15e9), bytes_accessed=10_000, transcendentals=0)


def shape(*dims, dtype=F32):
    return jax.ShapeDtypeStruct(dims, dtype)


def settle(copies):
    for copy in copies:
        copy.wait()


def fetch(sems, *pairs):
    copies = [pltpu.make_async_copy(src, dst, sems.at[k]) for k, (src, dst) in enumerate(pairs)]
    for copy in copies:
        copy.start()
    return copies


def high(a):
    return a.astype(BF16).astype(F32)


def velocity_rows(order_ref, padded):
    padded[...] = jnp.zeros((1, NPAD), jnp.int32)
    padded[:, pl.ds(0, NSLOT)] = order_ref[...].reshape(1, NSLOT)
    order = padded[...]
    upper = (order * 43691) >> 20
    kx = (upper * 43691) >> 20
    ky = upper - kx * NV1
    kz = order - upper * NV1
    live = (lax.broadcasted_iota(jnp.int32, (1, NPAD), 1) < NSLOT).astype(F32)

    def coordinate(k):
        return (2 * k - (NV1 - 1)).astype(F32) * (0.5 * SPACING) * live

    cx, cy, cz = coordinate(kx), coordinate(ky), coordinate(kz)
    sq = cx * cx + cy * cy + cz * cz
    phi = [live, cx, cy, cz, cx * cx, cy * cy, cz * cz, cx * cy, cx * cz, cy * cz, cx * sq, cy * sq, cz * sq]
    return cx, cy, cz, sq, phi


def put_left(order_ref, padded, table, left_ref):
    _, _, cz, sq, phi = velocity_rows(order_ref, padded)
    zero = jnp.zeros_like(cz)
    down, up = jnp.maximum(-cz, 0.0), jnp.maximum(cz, 0.0)
    sums = phi + [down, down * (0.5 * sq), zero] + [zero] * 5 + [up, up * (0.5 * sq), zero]
    for r, a in enumerate(sums):
        table[pl.ds(r, 1), :] = high(a)
        table[pl.ds(24 + r, 1), :] = a - high(a)
    left_ref[...] = table[pl.ds(0, 48), :].astype(BF16)


def put_phi(order_ref, padded, table, phi_ref):
    cx, cy, cz, sq, phi = velocity_rows(order_ref, padded)
    zero = jnp.zeros_like(cx)
    down, up = jnp.maximum(-cz, 0.0), jnp.maximum(cz, 0.0)
    ghost = []
    for side, out in ((0, up), (1, down)):
        ghost += [out * KD * jnp.exp(sq * (-0.5 / t)) for t in WALL_T[side]]
    rows = []
    for _ in range(3):
        rows += [high(a) for a in phi] + [zero] * 3
    for _ in range(2):
        rows += [a - high(a) for a in phi] + [zero] * 3
    rows += [high(a) for a in ghost] + [high(a - high(a)) for a in ghost] + [zero] * 4
    rows += [high(a) for a in ghost] + [zero] * 10
    rows += [jnp.abs(cx), jnp.maximum(cy, 0.0), jnp.maximum(-cy, 0.0), up, down]
    rows += [jnp.abs(cx) + jnp.abs(cy) + jnp.abs(cz)] + [zero] * 10
    for r, a in enumerate(rows):
        table[pl.ds(r, 1), :] = a
    turned = table[...].T.astype(BF16)
    phi_ref[...] = turned[:NSLOT]


def coefs_of(phi, kinds):
    row = lax.broadcasted_iota(jnp.int32, (128, 128 * kinds), 0)
    lane = lax.broadcasted_iota(jnp.int32, (128, 128 * kinds), 1)
    kind, z = lane >> 7, lane & 7
    drop = ((kind == 3) & (z == 0)) | ((kind == 4) & (z == 7))
    pick = ((row == 112 + kind) & jnp.logical_not(drop)).astype(F32).astype(BF16)
    return jnp.dot(phi, pick, preferred_element_type=F32) * KD


def clear_tail(high_ref, low_ref):
    tail = jnp.zeros((NPAD - NSLOT, high_ref.shape[1]), BF16)
    high_ref[pl.ds(NSLOT, NPAD - NSLOT), :] = tail
    low_ref[pl.ds(NSLOT, NPAD - NSLOT), :] = tail


def sums_of(left, high, low):
    total = jnp.dot(left, high, preferred_element_type=F32) + jnp.dot(left, low, preferred_element_type=F32)
    total = total[:24] + total[24:]
    sub = lax.broadcasted_iota(jnp.int32, (8, 128), 0)
    lane = lax.broadcasted_iota(jnp.int32, (8, 128), 1)
    top = (sub >= 5) & ((lane & 7) >= 4)
    out = []
    for half in range(2):
        part = total[:, half * 128 : half * 128 + 128]
        out.append((part[0:8], jnp.where(top, part[16:24], part[8:16])))
    return out


def put_moments(forward, left_ref, high_ref, low_ref, out_ref):
    left = left_ref[...]
    for i in range(4):
        cols = pl.ds(i * COL, COL)
        row = column_of(forward, i) * 2
        for half, (low, mid) in enumerate(sums_of(left, high_ref[:, cols], low_ref[:, cols])):
            out_ref[pl.ds(row + half, 8, stride=8), :] = low
            out_ref[pl.ds(64 + row + half, 8, stride=8), :] = mid


def split_into(value, rows, cols, high_ref, low_ref):
    high = value.astype(BF16)
    high_ref[rows, cols] = high
    low_ref[rows, cols] = (value - high.astype(F32)).astype(BF16)


PARTS = 3
HALO = 2 * NSLOT
PIECES = (((0, 288), (288, 288), (576, 288)), ((0, 192), (192, 192), (384, 480)))
FIRST_COST, SECOND_COST, HOLD_COST = 4, 2, 3
DRIFT_COST = 2


def column_rows(ref, col):
    return ref.reshape(NSLOT * 2, 4, 128).at[:, col, :]


def unpack_kernel(
    dir_ref, in_ref, order_ref, near_any, m_ref, left_any, phi_any,
    left_ref, phi_ref, flux, whole, high_ref, low_ref, table, padded, sems, out_sems,
):
    forward = dir_ref[0]
    size = NSLOT // PARTS
    spans = [pl.ds(p * size * 8, size * 8) for p in range(PARTS)]
    copies = fetch(sems, *[(in_ref.at[a], whole.at[a]) for a in spans])
    put_phi(order_ref, padded, table, phi_ref)
    put_left(order_ref, padded, table, left_ref)
    clear_tail(high_ref, low_ref)
    step = 96

    for p in range(PARTS):
        copies[p].wait()

        def body(k, carry):
            first = pl.multiple_of(p * size + k * step, 16)
            rows = pl.ds(first, step)
            for i in range(4):
                for half in range(2):
                    start = first * 8 + half * 4 + column_of(forward, i)
                    part = whole[pl.ds(start, step, stride=8), :]
                    split_into(part, rows, pl.ds(i * COL + half * 128, 128), high_ref, low_ref)
            return carry

        lax.fori_loop(0, size // step, body, 0)
    col = column_of(forward, 3)
    near = column_rows(whole, col)
    outs = fetch(out_sems, (near, near_any.at[pl.ds(0, HALO)]), (left_ref, left_any), (phi_ref, phi_any))
    put_moments(forward, left_ref, high_ref, low_ref, m_ref)
    cx = coefs_of(phi_ref[...], 1)
    for half in range(2):
        share = cx * whole[pl.ds(half * 4 + col, NSLOT, stride=8), :]
        split_into(share, pl.ds(0, NSLOT), pl.ds(half * 128, 128), high_ref, low_ref)
    cols = pl.ds(0, COL)
    for half, parts in enumerate(sums_of(left_ref[...], high_ref[:, cols], low_ref[:, cols])):
        for k, part in enumerate(parts):
            flux[pl.ds((half * 2 + k) * 8, 8), :] = part
    outs += [pltpu.make_async_copy(flux, near_any.at[pl.ds(HALO, 32)], out_sems.at[3])]
    outs[-1].start()
    settle(outs)


def unpack(forward, flat, order):
    return pl.pallas_call(
        unpack_kernel,
        in_specs=[smem(), anywhere(), spec()],
        out_specs=[anywhere(), spec(), anywhere(), anywhere()],
        out_shape=[
            shape(HALO + 32, 128), shape(128, 128), shape(48, NPAD, dtype=BF16), shape(NSLOT, 128, dtype=BF16)
        ],
        scratch_shapes=[
            pltpu.VMEM((48, NPAD), BF16),
            pltpu.VMEM((NSLOT, 128), BF16),
            pltpu.VMEM((32, 128), F32),
            pltpu.VMEM((NSLOT * 8, 128), F32),
            pltpu.VMEM((NPAD, CELLS), BF16),
            pltpu.VMEM((NPAD, CELLS), BF16),
            pltpu.VMEM((128, NPAD), F32),
            pltpu.VMEM((1, NPAD), jnp.int32),
            pltpu.SemaphoreType.DMA((PARTS,)),
            pltpu.SemaphoreType.DMA((4,)),
        ],
        compiler_params=params(),
        name="unpack",
    )(forward, flat, order)


def tag_kernel(at_ref, tag_ref, out_ref):
    row = lax.broadcasted_iota(jnp.int32, (8, 64), 0)
    x = lax.broadcasted_iota(jnp.int32, (8, 64), 1)
    strip = (x == at_ref[0] * 4 + (row >> 1)).astype(F32).astype(BF16)
    picked = lax.dot_general(
        strip, tag_ref[...].astype(F32).astype(BF16), (((1,), (1,)), ((), ())), preferred_element_type=F32
    )
    row = lax.broadcasted_iota(jnp.int32, (64, COL), 0)
    lane = lax.broadcasted_iota(jnp.int32, (64, COL), 1)
    spread = row == ((lane >> 2) & 1) * 32 + (lane >> 3)
    spread = jnp.dot(picked.astype(BF16), spread.astype(F32).astype(BF16), preferred_element_type=F32)
    odd = (lax.broadcasted_iota(jnp.int32, (8, 128), 0) & 1) == 1
    out_ref[...] = jnp.where(odd, spread[:, 128:], spread[:, :128]).astype(jnp.int32)


def strip_tags(at, tags):
    return pl.pallas_call(
        tag_kernel,
        in_specs=[smem(), spec()],
        out_specs=spec(),
        out_shape=shape(8, 128, dtype=jnp.int32),
        compiler_params=params(),
        name="strip_tags",
    )(at, tags)


def put_fields(forward, m_ref, tag_ref, right_ref, keep_ref, table):
    m = [m_ref[pl.ds(f * 8, 8), :] * WEIGHT for f in range(15)]
    rho = m[0]
    inv = 1.0 / rho
    u = [a * inv for a in m[1:4]]
    energy = m[4] + m[5] + m[6]
    usq = u[0] * u[0] + u[1] * u[1] + u[2] * u[2]
    temp = (energy * inv - usq) * (1.0 / 3.0)
    stress = [[m[4], m[7], m[8]], [m[7], m[5], m[9]], [m[8], m[9], m[6]]]
    q = []
    for i in range(3):
        pu = stress[i][0] * u[0] + stress[i][1] * u[1] + stress[i][2] * u[2]
        q.append(0.5 * (m[10 + i] - 2.0 * pu - u[i] * energy + 2.0 * rho * usq * u[i]))
    log_t = jnp.log(temp)
    inv_t = 1.0 / temp
    rate = (DT / 0.05) * rho * jnp.exp(0.19 * log_t)
    amp = rate * rho * jnp.exp(-1.5 * log_t)
    half = (0.5 * LOG2E) * inv_t
    zero = jnp.zeros_like(rho)
    expo = [-half * usq] + [2.0 * half * a for a in u] + [-half] * 3 + [zero] * 9
    scale = inv * inv_t * inv_t * (1.0 / 15.0)
    a = [b * scale for b in q]
    s0 = u[0] * a[0] + u[1] * a[1] + u[2] * a[2]
    s1 = usq * inv_t - 5.0
    poly = [amp * (1.0 - s0 * s1)]
    poly += [amp * (a[i] * s1 + 2.0 * s0 * u[i] * inv_t) for i in range(3)]
    front = amp * inv_t
    poly += [-front * (2.0 * a[i] * u[i] + s0) for i in range(3)]
    poly += [-2.0 * front * (a[i] * u[j] + a[j] * u[i]) for i, j in ((0, 1), (0, 2), (1, 2))]
    poly += [front * a[i] for i in range(3)] + [zero] * 3
    z = lax.broadcasted_iota(jnp.int32, (8, 128), 1) & 7
    tag = tag_ref[...]
    density, heat = zero, zero
    walls = []
    for side, at in ((0, 0), (1, 7)):
        for level in range(3):
            here = (z == at) & (tag == level)
            n = jnp.where(here, m[13] * (1.0 / MASS[side][level]), 0.0)
            heat = jnp.where(here, n * ENERGY[side][level] - m[14], heat)
            walls.append(n * WALL_T[side][level] ** -1.5)
    for r, c in enumerate(expo + poly + walls + [zero] * 10):
        table[pl.ds(r * 8, 8), :] = c
    table[pl.ds(384, 8), :] = rate
    n = 4
    right_ref[...] = jnp.zeros(right_ref.shape, BF16)

    def pieces(value, count):
        out = []
        for _ in range(count):
            piece = value.astype(BF16)
            out.append(piece)
            value = value - piece.astype(F32)
        return out

    for k in range(n):
        col = column_of(forward, k)
        for hf in range(2):
            j = col * 2 + hf
            at = k * COL + hf * 128
            keep_ref[pl.ds(k * 2 + hf, 1), :] = table[pl.ds(384 + j, 1), :]
            for kind in range(2):
                lanes = pl.ds(kind * n * COL + at, 128)
                first, second, third = pieces(table[pl.ds(kind * 128 + j, 16, stride=8), :], 3)
                for g, piece in enumerate((first, second, third, first, second)):
                    right_ref[pl.ds(g * 16, 16), lanes] = piece
            wall = table[pl.ds(256 + j, 16, stride=8), :]
            twice = table[pl.ds(256 + j, 6, stride=8), :]
            twice = jnp.concatenate([twice, twice, jnp.zeros((4, 128), F32)], axis=0)
            lanes = pl.ds(2 * n * COL + at, 128)
            right_ref[pl.ds(80, 16), lanes] = pieces(twice, 1)[0]
            right_ref[pl.ds(96, 16), lanes] = pieces(wall, 2)[1]
    return heat


def field_scratch():
    return [pltpu.VMEM((128, 3 * CELLS), BF16), pltpu.VMEM((8, 128), F32), pltpu.VMEM((392, 128), F32)]


def put_heat(heat, table, out_ref):
    lane = lax.broadcasted_iota(jnp.int32, (128, 64), 0)
    to = lax.broadcasted_iota(jnp.int32, (128, 64), 1)
    pick = (lane == (to & 15) * 8 + 7 * (to >> 5)).astype(F32).astype(BF16)
    total = jnp.zeros((8, 64), F32)
    for _ in range(3):
        piece = heat.astype(BF16)
        total = total + jnp.dot(piece, pick, preferred_element_type=F32)
        heat = heat - piece.astype(F32)
    odd = lax.broadcasted_iota(jnp.int32, (8, 64), 0) & 1
    half = (lax.broadcasted_iota(jnp.int32, (8, 64), 1) >> 4) & 1
    total = jnp.where(odd == half, total, 0.0)
    table[pl.ds(0, 8), pl.ds(0, 64)] = total
    for x in range(4):
        for side in range(2):
            lanes = pl.ds(side * 32, 32)
            out_ref[x, pl.ds(side, 1), :] = table[pl.ds(2 * x, 1), lanes] + table[pl.ds(2 * x + 1, 1), lanes]


def products(n, phi_ref, right_ref, prod):
    phi = phi_ref[...]
    for k in range(3 * n):
        cols = pl.ds(k * COL, COL)
        prod[:, cols] = jnp.dot(phi, right_ref[:, cols], preferred_element_type=F32)


def drift_of(coefs, h, upwind):
    cx, cyp, cym, czp, czm, spill = coefs
    lane = lax.broadcasted_iota(jnp.int32, (1, 128), 1)
    plus = [pltpu.roll(a, 8, 1) for a in h]
    minus = [pltpu.roll(a, 120, 1) for a in h]
    out = []
    for hf in range(2):
        before = jnp.where(lane < 8, plus[1 - hf], plus[hf])
        after = jnp.where(lane >= 120, minus[1 - hf], minus[hf])
        new = h[hf] - spill * h[hf]
        new = new + (cyp * before + cym * after)
        new = new + (czp * pltpu.roll(h[hf], 1, 1) + czm * pltpu.roll(h[hf], 127, 1))
        if upwind is not None:
            new = new + cx * upwind[hf]
        out.append(new)
    return out


def read_coefs(coef_ref, rows):
    return [coef_ref[rows, pl.ds(c * 128, 128)] for c in range(6)]


def drift_kernel(dir_ref, phi_any, *refs, start, size, first_step):
    steps = size // 3
    if first_step:
        state_any, out_any, phi, state, out, coef, sems, out_sems = refs
        spans = [(pl.ds((start + q * steps) * 8, steps * 8), pl.ds(q * steps * 8, steps * 8)) for q in range(3)]
        pairs = [[(state_any.at[a], state.at[b])] for a, b in spans]
    else:
        state_any, halo_any, out_any, phi, state, halo, out, coef, sems, out_sems = refs
        spans = [(pl.ds(start + q * steps, steps), pl.ds(q * steps, steps)) for q in range(3)]
        pairs = [[(state_any.at[a], state.at[b])] for a, b in spans]
        pairs[0].append((halo_any.at[pl.ds(start * 2, size * 2)], halo))
    flat_pairs = [(phi_any.at[pl.ds(start, size)], phi)] + [pair for group in pairs for pair in group]
    copies = fetch(sems, *flat_pairs)
    forward = dir_ref[0]
    copies[0].wait()
    coef[...] = coefs_of(phi[...], 6)
    step = 32
    at = 1
    outs = []
    for q in range(3):
        settle(copies[at : at + len(pairs[q])])
        at += len(pairs[q])

        def body(k, carry):
            first = pl.multiple_of(q * steps + k * step, step)
            rows = pl.ds(first, step)
            coefs = read_coefs(coef, rows)
            upwind = None
            for i in range(4):
                if first_step:
                    col = column_of(forward, i)
                    h = [state[pl.ds(first * 8 + hf * 4 + col, step, stride=8), :] for hf in range(2)]
                else:
                    h = [state[rows, pl.ds(i * COL + hf * 128, 128)] for hf in range(2)]
                    if i == 0:
                        h = [a + coefs[0] * halo[pl.ds(first * 2 + hf, step, stride=2), :] for hf, a in enumerate(h)]
                for hf, new in enumerate(drift_of(coefs, h, upwind)):
                    out[rows, pl.ds(i * COL + hf * 128, 128)] = new
                upwind = h
            return carry

        lax.fori_loop(0, steps // step, body, 0)
        rows = pl.ds(q * steps, steps)
        outs.append(pltpu.make_async_copy(out.at[rows], out_any.at[rows], out_sems.at[q]))
        outs[-1].start()
    settle(outs)


def drift(forward, phi, piece, *states):
    first_step = len(states) == 1
    start, size = piece

    def kernel(*refs):
        drift_kernel(*refs, start=start, size=size, first_step=first_step)

    if first_step:
        held = [pltpu.VMEM((size * 8, 128), F32)]
    else:
        held = [pltpu.VMEM((size, CELLS), F32), pltpu.VMEM((size * 2, 128), F32)]
    return pl.pallas_call(
        kernel,
        in_specs=[smem()] + [anywhere()] * (1 + len(states)),
        out_specs=anywhere(),
        out_shape=shape(size, CELLS),
        scratch_shapes=[pltpu.VMEM((size, 128), BF16)]
        + held
        + [
            pltpu.VMEM((size, CELLS), F32),
            pltpu.VMEM((size, 768), F32),
            pltpu.SemaphoreType.DMA((5,)),
            pltpu.SemaphoreType.DMA((3,)),
        ],
        compiler_params=params(),
        cost_estimate=cost(DRIFT_COST),
        name="drift",
    )(forward, phi, *states)


def sweep(column, drifted, rate_ref, prod, put, start, stop):
    step = 32

    def body(k, carry):
        first = pl.multiple_of(k * step, step)
        rows = pl.ds(first, step)
        for i in range(4):
            for hf in range(2):
                at = i * COL + hf * 128
                expo = prod[rows, pl.ds(at, 128)]
                poly = prod[rows, pl.ds(CELLS + at, 128)]
                ghost = prod[rows, pl.ds(2 * CELLS + at, 128)]
                new = jnp.exp2(expo) * poly + ghost
                new = new + drifted[rows, pl.ds(at, 128)]
                new = new - rate_ref[pl.ds(2 * i + hf, 1), :] * column(i, hf, first, step)
                put(i, hf, first, step, new)
        return carry

    lax.fori_loop(start // step, stop // step, body, 0)


def fetch_parts(sems, pieces, drifted_any, drifted, state_any, state, scale):
    size = NSLOT // PARTS
    pairs, counts = [], []
    left = list(zip(pieces, drifted_any, strict=True))
    for p in range(PARTS):
        rows = pl.ds(p * size * scale, size * scale)
        group = [(state_any.at[rows], state.at[rows])]
        while left and left[0][0][0] < (p + 1) * size:
            (start, count), ref = left.pop(0)
            group.append((ref, drifted.at[pl.ds(start, count)]))
        pairs += group
        counts.append(len(group))
    copies = fetch(sems, *pairs)
    return [copies[sum(counts[:p]) : sum(counts[: p + 1])] for p in range(PARTS)]


def first_kernel(
    dir_ref, in_ref, d0_any, d1_any, d2_any, m0_ref, tag_ref, phi_ref, left_ref, h1_any, edge_any, m_ref,
    right, keep, table, prod, whole, drifted, phi, left, h1, edge, high_ref, low_ref, sems, part_sems, out_sems,
):
    forward = dir_ref[0]
    copies = fetch(sems, (phi_ref, phi), (left_ref, left))
    parts = fetch_parts(part_sems, PIECES[0], (d0_any, d1_any, d2_any), drifted, in_ref, whole, 8)
    clear_tail(high_ref, low_ref)
    put_fields(forward, m0_ref, tag_ref, right, keep, table)
    settle(copies)
    products(4, phi, right, prod)

    def column(i, hf, first, step):
        return whole[pl.ds(first * 8 + hf * 4 + column_of(forward, i), step, stride=8), :]

    def put(i, hf, first, step, new):
        rows = pl.ds(first, step)
        cols = pl.ds(i * COL + hf * 128, 128)
        h1[rows, cols] = new
        if i == 3:
            edge[pl.ds(first * 2 + hf, step, stride=2), :] = new
        split_into(new, rows, cols, high_ref, low_ref)

    size = NSLOT // PARTS
    outs = []
    for p in range(PARTS):
        settle(parts[p])
        sweep(column, drifted, keep, prod, put, p * size, p * size + size)
        rows = pl.ds(p * size, size)
        outs.append(pltpu.make_async_copy(h1.at[rows], h1_any.at[rows], out_sems.at[p]))
        outs[-1].start()
    outs.append(pltpu.make_async_copy(edge, edge_any, out_sems.at[PARTS]))
    outs[-1].start()
    put_moments(forward, left, high_ref, low_ref, m_ref)
    settle(outs)


def first_step(forward, flat, drifted, m, tags, phi, left):
    return pl.pallas_call(
        first_kernel,
        in_specs=[smem()] + [anywhere()] * 4 + [spec(), spec(), anywhere(), anywhere()],
        out_specs=[anywhere(), anywhere(), spec()],
        out_shape=[shape(NSLOT, CELLS), shape(NSLOT * 2, 128), shape(128, 128)],
        scratch_shapes=field_scratch()
        + [
            pltpu.VMEM((NSLOT, 3 * CELLS), F32),
            pltpu.VMEM((NSLOT * 8, 128), F32),
            pltpu.VMEM((NSLOT, CELLS), F32),
            pltpu.VMEM((NSLOT, 128), BF16),
            pltpu.VMEM((48, NPAD), BF16),
            pltpu.VMEM((NSLOT, CELLS), F32),
            pltpu.VMEM((NSLOT * 2, 128), F32),
            pltpu.VMEM((NPAD, CELLS), BF16),
            pltpu.VMEM((NPAD, CELLS), BF16),
            pltpu.SemaphoreType.DMA((2,)),
            pltpu.SemaphoreType.DMA((2 * PARTS,)),
            pltpu.SemaphoreType.DMA((PARTS + 1,)),
        ],
        compiler_params=params(),
        cost_estimate=cost(FIRST_COST),
        name="first_step",
    )(forward, flat, *drifted, m, tags, phi, left)


def inflow_kernel(dir_ref, halo_any, m_ref, out_ref, flux, sems):
    copies = fetch(sems, (halo_any.at[pl.ds(HALO, 32)], flux))
    out_ref[...] = m_ref[...]
    row = column_of(dir_ref[0], 0) * 2
    settle(copies)
    for half in range(2):
        for k in range(2):
            at = pl.ds(64 * k + row + half, 8, stride=8)
            out_ref[at, :] = m_ref[at, :] + flux[pl.ds((half * 2 + k) * 8, 8), :]


def inflow(forward, halo, m):
    return pl.pallas_call(
        inflow_kernel,
        in_specs=[smem(), anywhere(), spec()],
        out_specs=spec(),
        out_shape=shape(128, 128),
        scratch_shapes=[pltpu.VMEM((32, 128), F32), pltpu.SemaphoreType.DMA((1,))],
        compiler_params=params(53),
        name="inflow",
    )(forward, halo, m)


def second_kernel(
    dir_ref, h_any, halo_any, d0_any, d1_any, d2_any, m0_ref, tag_ref, phi_any, out_any, pre_any, heat_ref,
    right, keep, table, prod, h, halo, drifted, phi, cx, out_ref, pre_ref, sems, part_sems, out_sems,
):
    forward = dir_ref[0]
    copies = fetch(sems, (phi_any, phi), (halo_any.at[pl.ds(0, HALO)], halo))
    parts = fetch_parts(part_sems, PIECES[1], (d0_any, d1_any, d2_any), drifted, h_any, h, 1)
    heat = put_fields(forward, m0_ref, tag_ref, right, keep, table)
    put_heat(heat, table, heat_ref)
    copies[0].wait()
    products(4, phi, right, prod)
    cx[...] = coefs_of(phi[...], 1)
    copies[1].wait()

    def column(i, hf, first, step):
        rows = pl.ds(first, step)
        state = h[rows, pl.ds(i * COL + hf * 128, 128)]
        if i == 0:
            state = state + cx[rows, :] * halo[pl.ds(first * 2 + hf, step, stride=2), :]
        return state

    def put(i, hf, first, step, new):
        out_ref[pl.ds(first * 8 + hf * 4 + column_of(forward, i), step, stride=8), :] = new
        if i == 0:
            pre_ref[pl.ds(first * 2 + hf, step, stride=2), :] = new

    size = NSLOT // PARTS
    outs = []
    for p in range(PARTS):
        settle(parts[p])
        sweep(column, drifted, keep, prod, put, p * size, p * size + size)
        rows = pl.ds(p * size * 8, size * 8)
        outs.append(pltpu.make_async_copy(out_ref.at[rows], out_any.at[rows], out_sems.at[p]))
        outs[-1].start()
    outs.append(pltpu.make_async_copy(pre_ref, pre_any, out_sems.at[PARTS]))
    outs[-1].start()
    settle(outs)


def second_step(forward, h, halo, drifted, m, tags, phi):
    return pl.pallas_call(
        second_kernel,
        in_specs=[smem()] + [anywhere()] * 5 + [spec(), spec(), anywhere()],
        out_specs=[anywhere(), anywhere(), spec()],
        out_shape=[shape(NSLOT * 8, 128), shape(NSLOT * 2, 128), shape(4, 2, 32)],
        scratch_shapes=field_scratch()
        + [
            pltpu.VMEM((NSLOT, 3 * CELLS), F32),
            pltpu.VMEM((NSLOT, CELLS), F32),
            pltpu.VMEM((NSLOT * 2, 128), F32),
            pltpu.VMEM((NSLOT, CELLS), F32),
            pltpu.VMEM((NSLOT, 128), BF16),
            pltpu.VMEM((NSLOT, 128), F32),
            pltpu.VMEM((NSLOT * 8, 128), F32),
            pltpu.VMEM((NSLOT * 2, 128), F32),
            pltpu.SemaphoreType.DMA((2,)),
            pltpu.SemaphoreType.DMA((2 * PARTS,)),
            pltpu.SemaphoreType.DMA((PARTS + 1,)),
        ],
        compiler_params=params(),
        cost_estimate=cost(SECOND_COST),
        name="second_step",
    )(forward, h, halo, *drifted, m, tags, phi)


def last_kernel(dir_ref, h_any, pre_any, halo_any, phi_any, out_any, pre, halo, phi, sems, out_sems):
    del h_any
    size = HALO // PARTS
    spans = [pl.ds(p * size, size) for p in range(PARTS)]
    pairs = [(phi_any, phi)]
    for rows in spans:
        pairs += [(pre_any.at[rows], pre.at[rows]), (halo_any.at[rows], halo.at[rows])]
    copies = fetch(sems, *pairs)
    copies[0].wait()
    cx = coefs_of(phi[...], 1)
    column = column_rows(out_any, column_of(dir_ref[0], 0))
    outs = []
    for p, rows in enumerate(spans):
        settle(copies[1 + 2 * p : 3 + 2 * p])
        part = cx[p * (size // 2) : (p + 1) * (size // 2)]
        for half in range(2):
            at = pl.ds(p * size + half, size // 2, stride=2)
            pre[at, :] = pre[at, :] + part * halo[at, :]
        outs.append(pltpu.make_async_copy(pre.at[rows], column.at[rows], out_sems.at[p]))
        outs[-1].start()
    settle(outs)


def last(forward, h, pre, halo, phi):
    return pl.pallas_call(
        last_kernel,
        in_specs=[smem()] + [anywhere()] * 4,
        out_specs=anywhere(),
        out_shape=shape(NSLOT * 8, 128),
        input_output_aliases={1: 0},
        scratch_shapes=[
            pltpu.VMEM((NSLOT * 2, 128), F32),
            pltpu.VMEM((NSLOT * 2, 128), F32),
            pltpu.VMEM((NSLOT, 128), BF16),
            pltpu.SemaphoreType.DMA((1 + 2 * PARTS,)),
            pltpu.SemaphoreType.DMA((PARTS,)),
        ],
        compiler_params=params(),
        name="last",
    )(forward, h, pre, halo, phi)


def body(state, velocity_order, wall_tag):
    forward = upstream_first().reshape(1)
    at = lax.axis_index("space").astype(jnp.int32).reshape(1)
    flat = state.reshape(NSLOT, 4, 2, 128).transpose(0, 2, 1, 3).reshape(NSLOT * 8, 128)
    near, m, left, phi = unpack(forward, flat, velocity_order)
    drifted = [drift(forward, phi, piece, flat) for piece in PIECES[0]]
    m, drifted[0] = lax.optimization_barrier((over_y(m), drifted[0]))
    (near,) = hold(m, near)
    near = downstream(near)
    tags = strip_tags(at, jnp.transpose(wall_tag, (1, 2, 0)).reshape(64, 64))
    m, drifted = over_rest(over_x(m), *drifted)
    h1, edge, m = first_step(forward, flat, drifted, m, tags, phi, left)
    drifted = [drift(forward, phi, piece, h1, near) for piece in PIECES[1]]
    m, drifted[0] = lax.optimization_barrier((over_y(inflow(forward, near, m)), drifted[0]))
    m, drifted[1] = lax.optimization_barrier((over_x(m), drifted[1]))
    (edge,) = hold(m, edge)
    edge = downstream(edge)
    m, drifted = over_rest(m, *drifted)
    out, pre, wall_heat = second_step(forward, h1, near, drifted, m, tags, phi)
    out = last(forward, out, pre, edge, phi)
    state_next = out.reshape(NSLOT, 2, 4, 128).transpose(0, 2, 1, 3).reshape(NSLOT, 4, 256)
    return state_next, wall_heat


def solution(mesh):
    return jax.shard_map(
        body,
        mesh=mesh,
        in_specs=(P("vel", "space", None), P("vel"), P()),
        out_specs=(P("vel", "space", None), P("space", None, None)),
        check_vma=False,
    )
```

```python
import math

import jax
import jax.numpy as jnp
import numpy as np
from jax import lax
from jax.experimental import pallas as pl
from jax.experimental.pallas import tpu as pltpu
from jax.sharding import PartitionSpec as P

NV1 = 24
NSLOT = 864
NPAD = 896
CELLS = 1024
COL = 256
SPACING = 12.0 / NV1
TOP = (NV1 - 1) * 0.5 * SPACING
KD = 0.3 / TOP
DT = 0.3 / (8 * TOP)
WEIGHT = SPACING**3 / (2.0 * math.pi) ** 1.5
LOG2E = 1.0 / math.log(2.0)
WALL_T = [[b * (0.7 + 0.3 * level) for level in range(3)] for b in (1.4, 0.7)]
AXES = ("vel", "space")
F32 = jnp.float32
BF16 = jnp.bfloat16


def wall_norms():
    line = (2 * np.arange(NV1) - (NV1 - 1)) * 0.5 * SPACING
    cx, cy, cz = np.meshgrid(line, line, line, indexing="ij")
    sq = cx**2 + cy**2 + cz**2
    mass, energy = [], []
    for side in range(2):
        out = np.maximum(cz if side == 0 else -cz, 0.0) * WEIGHT
        prof = [out * t**-1.5 * np.exp(-sq / (2.0 * t)) for t in WALL_T[side]]
        mass.append([float(p.sum()) for p in prof])
        energy.append([float((p * 0.5 * sq).sum()) for p in prof])
    return mass, energy


MASS, ENERGY = wall_norms()


def device_of(i):
    v, s = divmod(i, 16)
    x, r = divmod(v, 4)
    return x, r >> 1, r & 1, s


def index_of(x, y, core, s):
    return ((x % 4 * 2 + y % 2) * 2 + core % 2) * 16 + s % 16


def permute(value, move):
    return lax.ppermute(value, AXES, [(i, index_of(*move(*device_of(i)))) for i in range(256)])


def downstream(value):
    return permute(value, lambda x, y, c, s: (x, y, c, s - 1 if x < 2 else s + 1))


def over_y(part):
    return part + permute(part, lambda x, y, c, s: (x, y ^ 1, c, s))


def over_x(part):
    return part + permute(part, lambda x, y, c, s: (x ^ 1, y, c, s))


def over_rest(part, *work):
    part = part + permute(part, lambda x, y, c, s: (x ^ 2, y, c, s))
    part, *work = lax.optimization_barrier((part, *work))
    return part + permute(part, lambda x, y, c, s: (x, y, c ^ 1, s)), work


def hold(token, *values):
    def kernel(*refs):
        del refs

    place = pl.BlockSpec(memory_space=pl.ANY)
    return pl.pallas_call(
        kernel,
        in_specs=[spec()] + [place] * len(values),
        out_specs=[place] * len(values),
        out_shape=[shape(*v.shape) for v in values],
        input_output_aliases={k + 1: k for k in range(len(values))},
        compiler_params=params(53),
        cost_estimate=cost(HOLD_COST),
        name="hold",
    )(token, *values)


def upstream_first():
    return (lax.axis_index("vel") >= 8).astype(jnp.int32)


def column_of(forward, i):
    return jnp.where(forward == 1, i, 3 - i)


def spec():
    return pl.BlockSpec(memory_space=pltpu.VMEM)


def anywhere():
    return pl.BlockSpec(memory_space=pltpu.HBM)


def smem():
    return pl.BlockSpec(memory_space=pltpu.SMEM)


def params(mib=63.5):
    return pltpu.CompilerParams(vmem_limit_bytes=int(mib * 2**20))


def cost(us):
    return pl.CostEstimate(flops=int(us * 1.15e9), bytes_accessed=10_000, transcendentals=0)


def shape(*dims, dtype=F32):
    return jax.ShapeDtypeStruct(dims, dtype)


def settle(copies):
    for copy in copies:
        copy.wait()


def fetch(sems, *pairs):
    copies = [pltpu.make_async_copy(src, dst, sems.at[k]) for k, (src, dst) in enumerate(pairs)]
    for copy in copies:
        copy.start()
    return copies


def high(a):
    return a.astype(BF16).astype(F32)


def velocity_rows(order_ref, padded):
    padded[...] = jnp.zeros((1, NPAD), jnp.int32)
    padded[:, pl.ds(0, NSLOT)] = order_ref[...].reshape(1, NSLOT)
    order = padded[...]
    upper = (order * 43691) >> 20
    kx = (upper * 43691) >> 20
    ky = upper - kx * NV1
    kz = order - upper * NV1
    live = (lax.broadcasted_iota(jnp.int32, (1, NPAD), 1) < NSLOT).astype(F32)

    def coordinate(k):
        return (2 * k - (NV1 - 1)).astype(F32) * (0.5 * SPACING) * live

    cx, cy, cz = coordinate(kx), coordinate(ky), coordinate(kz)
    sq = cx * cx + cy * cy + cz * cz
    phi = [live, cx, cy, cz, cx * cx, cy * cy, cz * cz, cx * cy, cx * cz, cy * cz, cx * sq, cy * sq, cz * sq]
    return cx, cy, cz, sq, phi


def put_left(order_ref, padded, table, left_ref):
    _, _, cz, sq, phi = velocity_rows(order_ref, padded)
    zero = jnp.zeros_like(cz)
    down, up = jnp.maximum(-cz, 0.0), jnp.maximum(cz, 0.0)
    sums = phi + [down, down * (0.5 * sq), zero] + [zero] * 5 + [up, up * (0.5 * sq), zero]
    for r, a in enumerate(sums):
        table[pl.ds(r, 1), :] = high(a)
        table[pl.ds(24 + r, 1), :] = a - high(a)
    left_ref[...] = table[pl.ds(0, 48), :].astype(BF16)


def put_phi(order_ref, padded, table, phi_ref):
    cx, cy, cz, sq, phi = velocity_rows(order_ref, padded)
    zero = jnp.zeros_like(cx)
    down, up = jnp.maximum(-cz, 0.0), jnp.maximum(cz, 0.0)
    ghost = []
    for side, out in ((0, up), (1, down)):
        ghost += [out * KD * jnp.exp(sq * (-0.5 / t)) for t in WALL_T[side]]
    rows = []
    for _ in range(3):
        rows += [high(a) for a in phi] + [zero] * 3
    for _ in range(2):
        rows += [a - high(a) for a in phi] + [zero] * 3
    rows += [high(a) for a in ghost] + [high(a - high(a)) for a in ghost] + [zero] * 4
    rows += [high(a) for a in ghost] + [zero] * 10
    rows += [jnp.abs(cx), jnp.maximum(cy, 0.0), jnp.maximum(-cy, 0.0), up, down]
    rows += [jnp.abs(cx) + jnp.abs(cy) + jnp.abs(cz)] + [zero] * 10
    for r, a in enumerate(rows):
        table[pl.ds(r, 1), :] = a
    turned = table[...].T.astype(BF16)
    phi_ref[...] = turned[:NSLOT]


def coefs_of(phi, kinds):
    row = lax.broadcasted_iota(jnp.int32, (128, 128 * kinds), 0)
    lane = lax.broadcasted_iota(jnp.int32, (128, 128 * kinds), 1)
    kind, z = lane >> 7, lane & 7
    drop = ((kind == 3) & (z == 0)) | ((kind == 4) & (z == 7))
    pick = ((row == 112 + kind) & jnp.logical_not(drop)).astype(F32).astype(BF16)
    return jnp.dot(phi, pick, preferred_element_type=F32) * KD


def clear_tail(high_ref, low_ref):
    tail = jnp.zeros((NPAD - NSLOT, high_ref.shape[1]), BF16)
    high_ref[pl.ds(NSLOT, NPAD - NSLOT), :] = tail
    low_ref[pl.ds(NSLOT, NPAD - NSLOT), :] = tail


def sums_of(left, high, low):
    total = jnp.dot(left, high, preferred_element_type=F32) + jnp.dot(left, low, preferred_element_type=F32)
    total = total[:24] + total[24:]
    sub = lax.broadcasted_iota(jnp.int32, (8, 128), 0)
    lane = lax.broadcasted_iota(jnp.int32, (8, 128), 1)
    top = (sub >= 5) & ((lane & 7) >= 4)
    out = []
    for half in range(2):
        part = total[:, half * 128 : half * 128 + 128]
        out.append((part[0:8], jnp.where(top, part[16:24], part[8:16])))
    return out


def put_moments(forward, left_ref, high_ref, low_ref, out_ref):
    left = left_ref[...]
    for i in range(4):
        cols = pl.ds(i * COL, COL)
        row = column_of(forward, i) * 2
        for half, (low, mid) in enumerate(sums_of(left, high_ref[:, cols], low_ref[:, cols])):
            out_ref[pl.ds(row + half, 8, stride=8), :] = low
            out_ref[pl.ds(64 + row + half, 8, stride=8), :] = mid


def split_into(value, rows, cols, high_ref, low_ref):
    high = value.astype(BF16)
    high_ref[rows, cols] = high
    low_ref[rows, cols] = (value - high.astype(F32)).astype(BF16)


PARTS = 3
HALO = 2 * NSLOT
PIECES = (((0, 288), (288, 576)), ((0, 192), (192, 192), (384, 480)))
FIRST_COST, SECOND_COST, HOLD_COST = 5, 2, 3
DRIFT_COST = 3


def column_rows(ref, col):
    return ref.reshape(NSLOT * 2, 4, 128).at[:, col, :]


def unpack_kernel(
    dir_ref, in_ref, order_ref, near_any, m_ref, left_any, phi_any,
    left_ref, phi_ref, flux, whole, high_ref, low_ref, table, padded, sems, out_sems,
):
    forward = dir_ref[0]
    size = NSLOT // PARTS
    spans = [pl.ds(p * size * 8, size * 8) for p in range(PARTS)]
    copies = fetch(sems, *[(in_ref.at[a], whole.at[a]) for a in spans])
    put_phi(order_ref, padded, table, phi_ref)
    put_left(order_ref, padded, table, left_ref)
    clear_tail(high_ref, low_ref)
    step = 96

    for p in range(PARTS):
        copies[p].wait()

        def body(k, carry):
            first = pl.multiple_of(p * size + k * step, 16)
            rows = pl.ds(first, step)
            for i in range(4):
                for half in range(2):
                    start = first * 8 + half * 4 + column_of(forward, i)
                    part = whole[pl.ds(start, step, stride=8), :]
                    split_into(part, rows, pl.ds(i * COL + half * 128, 128), high_ref, low_ref)
            return carry

        lax.fori_loop(0, size // step, body, 0)
    col = column_of(forward, 3)
    near = column_rows(whole, col)
    outs = fetch(out_sems, (near, near_any.at[pl.ds(0, HALO)]), (left_ref, left_any), (phi_ref, phi_any))
    put_moments(forward, left_ref, high_ref, low_ref, m_ref)
    cx = coefs_of(phi_ref[...], 1)
    for half in range(2):
        share = cx * whole[pl.ds(half * 4 + col, NSLOT, stride=8), :]
        split_into(share, pl.ds(0, NSLOT), pl.ds(half * 128, 128), high_ref, low_ref)
    cols = pl.ds(0, COL)
    for half, parts in enumerate(sums_of(left_ref[...], high_ref[:, cols], low_ref[:, cols])):
        for k, part in enumerate(parts):
            flux[pl.ds((half * 2 + k) * 8, 8), :] = part
    outs += [pltpu.make_async_copy(flux, near_any.at[pl.ds(HALO, 32)], out_sems.at[3])]
    outs[-1].start()
    settle(outs)


def unpack(forward, flat, order):
    return pl.pallas_call(
        unpack_kernel,
        in_specs=[smem(), anywhere(), spec()],
        out_specs=[anywhere(), spec(), anywhere(), anywhere()],
        out_shape=[
            shape(HALO + 32, 128), shape(128, 128), shape(48, NPAD, dtype=BF16), shape(NSLOT, 128, dtype=BF16)
        ],
        scratch_shapes=[
            pltpu.VMEM((48, NPAD), BF16),
            pltpu.VMEM((NSLOT, 128), BF16),
            pltpu.VMEM((32, 128), F32),
            pltpu.VMEM((NSLOT * 8, 128), F32),
            pltpu.VMEM((NPAD, CELLS), BF16),
            pltpu.VMEM((NPAD, CELLS), BF16),
            pltpu.VMEM((128, NPAD), F32),
            pltpu.VMEM((1, NPAD), jnp.int32),
            pltpu.SemaphoreType.DMA((PARTS,)),
            pltpu.SemaphoreType.DMA((4,)),
        ],
        compiler_params=params(),
        name="unpack",
    )(forward, flat, order)


def strip_tags(at_ref, tag_ref):
    row = lax.broadcasted_iota(jnp.int32, (8, 64), 0)
    x = lax.broadcasted_iota(jnp.int32, (8, 64), 1)
    strip = (x == at_ref[0] * 4 + (row >> 1)).astype(F32).astype(BF16)
    picked = lax.dot_general(
        strip, tag_ref[...].astype(F32).astype(BF16), (((1,), (1,)), ((), ())), preferred_element_type=F32
    )
    row = lax.broadcasted_iota(jnp.int32, (64, COL), 0)
    lane = lax.broadcasted_iota(jnp.int32, (64, COL), 1)
    spread = row == ((lane >> 2) & 1) * 32 + (lane >> 3)
    spread = jnp.dot(picked.astype(BF16), spread.astype(F32).astype(BF16), preferred_element_type=F32)
    odd = (lax.broadcasted_iota(jnp.int32, (8, 128), 0) & 1) == 1
    return jnp.where(odd, spread[:, 128:], spread[:, :128]).astype(jnp.int32)


def put_fields(forward, m_ref, at_ref, tag_ref, right_ref, keep_ref, table):
    m = [m_ref[pl.ds(f * 8, 8), :] * WEIGHT for f in range(15)]
    rho = m[0]
    inv = 1.0 / rho
    u = [a * inv for a in m[1:4]]
    energy = m[4] + m[5] + m[6]
    usq = u[0] * u[0] + u[1] * u[1] + u[2] * u[2]
    temp = (energy * inv - usq) * (1.0 / 3.0)
    stress = [[m[4], m[7], m[8]], [m[7], m[5], m[9]], [m[8], m[9], m[6]]]
    q = []
    for i in range(3):
        pu = stress[i][0] * u[0] + stress[i][1] * u[1] + stress[i][2] * u[2]
        q.append(0.5 * (m[10 + i] - 2.0 * pu - u[i] * energy + 2.0 * rho * usq * u[i]))
    log_t = jnp.log(temp)
    inv_t = 1.0 / temp
    rate = (DT / 0.05) * rho * jnp.exp(0.19 * log_t)
    amp = rate * rho * jnp.exp(-1.5 * log_t)
    half = (0.5 * LOG2E) * inv_t
    zero = jnp.zeros_like(rho)
    expo = [-half * usq] + [2.0 * half * a for a in u] + [-half] * 3 + [zero] * 9
    scale = inv * inv_t * inv_t * (1.0 / 15.0)
    a = [b * scale for b in q]
    s0 = u[0] * a[0] + u[1] * a[1] + u[2] * a[2]
    s1 = usq * inv_t - 5.0
    poly = [amp * (1.0 - s0 * s1)]
    poly += [amp * (a[i] * s1 + 2.0 * s0 * u[i] * inv_t) for i in range(3)]
    front = amp * inv_t
    poly += [-front * (2.0 * a[i] * u[i] + s0) for i in range(3)]
    poly += [-2.0 * front * (a[i] * u[j] + a[j] * u[i]) for i, j in ((0, 1), (0, 2), (1, 2))]
    poly += [front * a[i] for i in range(3)] + [zero] * 3
    z = lax.broadcasted_iota(jnp.int32, (8, 128), 1) & 7
    tag = strip_tags(at_ref, tag_ref)
    density, heat = zero, zero
    walls = []
    for side, at in ((0, 0), (1, 7)):
        for level in range(3):
            here = (z == at) & (tag == level)
            n = jnp.where(here, m[13] * (1.0 / MASS[side][level]), 0.0)
            heat = jnp.where(here, n * ENERGY[side][level] - m[14], heat)
            walls.append(n * WALL_T[side][level] ** -1.5)
    for r, c in enumerate(expo + poly + walls + [zero] * 10):
        table[pl.ds(r * 8, 8), :] = c
    table[pl.ds(384, 8), :] = rate
    n = 4
    right_ref[...] = jnp.zeros(right_ref.shape, BF16)

    def pieces(value, count):
        out = []
        for _ in range(count):
            piece = value.astype(BF16)
            out.append(piece)
            value = value - piece.astype(F32)
        return out

    for k in range(n):
        col = column_of(forward, k)
        for hf in range(2):
            j = col * 2 + hf
            at = k * COL + hf * 128
            keep_ref[pl.ds(k * 2 + hf, 1), :] = table[pl.ds(384 + j, 1), :]
            for kind in range(2):
                lanes = pl.ds(kind * n * COL + at, 128)
                first, second, third = pieces(table[pl.ds(kind * 128 + j, 16, stride=8), :], 3)
                for g, piece in enumerate((first, second, third, first, second)):
                    right_ref[pl.ds(g * 16, 16), lanes] = piece
            wall = table[pl.ds(256 + j, 16, stride=8), :]
            twice = table[pl.ds(256 + j, 6, stride=8), :]
            twice = jnp.concatenate([twice, twice, jnp.zeros((4, 128), F32)], axis=0)
            lanes = pl.ds(2 * n * COL + at, 128)
            right_ref[pl.ds(80, 16), lanes] = pieces(twice, 1)[0]
            right_ref[pl.ds(96, 16), lanes] = pieces(wall, 2)[1]
    return heat


def field_scratch():
    return [pltpu.VMEM((128, 3 * CELLS), BF16), pltpu.VMEM((8, 128), F32), pltpu.VMEM((392, 128), F32)]


def put_heat(heat, table, out_ref):
    lane = lax.broadcasted_iota(jnp.int32, (128, 64), 0)
    to = lax.broadcasted_iota(jnp.int32, (128, 64), 1)
    pick = (lane == (to & 15) * 8 + 7 * (to >> 5)).astype(F32).astype(BF16)
    total = jnp.zeros((8, 64), F32)
    for _ in range(3):
        piece = heat.astype(BF16)
        total = total + jnp.dot(piece, pick, preferred_element_type=F32)
        heat = heat - piece.astype(F32)
    odd = lax.broadcasted_iota(jnp.int32, (8, 64), 0) & 1
    half = (lax.broadcasted_iota(jnp.int32, (8, 64), 1) >> 4) & 1
    total = jnp.where(odd == half, total, 0.0)
    table[pl.ds(0, 8), pl.ds(0, 64)] = total
    for x in range(4):
        for side in range(2):
            lanes = pl.ds(side * 32, 32)
            out_ref[x, pl.ds(side, 1), :] = table[pl.ds(2 * x, 1), lanes] + table[pl.ds(2 * x + 1, 1), lanes]


def products(n, phi_ref, right_ref, prod):
    phi = phi_ref[...]
    for k in range(3 * n):
        cols = pl.ds(k * COL, COL)
        prod[:, cols] = jnp.dot(phi, right_ref[:, cols], preferred_element_type=F32)


def drift_of(coefs, h, upwind):
    cx, cyp, cym, czp, czm, spill = coefs
    lane = lax.broadcasted_iota(jnp.int32, (1, 128), 1)
    plus = [pltpu.roll(a, 8, 1) for a in h]
    minus = [pltpu.roll(a, 120, 1) for a in h]
    out = []
    for hf in range(2):
        before = jnp.where(lane < 8, plus[1 - hf], plus[hf])
        after = jnp.where(lane >= 120, minus[1 - hf], minus[hf])
        new = h[hf] - spill * h[hf]
        new = new + (cyp * before + cym * after)
        new = new + (czp * pltpu.roll(h[hf], 1, 1) + czm * pltpu.roll(h[hf], 127, 1))
        if upwind is not None:
            new = new + cx * upwind[hf]
        out.append(new)
    return out


def read_coefs(coef_ref, rows):
    return [coef_ref[rows, pl.ds(c * 128, 128)] for c in range(6)]


def drift_kernel(dir_ref, phi_any, *refs, start, size, first_step):
    steps = size // 3
    if first_step:
        state_any, out_any, phi, state, out, coef, sems, out_sems = refs
        spans = [(pl.ds((start + q * steps) * 8, steps * 8), pl.ds(q * steps * 8, steps * 8)) for q in range(3)]
        pairs = [[(state_any.at[a], state.at[b])] for a, b in spans]
    else:
        state_any, halo_any, out_any, phi, state, halo, out, coef, sems, out_sems = refs
        spans = [(pl.ds(start + q * steps, steps), pl.ds(q * steps, steps)) for q in range(3)]
        pairs = [[(state_any.at[a], state.at[b])] for a, b in spans]
        pairs[0].append((halo_any.at[pl.ds(start * 2, size * 2)], halo))
    flat_pairs = [(phi_any.at[pl.ds(start, size)], phi)] + [pair for group in pairs for pair in group]
    copies = fetch(sems, *flat_pairs)
    forward = dir_ref[0]
    copies[0].wait()
    coef[...] = coefs_of(phi[...], 6)
    step = 32
    at = 1
    outs = []
    for q in range(3):
        settle(copies[at : at + len(pairs[q])])
        at += len(pairs[q])

        def body(k, carry):
            first = pl.multiple_of(q * steps + k * step, step)
            rows = pl.ds(first, step)
            coefs = read_coefs(coef, rows)
            upwind = None
            for i in range(4):
                if first_step:
                    col = column_of(forward, i)
                    h = [state[pl.ds(first * 8 + hf * 4 + col, step, stride=8), :] for hf in range(2)]
                else:
                    h = [state[rows, pl.ds(i * COL + hf * 128, 128)] for hf in range(2)]
                    if i == 0:
                        h = [a + coefs[0] * halo[pl.ds(first * 2 + hf, step, stride=2), :] for hf, a in enumerate(h)]
                for hf, new in enumerate(drift_of(coefs, h, upwind)):
                    out[rows, pl.ds(i * COL + hf * 128, 128)] = new
                upwind = h
            return carry

        lax.fori_loop(0, steps // step, body, 0)
        rows = pl.ds(q * steps, steps)
        outs.append(pltpu.make_async_copy(out.at[rows], out_any.at[rows], out_sems.at[q]))
        outs[-1].start()
    settle(outs)


def drift(forward, phi, piece, *states):
    first_step = len(states) == 1
    start, size = piece

    def kernel(*refs):
        drift_kernel(*refs, start=start, size=size, first_step=first_step)

    if first_step:
        held = [pltpu.VMEM((size * 8, 128), F32)]
    else:
        held = [pltpu.VMEM((size, CELLS), F32), pltpu.VMEM((size * 2, 128), F32)]
    return pl.pallas_call(
        kernel,
        in_specs=[smem()] + [anywhere()] * (1 + len(states)),
        out_specs=anywhere(),
        out_shape=shape(size, CELLS),
        scratch_shapes=[pltpu.VMEM((size, 128), BF16)]
        + held
        + [
            pltpu.VMEM((size, CELLS), F32),
            pltpu.VMEM((size, 768), F32),
            pltpu.SemaphoreType.DMA((5,)),
            pltpu.SemaphoreType.DMA((3,)),
        ],
        compiler_params=params(),
        cost_estimate=cost(DRIFT_COST),
        name="drift",
    )(forward, phi, *states)


def sweep(column, drifted, rate_ref, prod, put, start, stop):
    step = 32

    def body(k, carry):
        first = pl.multiple_of(k * step, step)
        rows = pl.ds(first, step)
        for i in range(4):
            for hf in range(2):
                at = i * COL + hf * 128
                expo = prod[rows, pl.ds(at, 128)]
                poly = prod[rows, pl.ds(CELLS + at, 128)]
                ghost = prod[rows, pl.ds(2 * CELLS + at, 128)]
                new = jnp.exp2(expo) * poly + ghost
                new = new + drifted[rows, pl.ds(at, 128)]
                new = new - rate_ref[pl.ds(2 * i + hf, 1), :] * column(i, hf, first, step)
                put(i, hf, first, step, new)
        return carry

    lax.fori_loop(start // step, stop // step, body, 0)


def fetch_parts(sems, pieces, drifted_any, drifted, state_any, state, scale):
    size = NSLOT // PARTS
    pairs, counts = [], []
    left = list(zip(pieces, drifted_any, strict=True))
    for p in range(PARTS):
        rows = pl.ds(p * size * scale, size * scale)
        group = [(state_any.at[rows], state.at[rows])]
        while left and left[0][0][0] < (p + 1) * size:
            (start, count), ref = left.pop(0)
            group.append((ref, drifted.at[pl.ds(start, count)]))
        pairs += group
        counts.append(len(group))
    copies = fetch(sems, *pairs)
    return [copies[sum(counts[:p]) : sum(counts[: p + 1])] for p in range(PARTS)]


def first_kernel(
    drifted_any, dir_ref, at_ref, in_ref, m0_ref, tag_ref, phi_ref, left_ref, h1_any, edge_any, m_ref,
    right, keep, table, prod, whole, drifted, phi, left, h1, edge, high_ref, low_ref, sems, part_sems, out_sems,
):
    forward = dir_ref[0]
    copies = fetch(sems, (phi_ref, phi), (left_ref, left))
    parts = fetch_parts(part_sems, PIECES[0], drifted_any, drifted, in_ref, whole, 8)
    clear_tail(high_ref, low_ref)
    put_fields(forward, m0_ref, at_ref, tag_ref, right, keep, table)
    settle(copies)
    products(4, phi, right, prod)

    def column(i, hf, first, step):
        return whole[pl.ds(first * 8 + hf * 4 + column_of(forward, i), step, stride=8), :]

    def put(i, hf, first, step, new):
        rows = pl.ds(first, step)
        cols = pl.ds(i * COL + hf * 128, 128)
        h1[rows, cols] = new
        if i == 3:
            edge[pl.ds(first * 2 + hf, step, stride=2), :] = new
        split_into(new, rows, cols, high_ref, low_ref)

    size = NSLOT // PARTS
    outs = []
    for p in range(PARTS):
        settle(parts[p])
        sweep(column, drifted, keep, prod, put, p * size, p * size + size)
        rows = pl.ds(p * size, size)
        outs.append(pltpu.make_async_copy(h1.at[rows], h1_any.at[rows], out_sems.at[p]))
        outs[-1].start()
    outs.append(pltpu.make_async_copy(edge, edge_any, out_sems.at[PARTS]))
    outs[-1].start()
    put_moments(forward, left, high_ref, low_ref, m_ref)
    settle(outs)


def first_step(forward, at, flat, drifted, m, tags, phi, left):
    n = len(drifted)

    def kernel(*refs):
        first_kernel(refs[3 : 3 + n], *refs[:3], *refs[3 + n :])

    return pl.pallas_call(
        kernel,
        in_specs=[smem(), smem()] + [anywhere()] * (1 + n) + [spec(), spec(), anywhere(), anywhere()],
        out_specs=[anywhere(), anywhere(), spec()],
        out_shape=[shape(NSLOT, CELLS), shape(NSLOT * 2, 128), shape(128, 128)],
        scratch_shapes=field_scratch()
        + [
            pltpu.VMEM((NSLOT, 3 * CELLS), F32),
            pltpu.VMEM((NSLOT * 8, 128), F32),
            pltpu.VMEM((NSLOT, CELLS), F32),
            pltpu.VMEM((NSLOT, 128), BF16),
            pltpu.VMEM((48, NPAD), BF16),
            pltpu.VMEM((NSLOT, CELLS), F32),
            pltpu.VMEM((NSLOT * 2, 128), F32),
            pltpu.VMEM((NPAD, CELLS), BF16),
            pltpu.VMEM((NPAD, CELLS), BF16),
            pltpu.SemaphoreType.DMA((2,)),
            pltpu.SemaphoreType.DMA((PARTS + n,)),
            pltpu.SemaphoreType.DMA((PARTS + 1,)),
        ],
        compiler_params=params(53.7),
        cost_estimate=cost(FIRST_COST),
        name="first_step",
    )(forward, at, flat, *drifted, m, tags, phi, left)


def inflow_kernel(dir_ref, halo_any, m_any, out_ref, m_ref, flux, sems):
    copies = fetch(sems, (halo_any.at[pl.ds(HALO, 32)], flux), (m_any, m_ref))
    row = column_of(dir_ref[0], 0) * 2
    settle(copies)
    out_ref[...] = m_ref[...]
    for half in range(2):
        for k in range(2):
            at = pl.ds(64 * k + row + half, 8, stride=8)
            out_ref[at, :] = m_ref[at, :] + flux[pl.ds((half * 2 + k) * 8, 8), :]


def inflow(forward, halo, m):
    return pl.pallas_call(
        inflow_kernel,
        in_specs=[smem(), anywhere(), anywhere()],
        out_specs=spec(),
        out_shape=shape(128, 128),
        scratch_shapes=[pltpu.VMEM((128, 128), F32), pltpu.VMEM((32, 128), F32), pltpu.SemaphoreType.DMA((2,))],
        compiler_params=params(53),
        name="inflow",
    )(forward, halo, m)


def second_kernel(
    drifted_any, dir_ref, at_ref, h_any, halo_any, m0_ref, tag_ref, phi_any, out_any, pre_any, heat_ref,
    right, keep, table, prod, h, halo, drifted, phi, cx, out_ref, pre_ref, sems, part_sems, out_sems,
):
    forward = dir_ref[0]
    copies = fetch(sems, (phi_any, phi), (halo_any.at[pl.ds(0, HALO)], halo))
    parts = fetch_parts(part_sems, PIECES[1], drifted_any, drifted, h_any, h, 1)
    heat = put_fields(forward, m0_ref, at_ref, tag_ref, right, keep, table)
    put_heat(heat, table, heat_ref)
    copies[0].wait()
    products(4, phi, right, prod)
    cx[...] = coefs_of(phi[...], 1)
    copies[1].wait()

    def column(i, hf, first, step):
        rows = pl.ds(first, step)
        state = h[rows, pl.ds(i * COL + hf * 128, 128)]
        if i == 0:
            state = state + cx[rows, :] * halo[pl.ds(first * 2 + hf, step, stride=2), :]
        return state

    def put(i, hf, first, step, new):
        out_ref[pl.ds(first * 8 + hf * 4 + column_of(forward, i), step, stride=8), :] = new
        if i == 0:
            pre_ref[pl.ds(first * 2 + hf, step, stride=2), :] = new

    size = NSLOT // PARTS
    outs = []
    for p in range(PARTS):
        settle(parts[p])
        sweep(column, drifted, keep, prod, put, p * size, p * size + size)
        rows = pl.ds(p * size * 8, size * 8)
        outs.append(pltpu.make_async_copy(out_ref.at[rows], out_any.at[rows], out_sems.at[p]))
        outs[-1].start()
    outs.append(pltpu.make_async_copy(pre_ref, pre_any, out_sems.at[PARTS]))
    outs[-1].start()
    settle(outs)


def second_step(forward, at, h, halo, drifted, m, tags, phi):
    n = len(drifted)

    def kernel(*refs):
        second_kernel(refs[4 : 4 + n], *refs[:4], *refs[4 + n :])

    return pl.pallas_call(
        kernel,
        in_specs=[smem(), smem()] + [anywhere()] * (2 + n) + [spec(), spec(), anywhere()],
        out_specs=[anywhere(), anywhere(), spec()],
        out_shape=[shape(NSLOT * 8, 128), shape(NSLOT * 2, 128), shape(4, 2, 32)],
        scratch_shapes=field_scratch()
        + [
            pltpu.VMEM((NSLOT, 3 * CELLS), F32),
            pltpu.VMEM((NSLOT, CELLS), F32),
            pltpu.VMEM((NSLOT * 2, 128), F32),
            pltpu.VMEM((NSLOT, CELLS), F32),
            pltpu.VMEM((NSLOT, 128), BF16),
            pltpu.VMEM((NSLOT, 128), F32),
            pltpu.VMEM((NSLOT * 8, 128), F32),
            pltpu.VMEM((NSLOT * 2, 128), F32),
            pltpu.SemaphoreType.DMA((2,)),
            pltpu.SemaphoreType.DMA((PARTS + n,)),
            pltpu.SemaphoreType.DMA((PARTS + 1,)),
        ],
        compiler_params=params(53.7),
        cost_estimate=cost(SECOND_COST),
        name="second_step",
    )(forward, at, h, halo, *drifted, m, tags, phi)


def last_kernel(dir_ref, h_any, pre_any, halo_any, phi_any, out_any, pre, halo, phi, sems, out_sems):
    del h_any
    size = HALO // PARTS
    spans = [pl.ds(p * size, size) for p in range(PARTS)]
    pairs = [(phi_any, phi)]
    for rows in spans:
        pairs += [(pre_any.at[rows], pre.at[rows]), (halo_any.at[rows], halo.at[rows])]
    copies = fetch(sems, *pairs)
    copies[0].wait()
    cx = coefs_of(phi[...], 1)
    column = column_rows(out_any, column_of(dir_ref[0], 0))
    outs = []
    for p, rows in enumerate(spans):
        settle(copies[1 + 2 * p : 3 + 2 * p])
        part = cx[p * (size // 2) : (p + 1) * (size // 2)]
        for half in range(2):
            at = pl.ds(p * size + half, size // 2, stride=2)
            pre[at, :] = pre[at, :] + part * halo[at, :]
        outs.append(pltpu.make_async_copy(pre.at[rows], column.at[rows], out_sems.at[p]))
        outs[-1].start()
    settle(outs)


def last(forward, h, pre, halo, phi):
    return pl.pallas_call(
        last_kernel,
        in_specs=[smem()] + [anywhere()] * 4,
        out_specs=anywhere(),
        out_shape=shape(NSLOT * 8, 128),
        input_output_aliases={1: 0},
        scratch_shapes=[
            pltpu.VMEM((NSLOT * 2, 128), F32),
            pltpu.VMEM((NSLOT * 2, 128), F32),
            pltpu.VMEM((NSLOT, 128), BF16),
            pltpu.SemaphoreType.DMA((1 + 2 * PARTS,)),
            pltpu.SemaphoreType.DMA((PARTS,)),
        ],
        compiler_params=params(),
        name="last",
    )(forward, h, pre, halo, phi)


def body(state, velocity_order, wall_tag):
    forward = upstream_first().reshape(1)
    at = lax.axis_index("space").astype(jnp.int32).reshape(1)
    flat = state.reshape(NSLOT, 4, 2, 128).transpose(0, 2, 1, 3).reshape(NSLOT * 8, 128)
    near, m, left, phi = unpack(forward, flat, velocity_order)
    drifted = [drift(forward, phi, piece, flat) for piece in PIECES[0]]
    m, drifted[0] = lax.optimization_barrier((over_y(m), drifted[0]))
    (near,) = hold(m, near)
    near = downstream(near)
    tags = jnp.transpose(wall_tag, (1, 2, 0)).reshape(64, 64)
    m, drifted = over_rest(over_x(m), *drifted)
    h1, edge, m = first_step(forward, at, flat, drifted, m, tags, phi, left)
    drifted = [drift(forward, phi, piece, h1, near) for piece in PIECES[1]]
    m, drifted[0] = lax.optimization_barrier((over_y(inflow(forward, near, m)), drifted[0]))
    m, drifted[1] = lax.optimization_barrier((over_x(m), drifted[1]))
    (edge,) = hold(m, edge)
    edge = downstream(edge)
    m, drifted = over_rest(m, *drifted)
    out, pre, wall_heat = second_step(forward, at, h1, near, drifted, m, tags, phi)
    out = last(forward, out, pre, edge, phi)
    state_next = out.reshape(NSLOT, 2, 4, 128).transpose(0, 2, 1, 3).reshape(NSLOT, 4, 256)
    return state_next, wall_heat


def solution(mesh):
    return jax.shard_map(
        body,
        mesh=mesh,
        in_specs=(P("vel", "space", None), P("vel"), P()),
        out_specs=(P("vel", "space", None), P("space", None, None)),
        check_vma=False,
    )
```

```python
import math

import jax
import jax.numpy as jnp
import numpy as np
from jax import lax
from jax.experimental import pallas as pl
from jax.experimental.pallas import tpu as pltpu
from jax.sharding import PartitionSpec as P

NV1 = 24
NSLOT = 864
NPAD = 896
CELLS = 1024
COL = 256
SPACING = 12.0 / NV1
TOP = (NV1 - 1) * 0.5 * SPACING
KD = 0.3 / TOP
DT = 0.3 / (8 * TOP)
WEIGHT = SPACING**3 / (2.0 * math.pi) ** 1.5
LOG2E = 1.0 / math.log(2.0)
WALL_T = [[b * (0.7 + 0.3 * level) for level in range(3)] for b in (1.4, 0.7)]
AXES = ("vel", "space")
F32 = jnp.float32
BF16 = jnp.bfloat16


def wall_norms():
    line = (2 * np.arange(NV1) - (NV1 - 1)) * 0.5 * SPACING
    cx, cy, cz = np.meshgrid(line, line, line, indexing="ij")
    sq = cx**2 + cy**2 + cz**2
    mass, energy = [], []
    for side in range(2):
        out = np.maximum(cz if side == 0 else -cz, 0.0) * WEIGHT
        prof = [out * t**-1.5 * np.exp(-sq / (2.0 * t)) for t in WALL_T[side]]
        mass.append([float(p.sum()) for p in prof])
        energy.append([float((p * 0.5 * sq).sum()) for p in prof])
    return mass, energy


MASS, ENERGY = wall_norms()


def device_of(i):
    v, s = divmod(i, 16)
    x, r = divmod(v, 4)
    return x, r >> 1, r & 1, s


def index_of(x, y, core, s):
    return ((x % 4 * 2 + y % 2) * 2 + core % 2) * 16 + s % 16


def permute(value, move):
    return lax.ppermute(value, AXES, [(i, index_of(*move(*device_of(i)))) for i in range(256)])


def downstream(value):
    return permute(value, lambda x, y, c, s: (x, y, c, s - 1 if x < 2 else s + 1))


def over_y(part):
    return part + permute(part, lambda x, y, c, s: (x, y ^ 1, c, s))


def over_x(part):
    return part + permute(part, lambda x, y, c, s: (x ^ 1, y, c, s))


def over_rest(part, *work):
    part = part + permute(part, lambda x, y, c, s: (x ^ 2, y, c, s))
    part, *work = lax.optimization_barrier((part, *work))
    return part + permute(part, lambda x, y, c, s: (x, y, c ^ 1, s)), work


def hold(token, *values):
    def kernel(*refs):
        del refs

    place = pl.BlockSpec(memory_space=pl.ANY)
    return pl.pallas_call(
        kernel,
        in_specs=[spec()] + [place] * len(values),
        out_specs=[place] * len(values),
        out_shape=[shape(*v.shape) for v in values],
        input_output_aliases={k + 1: k for k in range(len(values))},
        compiler_params=params(53),
        cost_estimate=cost(HOLD_COST),
        name="hold",
    )(token, *values)


def upstream_first():
    return (lax.axis_index("vel") >= 8).astype(jnp.int32)


def column_of(forward, i):
    return jnp.where(forward == 1, i, 3 - i)


def spec():
    return pl.BlockSpec(memory_space=pltpu.VMEM)


def anywhere():
    return pl.BlockSpec(memory_space=pltpu.HBM)


def smem():
    return pl.BlockSpec(memory_space=pltpu.SMEM)


def params(mib=63.5):
    return pltpu.CompilerParams(vmem_limit_bytes=int(mib * 2**20))


def cost(us):
    return pl.CostEstimate(flops=int(us * 1.15e9), bytes_accessed=10_000, transcendentals=0)


def shape(*dims, dtype=F32):
    return jax.ShapeDtypeStruct(dims, dtype)


def settle(copies):
    for copy in copies:
        copy.wait()


def fetch(sems, *pairs):
    copies = [pltpu.make_async_copy(src, dst, sems.at[k]) for k, (src, dst) in enumerate(pairs)]
    for copy in copies:
        copy.start()
    return copies


def high(a):
    return a.astype(BF16).astype(F32)


def velocity_rows(order_ref, padded):
    padded[...] = jnp.zeros((1, NPAD), jnp.int32)
    padded[:, pl.ds(0, NSLOT)] = order_ref[...].reshape(1, NSLOT)
    order = padded[...]
    upper = (order * 43691) >> 20
    kx = (upper * 43691) >> 20
    ky = upper - kx * NV1
    kz = order - upper * NV1
    live = (lax.broadcasted_iota(jnp.int32, (1, NPAD), 1) < NSLOT).astype(F32)

    def coordinate(k):
        return (2 * k - (NV1 - 1)).astype(F32) * (0.5 * SPACING) * live

    cx, cy, cz = coordinate(kx), coordinate(ky), coordinate(kz)
    sq = cx * cx + cy * cy + cz * cz
    phi = [live, cx, cy, cz, cx * cx, cy * cy, cz * cz, cx * cy, cx * cz, cy * cz, cx * sq, cy * sq, cz * sq]
    return cx, cy, cz, sq, phi


def put_left(order_ref, padded, table, left_ref):
    _, _, cz, sq, phi = velocity_rows(order_ref, padded)
    zero = jnp.zeros_like(cz)
    down, up = jnp.maximum(-cz, 0.0), jnp.maximum(cz, 0.0)
    sums = phi + [down, down * (0.5 * sq), zero] + [zero] * 5 + [up, up * (0.5 * sq), zero]
    for r, a in enumerate(sums):
        table[pl.ds(r, 1), :] = high(a)
        table[pl.ds(24 + r, 1), :] = a - high(a)
    left_ref[...] = table[pl.ds(0, 48), :].astype(BF16)


def put_phi(order_ref, padded, table, phi_ref):
    cx, cy, cz, sq, phi = velocity_rows(order_ref, padded)
    zero = jnp.zeros_like(cx)
    down, up = jnp.maximum(-cz, 0.0), jnp.maximum(cz, 0.0)
    ghost = []
    for side, out in ((0, up), (1, down)):
        ghost += [out * KD * jnp.exp(sq * (-0.5 / t)) for t in WALL_T[side]]
    rows = []
    for _ in range(3):
        rows += [high(a) for a in phi] + [zero] * 3
    for _ in range(2):
        rows += [a - high(a) for a in phi] + [zero] * 3
    rows += [high(a) for a in ghost] + [high(a - high(a)) for a in ghost] + [zero] * 4
    rows += [high(a) for a in ghost] + [zero] * 10
    rows += [jnp.abs(cx), jnp.maximum(cy, 0.0), jnp.maximum(-cy, 0.0), up, down]
    rows += [jnp.abs(cx) + jnp.abs(cy) + jnp.abs(cz)] + [zero] * 10
    for r, a in enumerate(rows):
        table[pl.ds(r, 1), :] = a
    turned = table[...].T.astype(BF16)
    phi_ref[...] = turned[:NSLOT]


def coefs_of(phi, kinds):
    row = lax.broadcasted_iota(jnp.int32, (128, 128 * kinds), 0)
    lane = lax.broadcasted_iota(jnp.int32, (128, 128 * kinds), 1)
    kind, z = lane >> 7, lane & 7
    drop = ((kind == 3) & (z == 0)) | ((kind == 4) & (z == 7))
    pick = ((row == 112 + kind) & jnp.logical_not(drop)).astype(F32).astype(BF16)
    return jnp.dot(phi, pick, preferred_element_type=F32) * KD


def clear_tail(high_ref, low_ref):
    tail = jnp.zeros((NPAD - NSLOT, high_ref.shape[1]), BF16)
    high_ref[pl.ds(NSLOT, NPAD - NSLOT), :] = tail
    low_ref[pl.ds(NSLOT, NPAD - NSLOT), :] = tail


def sums_of(left, high, low):
    total = jnp.dot(left, high, preferred_element_type=F32) + jnp.dot(left, low, preferred_element_type=F32)
    total = total[:24] + total[24:]
    sub = lax.broadcasted_iota(jnp.int32, (8, 128), 0)
    lane = lax.broadcasted_iota(jnp.int32, (8, 128), 1)
    top = (sub >= 5) & ((lane & 7) >= 4)
    out = []
    for half in range(2):
        part = total[:, half * 128 : half * 128 + 128]
        out.append((part[0:8], jnp.where(top, part[16:24], part[8:16])))
    return out


def put_moments(forward, left_ref, high_ref, low_ref, out_ref):
    left = left_ref[...]
    for i in range(4):
        cols = pl.ds(i * COL, COL)
        row = column_of(forward, i) * 2
        for half, (low, mid) in enumerate(sums_of(left, high_ref[:, cols], low_ref[:, cols])):
            out_ref[pl.ds(row + half, 8, stride=8), :] = low
            out_ref[pl.ds(64 + row + half, 8, stride=8), :] = mid


def split_into(value, rows, cols, high_ref, low_ref):
    high = value.astype(BF16)
    high_ref[rows, cols] = high
    low_ref[rows, cols] = (value - high.astype(F32)).astype(BF16)


PARTS = 9
LAST_PARTS = 3
HALO = 2 * NSLOT
PIECES = (((0, 192), (192, 672)), ((0, 192), (192, 192), (384, 480)))
FIRST_COST, SECOND_COST, HOLD_COST = 5, 2, 3
DRIFT_COST = 3


def column_rows(ref, col):
    return ref.reshape(NSLOT * 2, 4, 128).at[:, col, :]


def unpack_kernel(
    dir_ref, in_ref, order_ref, near_any, m_ref, left_any, phi_any,
    left_ref, phi_ref, flux, whole, high_ref, low_ref, table, padded, sems, out_sems,
):
    forward = dir_ref[0]
    size = NSLOT // PARTS
    spans = [pl.ds(p * size * 8, size * 8) for p in range(PARTS)]
    copies = fetch(sems, *[(in_ref.at[a], whole.at[a]) for a in spans])
    put_phi(order_ref, padded, table, phi_ref)
    put_left(order_ref, padded, table, left_ref)
    clear_tail(high_ref, low_ref)
    step = 96

    for p in range(PARTS):
        copies[p].wait()

        def body(k, carry):
            first = pl.multiple_of(p * size + k * step, 16)
            rows = pl.ds(first, step)
            for i in range(4):
                for half in range(2):
                    start = first * 8 + half * 4 + column_of(forward, i)
                    part = whole[pl.ds(start, step, stride=8), :]
                    split_into(part, rows, pl.ds(i * COL + half * 128, 128), high_ref, low_ref)
            return carry

        lax.fori_loop(0, size // step, body, 0)
    col = column_of(forward, 3)
    near = column_rows(whole, col)
    outs = fetch(out_sems, (near, near_any.at[pl.ds(0, HALO)]), (left_ref, left_any), (phi_ref, phi_any))
    put_moments(forward, left_ref, high_ref, low_ref, m_ref)
    cx = coefs_of(phi_ref[...], 1)
    for half in range(2):
        share = cx * whole[pl.ds(half * 4 + col, NSLOT, stride=8), :]
        split_into(share, pl.ds(0, NSLOT), pl.ds(half * 128, 128), high_ref, low_ref)
    cols = pl.ds(0, COL)
    for half, parts in enumerate(sums_of(left_ref[...], high_ref[:, cols], low_ref[:, cols])):
        for k, part in enumerate(parts):
            flux[pl.ds((half * 2 + k) * 8, 8), :] = part
    outs += [pltpu.make_async_copy(flux, near_any.at[pl.ds(HALO, 32)], out_sems.at[3])]
    outs[-1].start()
    settle(outs)


def unpack(forward, flat, order):
    return pl.pallas_call(
        unpack_kernel,
        in_specs=[smem(), anywhere(), spec()],
        out_specs=[anywhere(), spec(), anywhere(), anywhere()],
        out_shape=[
            shape(HALO + 32, 128), shape(128, 128), shape(48, NPAD, dtype=BF16), shape(NSLOT, 128, dtype=BF16)
        ],
        scratch_shapes=[
            pltpu.VMEM((48, NPAD), BF16),
            pltpu.VMEM((NSLOT, 128), BF16),
            pltpu.VMEM((32, 128), F32),
            pltpu.VMEM((NSLOT * 8, 128), F32),
            pltpu.VMEM((NPAD, CELLS), BF16),
            pltpu.VMEM((NPAD, CELLS), BF16),
            pltpu.VMEM((128, NPAD), F32),
            pltpu.VMEM((1, NPAD), jnp.int32),
            pltpu.SemaphoreType.DMA((PARTS,)),
            pltpu.SemaphoreType.DMA((4,)),
        ],
        compiler_params=params(),
        name="unpack",
    )(forward, flat, order)


def strip_tags(at_ref, tag_ref):
    row = lax.broadcasted_iota(jnp.int32, (8, 64), 0)
    x = lax.broadcasted_iota(jnp.int32, (8, 64), 1)
    strip = (x == at_ref[0] * 4 + (row >> 1)).astype(F32).astype(BF16)
    picked = lax.dot_general(
        strip, tag_ref[...].astype(F32).astype(BF16), (((1,), (1,)), ((), ())), preferred_element_type=F32
    )
    row = lax.broadcasted_iota(jnp.int32, (64, COL), 0)
    lane = lax.broadcasted_iota(jnp.int32, (64, COL), 1)
    spread = row == ((lane >> 2) & 1) * 32 + (lane >> 3)
    spread = jnp.dot(picked.astype(BF16), spread.astype(F32).astype(BF16), preferred_element_type=F32)
    odd = (lax.broadcasted_iota(jnp.int32, (8, 128), 0) & 1) == 1
    return jnp.where(odd, spread[:, 128:], spread[:, :128]).astype(jnp.int32)


def put_fields(forward, m_ref, at_ref, tag_ref, right_ref, keep_ref, table):
    m = [m_ref[pl.ds(f * 8, 8), :] * WEIGHT for f in range(15)]
    rho = m[0]
    inv = 1.0 / rho
    u = [a * inv for a in m[1:4]]
    energy = m[4] + m[5] + m[6]
    usq = u[0] * u[0] + u[1] * u[1] + u[2] * u[2]
    temp = (energy * inv - usq) * (1.0 / 3.0)
    stress = [[m[4], m[7], m[8]], [m[7], m[5], m[9]], [m[8], m[9], m[6]]]
    q = []
    for i in range(3):
        pu = stress[i][0] * u[0] + stress[i][1] * u[1] + stress[i][2] * u[2]
        q.append(0.5 * (m[10 + i] - 2.0 * pu - u[i] * energy + 2.0 * rho * usq * u[i]))
    log_t = jnp.log(temp)
    inv_t = 1.0 / temp
    rate = (DT / 0.05) * rho * jnp.exp(0.19 * log_t)
    amp = rate * rho * jnp.exp(-1.5 * log_t)
    half = (0.5 * LOG2E) * inv_t
    zero = jnp.zeros_like(rho)
    expo = [-half * usq] + [2.0 * half * a for a in u] + [-half] * 3 + [zero] * 9
    scale = inv * inv_t * inv_t * (1.0 / 15.0)
    a = [b * scale for b in q]
    s0 = u[0] * a[0] + u[1] * a[1] + u[2] * a[2]
    s1 = usq * inv_t - 5.0
    poly = [amp * (1.0 - s0 * s1)]
    poly += [amp * (a[i] * s1 + 2.0 * s0 * u[i] * inv_t) for i in range(3)]
    front = amp * inv_t
    poly += [-front * (2.0 * a[i] * u[i] + s0) for i in range(3)]
    poly += [-2.0 * front * (a[i] * u[j] + a[j] * u[i]) for i, j in ((0, 1), (0, 2), (1, 2))]
    poly += [front * a[i] for i in range(3)] + [zero] * 3
    z = lax.broadcasted_iota(jnp.int32, (8, 128), 1) & 7
    tag = strip_tags(at_ref, tag_ref)
    density, heat = zero, zero
    walls = []
    for side, at in ((0, 0), (1, 7)):
        for level in range(3):
            here = (z == at) & (tag == level)
            n = jnp.where(here, m[13] * (1.0 / MASS[side][level]), 0.0)
            heat = jnp.where(here, n * ENERGY[side][level] - m[14], heat)
            walls.append(n * WALL_T[side][level] ** -1.5)
    for r, c in enumerate(expo + poly + walls + [zero] * 10):
        table[pl.ds(r * 8, 8), :] = c
    table[pl.ds(384, 8), :] = rate
    n = 4
    right_ref[...] = jnp.zeros(right_ref.shape, BF16)

    def pieces(value, count):
        out = []
        for _ in range(count):
            piece = value.astype(BF16)
            out.append(piece)
            value = value - piece.astype(F32)
        return out

    for k in range(n):
        col = column_of(forward, k)
        for hf in range(2):
            j = col * 2 + hf
            at = k * COL + hf * 128
            keep_ref[pl.ds(k * 2 + hf, 1), :] = table[pl.ds(384 + j, 1), :]
            for kind in range(2):
                lanes = pl.ds(kind * n * COL + at, 128)
                first, second, third = pieces(table[pl.ds(kind * 128 + j, 16, stride=8), :], 3)
                for g, piece in enumerate((first, second, third, first, second)):
                    right_ref[pl.ds(g * 16, 16), lanes] = piece
            wall = table[pl.ds(256 + j, 16, stride=8), :]
            twice = table[pl.ds(256 + j, 6, stride=8), :]
            twice = jnp.concatenate([twice, twice, jnp.zeros((4, 128), F32)], axis=0)
            lanes = pl.ds(2 * n * COL + at, 128)
            right_ref[pl.ds(80, 16), lanes] = pieces(twice, 1)[0]
            right_ref[pl.ds(96, 16), lanes] = pieces(wall, 2)[1]
    return heat


def field_scratch():
    return [pltpu.VMEM((128, 3 * CELLS), BF16), pltpu.VMEM((8, 128), F32), pltpu.VMEM((392, 128), F32)]


def put_heat(heat, table, out_ref):
    lane = lax.broadcasted_iota(jnp.int32, (128, 64), 0)
    to = lax.broadcasted_iota(jnp.int32, (128, 64), 1)
    pick = (lane == (to & 15) * 8 + 7 * (to >> 5)).astype(F32).astype(BF16)
    total = jnp.zeros((8, 64), F32)
    for _ in range(3):
        piece = heat.astype(BF16)
        total = total + jnp.dot(piece, pick, preferred_element_type=F32)
        heat = heat - piece.astype(F32)
    odd = lax.broadcasted_iota(jnp.int32, (8, 64), 0) & 1
    half = (lax.broadcasted_iota(jnp.int32, (8, 64), 1) >> 4) & 1
    total = jnp.where(odd == half, total, 0.0)
    table[pl.ds(0, 8), pl.ds(0, 64)] = total
    for x in range(4):
        for side in range(2):
            lanes = pl.ds(side * 32, 32)
            out_ref[x, pl.ds(side, 1), :] = table[pl.ds(2 * x, 1), lanes] + table[pl.ds(2 * x + 1, 1), lanes]


def products(n, phi_ref, right_ref, prod):
    phi = phi_ref[...]
    for k in range(3 * n):
        cols = pl.ds(k * COL, COL)
        prod[:, cols] = jnp.dot(phi, right_ref[:, cols], preferred_element_type=F32)


def drift_of(coefs, h, upwind):
    cx, cyp, cym, czp, czm, spill = coefs
    lane = lax.broadcasted_iota(jnp.int32, (1, 128), 1)
    plus = [pltpu.roll(a, 8, 1) for a in h]
    minus = [pltpu.roll(a, 120, 1) for a in h]
    out = []
    for hf in range(2):
        before = jnp.where(lane < 8, plus[1 - hf], plus[hf])
        after = jnp.where(lane >= 120, minus[1 - hf], minus[hf])
        new = h[hf] - spill * h[hf]
        new = new + (cyp * before + cym * after)
        new = new + (czp * pltpu.roll(h[hf], 1, 1) + czm * pltpu.roll(h[hf], 127, 1))
        if upwind is not None:
            new = new + cx * upwind[hf]
        out.append(new)
    return out


def read_coefs(coef_ref, rows):
    return [coef_ref[rows, pl.ds(c * 128, 128)] for c in range(6)]


def drift_kernel(dir_ref, phi_any, *refs, start, size, first_step):
    steps = 96
    count = size // steps
    if first_step:
        state_any, out_any, phi, state, out, coef, sems, out_sems = refs
        spans = [(pl.ds((start + q * steps) * 8, steps * 8), pl.ds(q * steps * 8, steps * 8)) for q in range(count)]
        pairs = [[(state_any.at[a], state.at[b])] for a, b in spans]
    else:
        state_any, halo_any, out_any, phi, state, halo, out, coef, sems, out_sems = refs
        spans = [(pl.ds(start + q * steps, steps), pl.ds(q * steps, steps)) for q in range(count)]
        pairs = [[(state_any.at[a], state.at[b])] for a, b in spans]
        pairs[0].append((halo_any.at[pl.ds(start * 2, size * 2)], halo))
    flat_pairs = [(phi_any.at[pl.ds(start, size)], phi)] + [pair for group in pairs for pair in group]
    copies = fetch(sems, *flat_pairs)
    forward = dir_ref[0]
    copies[0].wait()
    coef[...] = coefs_of(phi[...], 6)
    step = 32
    at = 1
    outs = []
    for q in range(count):
        settle(copies[at : at + len(pairs[q])])
        at += len(pairs[q])

        def body(k, carry):
            first = pl.multiple_of(q * steps + k * step, step)
            rows = pl.ds(first, step)
            coefs = read_coefs(coef, rows)
            upwind = None
            for i in range(4):
                if first_step:
                    col = column_of(forward, i)
                    h = [state[pl.ds(first * 8 + hf * 4 + col, step, stride=8), :] for hf in range(2)]
                else:
                    h = [state[rows, pl.ds(i * COL + hf * 128, 128)] for hf in range(2)]
                    if i == 0:
                        h = [a + coefs[0] * halo[pl.ds(first * 2 + hf, step, stride=2), :] for hf, a in enumerate(h)]
                for hf, new in enumerate(drift_of(coefs, h, upwind)):
                    out[rows, pl.ds(i * COL + hf * 128, 128)] = new
                upwind = h
            return carry

        lax.fori_loop(0, steps // step, body, 0)
        rows = pl.ds(q * steps, steps)
        outs.append(pltpu.make_async_copy(out.at[rows], out_any.at[rows], out_sems.at[q]))
        outs[-1].start()
    settle(outs)


def drift(forward, phi, piece, *states):
    first_step = len(states) == 1
    start, size = piece

    def kernel(*refs):
        drift_kernel(*refs, start=start, size=size, first_step=first_step)

    if first_step:
        held = [pltpu.VMEM((size * 8, 128), F32)]
    else:
        held = [pltpu.VMEM((size, CELLS), F32), pltpu.VMEM((size * 2, 128), F32)]
    return pl.pallas_call(
        kernel,
        in_specs=[smem()] + [anywhere()] * (1 + len(states)),
        out_specs=anywhere(),
        out_shape=shape(size, CELLS),
        scratch_shapes=[pltpu.VMEM((size, 128), BF16)]
        + held
        + [
            pltpu.VMEM((size, CELLS), F32),
            pltpu.VMEM((size, 768), F32),
            pltpu.SemaphoreType.DMA((2 + size // 96,)),
            pltpu.SemaphoreType.DMA((size // 96,)),
        ],
        compiler_params=params(),
        cost_estimate=cost(DRIFT_COST),
        name="drift",
    )(forward, phi, *states)


def sweep(column, drifted, rate_ref, prod, put, start, stop):
    step = 32

    def body(k, carry):
        first = pl.multiple_of(k * step, step)
        rows = pl.ds(first, step)
        for i in range(4):
            for hf in range(2):
                at = i * COL + hf * 128
                expo = prod[rows, pl.ds(at, 128)]
                poly = prod[rows, pl.ds(CELLS + at, 128)]
                ghost = prod[rows, pl.ds(2 * CELLS + at, 128)]
                new = jnp.exp2(expo) * poly + ghost
                new = new + drifted[rows, pl.ds(at, 128)]
                new = new - rate_ref[pl.ds(2 * i + hf, 1), :] * column(i, hf, first, step)
                put(i, hf, first, step, new)
        return carry

    lax.fori_loop(start // step, stop // step, body, 0)


def fetch_parts(sems, pieces, drifted_any, drifted, state_any, state, scale):
    size = NSLOT // PARTS
    pairs, counts = [], []
    left = list(zip(pieces, drifted_any, strict=True))
    for p in range(PARTS):
        rows = pl.ds(p * size * scale, size * scale)
        group = [(state_any.at[rows], state.at[rows])]
        while left and left[0][0][0] < (p + 1) * size:
            (start, count), ref = left.pop(0)
            group.append((ref, drifted.at[pl.ds(start, count)]))
        pairs += group
        counts.append(len(group))
    copies = fetch(sems, *pairs)
    return [copies[sum(counts[:p]) : sum(counts[: p + 1])] for p in range(PARTS)]


def first_kernel(
    drifted_any, dir_ref, at_ref, in_ref, m0_ref, tag_ref, phi_ref, left_ref, h1_any, edge_any, m_ref,
    right, keep, table, prod, whole, drifted, phi, left, h1, edge, high_ref, low_ref, sems, part_sems, out_sems,
):
    forward = dir_ref[0]
    copies = fetch(sems, (phi_ref, phi), (left_ref, left))
    parts = fetch_parts(part_sems, PIECES[0], drifted_any, drifted, in_ref, whole, 8)
    clear_tail(high_ref, low_ref)
    put_fields(forward, m0_ref, at_ref, tag_ref, right, keep, table)
    settle(copies)
    products(4, phi, right, prod)

    def column(i, hf, first, step):
        return whole[pl.ds(first * 8 + hf * 4 + column_of(forward, i), step, stride=8), :]

    def put(i, hf, first, step, new):
        rows = pl.ds(first, step)
        cols = pl.ds(i * COL + hf * 128, 128)
        h1[rows, cols] = new
        if i == 3:
            edge[pl.ds(first * 2 + hf, step, stride=2), :] = new
        split_into(new, rows, cols, high_ref, low_ref)

    size = NSLOT // PARTS
    outs = []
    for p in range(PARTS):
        settle(parts[p])
        sweep(column, drifted, keep, prod, put, p * size, p * size + size)
        rows = pl.ds(p * size, size)
        outs.append(pltpu.make_async_copy(h1.at[rows], h1_any.at[rows], out_sems.at[p]))
        outs[-1].start()
    outs.append(pltpu.make_async_copy(edge, edge_any, out_sems.at[PARTS]))
    outs[-1].start()
    put_moments(forward, left, high_ref, low_ref, m_ref)
    settle(outs)


def first_step(forward, at, flat, drifted, m, tags, phi, left):
    n = len(drifted)

    def kernel(*refs):
        first_kernel(refs[3 : 3 + n], *refs[:3], *refs[3 + n :])

    return pl.pallas_call(
        kernel,
        in_specs=[smem(), smem()] + [anywhere()] * (1 + n) + [spec(), spec(), anywhere(), anywhere()],
        out_specs=[anywhere(), anywhere(), spec()],
        out_shape=[shape(NSLOT, CELLS), shape(NSLOT * 2, 128), shape(128, 128)],
        scratch_shapes=field_scratch()
        + [
            pltpu.VMEM((NSLOT, 3 * CELLS), F32),
            pltpu.VMEM((NSLOT * 8, 128), F32),
            pltpu.VMEM((NSLOT, CELLS), F32),
            pltpu.VMEM((NSLOT, 128), BF16),
            pltpu.VMEM((48, NPAD), BF16),
            pltpu.VMEM((NSLOT, CELLS), F32),
            pltpu.VMEM((NSLOT * 2, 128), F32),
            pltpu.VMEM((NPAD, CELLS), BF16),
            pltpu.VMEM((NPAD, CELLS), BF16),
            pltpu.SemaphoreType.DMA((2,)),
            pltpu.SemaphoreType.DMA((PARTS + n,)),
            pltpu.SemaphoreType.DMA((PARTS + 1,)),
        ],
        compiler_params=params(53.7),
        cost_estimate=cost(FIRST_COST),
        name="first_step",
    )(forward, at, flat, *drifted, m, tags, phi, left)


def inflow_kernel(dir_ref, halo_any, m_any, out_ref, m_ref, flux, sems):
    copies = fetch(sems, (halo_any.at[pl.ds(HALO, 32)], flux), (m_any, m_ref))
    row = column_of(dir_ref[0], 0) * 2
    settle(copies)
    out_ref[...] = m_ref[...]
    for half in range(2):
        for k in range(2):
            at = pl.ds(64 * k + row + half, 8, stride=8)
            out_ref[at, :] = m_ref[at, :] + flux[pl.ds((half * 2 + k) * 8, 8), :]


def inflow(forward, halo, m):
    return pl.pallas_call(
        inflow_kernel,
        in_specs=[smem(), anywhere(), anywhere()],
        out_specs=spec(),
        out_shape=shape(128, 128),
        scratch_shapes=[pltpu.VMEM((128, 128), F32), pltpu.VMEM((32, 128), F32), pltpu.SemaphoreType.DMA((2,))],
        compiler_params=params(53),
        name="inflow",
    )(forward, halo, m)


def second_kernel(
    drifted_any, dir_ref, at_ref, h_any, halo_any, m0_ref, tag_ref, phi_any, out_any, pre_any, heat_ref,
    right, keep, table, prod, h, halo, drifted, phi, cx, out_ref, pre_ref, sems, part_sems, out_sems,
):
    forward = dir_ref[0]
    copies = fetch(sems, (phi_any, phi), (halo_any.at[pl.ds(0, HALO)], halo))
    parts = fetch_parts(part_sems, PIECES[1], drifted_any, drifted, h_any, h, 1)
    heat = put_fields(forward, m0_ref, at_ref, tag_ref, right, keep, table)
    copies[0].wait()
    products(4, phi, right, prod)
    cx[...] = coefs_of(phi[...], 1)
    copies[1].wait()

    def column(i, hf, first, step):
        rows = pl.ds(first, step)
        state = h[rows, pl.ds(i * COL + hf * 128, 128)]
        if i == 0:
            state = state + cx[rows, :] * halo[pl.ds(first * 2 + hf, step, stride=2), :]
        return state

    def put(i, hf, first, step, new):
        out_ref[pl.ds(first * 8 + hf * 4 + column_of(forward, i), step, stride=8), :] = new
        if i == 0:
            pre_ref[pl.ds(first * 2 + hf, step, stride=2), :] = new

    size = NSLOT // PARTS
    outs = []
    for p in range(PARTS):
        settle(parts[p])
        sweep(column, drifted, keep, prod, put, p * size, p * size + size)
        rows = pl.ds(p * size * 8, size * 8)
        outs.append(pltpu.make_async_copy(out_ref.at[rows], out_any.at[rows], out_sems.at[p]))
        outs[-1].start()
    outs.append(pltpu.make_async_copy(pre_ref, pre_any, out_sems.at[PARTS]))
    outs[-1].start()
    put_heat(heat, table, heat_ref)
    settle(outs)


def second_step(forward, at, h, halo, drifted, m, tags, phi):
    n = len(drifted)

    def kernel(*refs):
        second_kernel(refs[4 : 4 + n], *refs[:4], *refs[4 + n :])

    return pl.pallas_call(
        kernel,
        in_specs=[smem(), smem()] + [anywhere()] * (2 + n) + [spec(), spec(), anywhere()],
        out_specs=[anywhere(), anywhere(), spec()],
        out_shape=[shape(NSLOT * 8, 128), shape(NSLOT * 2, 128), shape(4, 2, 32)],
        scratch_shapes=field_scratch()
        + [
            pltpu.VMEM((NSLOT, 3 * CELLS), F32),
            pltpu.VMEM((NSLOT, CELLS), F32),
            pltpu.VMEM((NSLOT * 2, 128), F32),
            pltpu.VMEM((NSLOT, CELLS), F32),
            pltpu.VMEM((NSLOT, 128), BF16),
            pltpu.VMEM((NSLOT, 128), F32),
            pltpu.VMEM((NSLOT * 8, 128), F32),
            pltpu.VMEM((NSLOT * 2, 128), F32),
            pltpu.SemaphoreType.DMA((2,)),
            pltpu.SemaphoreType.DMA((PARTS + n,)),
            pltpu.SemaphoreType.DMA((PARTS + 1,)),
        ],
        compiler_params=params(53.7),
        cost_estimate=cost(SECOND_COST),
        name="second_step",
    )(forward, at, h, halo, *drifted, m, tags, phi)


def last_kernel(dir_ref, h_any, pre_any, halo_any, phi_any, out_any, pre, halo, phi, sems, out_sems):
    del h_any
    size = HALO // LAST_PARTS
    spans = [pl.ds(p * size, size) for p in range(LAST_PARTS)]
    pairs = [(phi_any, phi)]
    for rows in spans:
        pairs += [(pre_any.at[rows], pre.at[rows]), (halo_any.at[rows], halo.at[rows])]
    copies = fetch(sems, *pairs)
    copies[0].wait()
    cx = coefs_of(phi[...], 1)
    column = column_rows(out_any, column_of(dir_ref[0], 0))
    outs = []
    for p, rows in enumerate(spans):
        settle(copies[1 + 2 * p : 3 + 2 * p])
        part = cx[p * (size // 2) : (p + 1) * (size // 2)]
        for half in range(2):
            at = pl.ds(p * size + half, size // 2, stride=2)
            pre[at, :] = pre[at, :] + part * halo[at, :]
        outs.append(pltpu.make_async_copy(pre.at[rows], column.at[rows], out_sems.at[p]))
        outs[-1].start()
    settle(outs)


def last(forward, h, pre, halo, phi):
    return pl.pallas_call(
        last_kernel,
        in_specs=[smem()] + [anywhere()] * 4,
        out_specs=anywhere(),
        out_shape=shape(NSLOT * 8, 128),
        input_output_aliases={1: 0},
        scratch_shapes=[
            pltpu.VMEM((NSLOT * 2, 128), F32),
            pltpu.VMEM((NSLOT * 2, 128), F32),
            pltpu.VMEM((NSLOT, 128), BF16),
            pltpu.SemaphoreType.DMA((1 + 2 * LAST_PARTS,)),
            pltpu.SemaphoreType.DMA((LAST_PARTS,)),
        ],
        compiler_params=params(),
        name="last",
    )(forward, h, pre, halo, phi)


def body(state, velocity_order, wall_tag):
    forward = upstream_first().reshape(1)
    at = lax.axis_index("space").astype(jnp.int32).reshape(1)
    flat = state.reshape(NSLOT, 4, 2, 128).transpose(0, 2, 1, 3).reshape(NSLOT * 8, 128)
    near, m, left, phi = unpack(forward, flat, velocity_order)
    drifted = [drift(forward, phi, piece, flat) for piece in PIECES[0]]
    m, drifted[0] = lax.optimization_barrier((over_y(m), drifted[0]))
    (near,) = hold(m, near)
    near = downstream(near)
    tags = jnp.transpose(wall_tag, (1, 2, 0)).reshape(64, 64)
    m, drifted = over_rest(over_x(m), *drifted)
    h1, edge, m = first_step(forward, at, flat, drifted, m, tags, phi, left)
    drifted = [drift(forward, phi, piece, h1, near) for piece in PIECES[1]]
    m, drifted[0] = lax.optimization_barrier((over_y(inflow(forward, near, m)), drifted[0]))
    m, drifted[1] = lax.optimization_barrier((over_x(m), drifted[1]))
    (edge,) = hold(m, edge)
    edge = downstream(edge)
    m, drifted = over_rest(m, *drifted)
    out, pre, wall_heat = second_step(forward, at, h1, near, drifted, m, tags, phi)
    out = last(forward, out, pre, edge, phi)
    state_next = out.reshape(NSLOT, 2, 4, 128).transpose(0, 2, 1, 3).reshape(NSLOT, 4, 256)
    return state_next, wall_heat


def solution(mesh):
    return jax.shard_map(
        body,
        mesh=mesh,
        in_specs=(P("vel", "space", None), P("vel"), P()),
        out_specs=(P("vel", "space", None), P("space", None, None)),
        check_vma=False,
    )
```

```python
import math

import jax
import jax.numpy as jnp
import numpy as np
from jax import lax
from jax.experimental import pallas as pl
from jax.experimental.pallas import tpu as pltpu
from jax.sharding import PartitionSpec as P

NV1 = 24
NSLOT = 864
NPAD = 896
CELLS = 1024
COL = 256
SPACING = 12.0 / NV1
TOP = (NV1 - 1) * 0.5 * SPACING
KD = 0.3 / TOP
DT = 0.3 / (8 * TOP)
WEIGHT = SPACING**3 / (2.0 * math.pi) ** 1.5
LOG2E = 1.0 / math.log(2.0)
WALL_T = [[b * (0.7 + 0.3 * level) for level in range(3)] for b in (1.4, 0.7)]
AXES = ("vel", "space")
F32 = jnp.float32
BF16 = jnp.bfloat16


def wall_norms():
    line = (2 * np.arange(NV1) - (NV1 - 1)) * 0.5 * SPACING
    cx, cy, cz = np.meshgrid(line, line, line, indexing="ij")
    sq = cx**2 + cy**2 + cz**2
    mass, energy = [], []
    for side in range(2):
        out = np.maximum(cz if side == 0 else -cz, 0.0) * WEIGHT
        prof = [out * t**-1.5 * np.exp(-sq / (2.0 * t)) for t in WALL_T[side]]
        mass.append([float(p.sum()) for p in prof])
        energy.append([float((p * 0.5 * sq).sum()) for p in prof])
    return mass, energy


MASS, ENERGY = wall_norms()


def device_of(i):
    v, s = divmod(i, 16)
    x, r = divmod(v, 4)
    return x, r >> 1, r & 1, s


def index_of(x, y, core, s):
    return ((x % 4 * 2 + y % 2) * 2 + core % 2) * 16 + s % 16


def permute(value, move):
    return lax.ppermute(value, AXES, [(i, index_of(*move(*device_of(i)))) for i in range(256)])


def downstream(value):
    return permute(value, lambda x, y, c, s: (x, y, c, s - 1 if x < 2 else s + 1))


def over_y(part):
    return part + permute(part, lambda x, y, c, s: (x, y ^ 1, c, s))


def over_x(part):
    return part + permute(part, lambda x, y, c, s: (x ^ 1, y, c, s))


def over_rest(part, *work):
    part = part + permute(part, lambda x, y, c, s: (x ^ 2, y, c, s))
    part, *work = lax.optimization_barrier((part, *work))
    return part + permute(part, lambda x, y, c, s: (x, y, c ^ 1, s)), work


def hold(token, *values):
    def kernel(*refs):
        del refs

    place = pl.BlockSpec(memory_space=pl.ANY)
    return pl.pallas_call(
        kernel,
        in_specs=[spec()] + [place] * len(values),
        out_specs=[place] * len(values),
        out_shape=[shape(*v.shape) for v in values],
        input_output_aliases={k + 1: k for k in range(len(values))},
        compiler_params=params(53),
        cost_estimate=cost(HOLD_COST),
        name="hold",
    )(token, *values)


def upstream_first():
    return (lax.axis_index("vel") >= 8).astype(jnp.int32)


def column_of(forward, i):
    return jnp.where(forward == 1, i, 3 - i)


def spec():
    return pl.BlockSpec(memory_space=pltpu.VMEM)


def anywhere():
    return pl.BlockSpec(memory_space=pltpu.HBM)


def smem():
    return pl.BlockSpec(memory_space=pltpu.SMEM)


def params(mib=63.5):
    return pltpu.CompilerParams(vmem_limit_bytes=int(mib * 2**20))


def cost(us):
    return pl.CostEstimate(flops=int(us * 1.15e9), bytes_accessed=10_000, transcendentals=0)


def shape(*dims, dtype=F32):
    return jax.ShapeDtypeStruct(dims, dtype)


def settle(copies):
    for copy in copies:
        copy.wait()


def fetch(sems, *pairs):
    copies = [pltpu.make_async_copy(src, dst, sems.at[k]) for k, (src, dst) in enumerate(pairs)]
    for copy in copies:
        copy.start()
    return copies


def high(a):
    return a.astype(BF16).astype(F32)


def velocity_rows(order_ref, padded):
    padded[...] = jnp.zeros((1, NPAD), jnp.int32)
    padded[:, pl.ds(0, NSLOT)] = order_ref[...].reshape(1, NSLOT)
    order = padded[...]
    upper = (order * 43691) >> 20
    kx = (upper * 43691) >> 20
    ky = upper - kx * NV1
    kz = order - upper * NV1
    live = (lax.broadcasted_iota(jnp.int32, (1, NPAD), 1) < NSLOT).astype(F32)

    def coordinate(k):
        return (2 * k - (NV1 - 1)).astype(F32) * (0.5 * SPACING) * live

    cx, cy, cz = coordinate(kx), coordinate(ky), coordinate(kz)
    sq = cx * cx + cy * cy + cz * cz
    phi = [live, cx, cy, cz, cx * cx, cy * cy, cz * cz, cx * cy, cx * cz, cy * cz, cx * sq, cy * sq, cz * sq]
    return cx, cy, cz, sq, phi


def put_left(order_ref, padded, table, left_ref):
    _, _, cz, sq, phi = velocity_rows(order_ref, padded)
    zero = jnp.zeros_like(cz)
    down, up = jnp.maximum(-cz, 0.0), jnp.maximum(cz, 0.0)
    sums = phi + [down, down * (0.5 * sq), zero] + [zero] * 5 + [up, up * (0.5 * sq), zero]
    for r, a in enumerate(sums):
        table[pl.ds(r, 1), :] = high(a)
        table[pl.ds(24 + r, 1), :] = a - high(a)
    left_ref[...] = table[pl.ds(0, 48), :].astype(BF16)


def put_phi(order_ref, padded, table, phi_ref):
    cx, cy, cz, sq, phi = velocity_rows(order_ref, padded)
    zero = jnp.zeros_like(cx)
    down, up = jnp.maximum(-cz, 0.0), jnp.maximum(cz, 0.0)
    ghost = []
    for side, out in ((0, up), (1, down)):
        ghost += [out * KD * jnp.exp(sq * (-0.5 / t)) for t in WALL_T[side]]
    rows = []
    for _ in range(3):
        rows += [high(a) for a in phi] + [zero] * 3
    for _ in range(2):
        rows += [a - high(a) for a in phi] + [zero] * 3
    rows += [high(a) for a in ghost] + [high(a - high(a)) for a in ghost] + [zero] * 4
    rows += [high(a) for a in ghost] + [zero] * 10
    rows += [jnp.abs(cx), jnp.maximum(cy, 0.0), jnp.maximum(-cy, 0.0), up, down]
    rows += [jnp.abs(cx) + jnp.abs(cy) + jnp.abs(cz)] + [zero] * 10
    for r, a in enumerate(rows):
        table[pl.ds(r, 1), :] = a
    turned = table[...].T.astype(BF16)
    phi_ref[...] = turned[:NSLOT]


def coefs_of(phi, kinds):
    row = lax.broadcasted_iota(jnp.int32, (128, 128 * kinds), 0)
    lane = lax.broadcasted_iota(jnp.int32, (128, 128 * kinds), 1)
    kind, z = lane >> 7, lane & 7
    drop = ((kind == 3) & (z == 0)) | ((kind == 4) & (z == 7))
    pick = ((row == 112 + kind) & jnp.logical_not(drop)).astype(F32).astype(BF16)
    return jnp.dot(phi, pick, preferred_element_type=F32) * KD


def clear_tail(high_ref, low_ref):
    tail = jnp.zeros((NPAD - NSLOT, high_ref.shape[1]), BF16)
    high_ref[pl.ds(NSLOT, NPAD - NSLOT), :] = tail
    low_ref[pl.ds(NSLOT, NPAD - NSLOT), :] = tail


def sums_of(left, high, low):
    total = jnp.dot(left, high, preferred_element_type=F32) + jnp.dot(left, low, preferred_element_type=F32)
    total = total[:24] + total[24:]
    sub = lax.broadcasted_iota(jnp.int32, (8, 128), 0)
    lane = lax.broadcasted_iota(jnp.int32, (8, 128), 1)
    top = (sub >= 5) & ((lane & 7) >= 4)
    out = []
    for half in range(2):
        part = total[:, half * 128 : half * 128 + 128]
        out.append((part[0:8], jnp.where(top, part[16:24], part[8:16])))
    return out


def put_moments(forward, left_ref, high_ref, low_ref, out_ref):
    left = left_ref[...]
    for i in range(4):
        cols = pl.ds(i * COL, COL)
        row = column_of(forward, i) * 2
        for half, (low, mid) in enumerate(sums_of(left, high_ref[:, cols], low_ref[:, cols])):
            out_ref[pl.ds(row + half, 8, stride=8), :] = low
            out_ref[pl.ds(64 + row + half, 8, stride=8), :] = mid


def split_into(value, rows, cols, high_ref, low_ref):
    high = value.astype(BF16)
    high_ref[rows, cols] = high
    low_ref[rows, cols] = (value - high.astype(F32)).astype(BF16)


PARTS = 9
LAST_PARTS = 3
HALO = 2 * NSLOT
PIECES = (((0, 192), (192, 672)), ((0, 192), (192, 192), (384, 480)))
FIRST_COST, SECOND_COST, HOLD_COST = 5, 2, 3
DRIFT_COST = 3


def column_rows(ref, col):
    return ref.reshape(NSLOT * 2, 4, 128).at[:, col, :]


def unpack_kernel(
    dir_ref, in_ref, order_ref, near_any, m_ref, left_any, phi_any,
    left_ref, phi_ref, flux, flux_high, flux_low, whole, high_ref, low_ref, table, padded, sems, out_sems,
):
    forward = dir_ref[0]
    size = NSLOT // PARTS
    spans = [pl.ds(p * size * 8, size * 8) for p in range(PARTS)]
    copies = fetch(sems, *[(in_ref.at[a], whole.at[a]) for a in spans])
    put_phi(order_ref, padded, table, phi_ref)
    put_left(order_ref, padded, table, left_ref)
    clear_tail(high_ref, low_ref)
    clear_tail(flux_high, flux_low)
    step = 96

    for p in range(PARTS):
        copies[p].wait()

        def body(k, carry):
            first = pl.multiple_of(p * size + k * step, 16)
            rows = pl.ds(first, step)
            for i in range(4):
                for half in range(2):
                    start = first * 8 + half * 4 + column_of(forward, i)
                    part = whole[pl.ds(start, step, stride=8), :]
                    split_into(part, rows, pl.ds(i * COL + half * 128, 128), high_ref, low_ref)
            return carry

        lax.fori_loop(0, size // step, body, 0)
    col = column_of(forward, 3)
    near = column_rows(whole, col)
    outs = fetch(out_sems, (near, near_any.at[pl.ds(0, HALO)]), (left_ref, left_any), (phi_ref, phi_any))
    cx = coefs_of(phi_ref[...], 1)
    for half in range(2):
        share = cx * whole[pl.ds(half * 4 + col, NSLOT, stride=8), :]
        split_into(share, pl.ds(0, NSLOT), pl.ds(half * 128, 128), flux_high, flux_low)
    for half, parts in enumerate(sums_of(left_ref[...], flux_high[...], flux_low[...])):
        for k, part in enumerate(parts):
            flux[pl.ds((half * 2 + k) * 8, 8), :] = part
    outs += [pltpu.make_async_copy(flux, near_any.at[pl.ds(HALO, 32)], out_sems.at[3])]
    outs[-1].start()
    put_moments(forward, left_ref, high_ref, low_ref, m_ref)
    settle(outs)


def unpack(forward, flat, order):
    return pl.pallas_call(
        unpack_kernel,
        in_specs=[smem(), anywhere(), spec()],
        out_specs=[anywhere(), spec(), anywhere(), anywhere()],
        out_shape=[
            shape(HALO + 32, 128), shape(128, 128), shape(48, NPAD, dtype=BF16), shape(NSLOT, 128, dtype=BF16)
        ],
        scratch_shapes=[
            pltpu.VMEM((48, NPAD), BF16),
            pltpu.VMEM((NSLOT, 128), BF16),
            pltpu.VMEM((32, 128), F32),
            pltpu.VMEM((NPAD, COL), BF16),
            pltpu.VMEM((NPAD, COL), BF16),
            pltpu.VMEM((NSLOT * 8, 128), F32),
            pltpu.VMEM((NPAD, CELLS), BF16),
            pltpu.VMEM((NPAD, CELLS), BF16),
            pltpu.VMEM((128, NPAD), F32),
            pltpu.VMEM((1, NPAD), jnp.int32),
            pltpu.SemaphoreType.DMA((PARTS,)),
            pltpu.SemaphoreType.DMA((4,)),
        ],
        compiler_params=params(),
        name="unpack",
    )(forward, flat, order)


def strip_tags(at_ref, tag_ref):
    row = lax.broadcasted_iota(jnp.int32, (8, 64), 0)
    x = lax.broadcasted_iota(jnp.int32, (8, 64), 1)
    strip = (x == at_ref[0] * 4 + (row >> 1)).astype(F32).astype(BF16)
    picked = lax.dot_general(
        strip, tag_ref[...].astype(F32).astype(BF16), (((1,), (1,)), ((), ())), preferred_element_type=F32
    )
    row = lax.broadcasted_iota(jnp.int32, (64, COL), 0)
    lane = lax.broadcasted_iota(jnp.int32, (64, COL), 1)
    spread = row == ((lane >> 2) & 1) * 32 + (lane >> 3)
    spread = jnp.dot(picked.astype(BF16), spread.astype(F32).astype(BF16), preferred_element_type=F32)
    odd = (lax.broadcasted_iota(jnp.int32, (8, 128), 0) & 1) == 1
    return jnp.where(odd, spread[:, 128:], spread[:, :128]).astype(jnp.int32)


def put_fields(forward, m_ref, at_ref, tag_ref, right_ref, keep_ref, table):
    m = [m_ref[pl.ds(f * 8, 8), :] * WEIGHT for f in range(15)]
    rho = m[0]
    inv = 1.0 / rho
    u = [a * inv for a in m[1:4]]
    energy = m[4] + m[5] + m[6]
    usq = u[0] * u[0] + u[1] * u[1] + u[2] * u[2]
    temp = (energy * inv - usq) * (1.0 / 3.0)
    stress = [[m[4], m[7], m[8]], [m[7], m[5], m[9]], [m[8], m[9], m[6]]]
    q = []
    for i in range(3):
        pu = stress[i][0] * u[0] + stress[i][1] * u[1] + stress[i][2] * u[2]
        q.append(0.5 * (m[10 + i] - 2.0 * pu - u[i] * energy + 2.0 * rho * usq * u[i]))
    log_t = jnp.log(temp)
    inv_t = 1.0 / temp
    rate = (DT / 0.05) * rho * jnp.exp(0.19 * log_t)
    amp = rate * rho * jnp.exp(-1.5 * log_t)
    half = (0.5 * LOG2E) * inv_t
    zero = jnp.zeros_like(rho)
    expo = [-half * usq] + [2.0 * half * a for a in u] + [-half] * 3 + [zero] * 9
    scale = inv * inv_t * inv_t * (1.0 / 15.0)
    a = [b * scale for b in q]
    s0 = u[0] * a[0] + u[1] * a[1] + u[2] * a[2]
    s1 = usq * inv_t - 5.0
    poly = [amp * (1.0 - s0 * s1)]
    poly += [amp * (a[i] * s1 + 2.0 * s0 * u[i] * inv_t) for i in range(3)]
    front = amp * inv_t
    poly += [-front * (2.0 * a[i] * u[i] + s0) for i in range(3)]
    poly += [-2.0 * front * (a[i] * u[j] + a[j] * u[i]) for i, j in ((0, 1), (0, 2), (1, 2))]
    poly += [front * a[i] for i in range(3)] + [zero] * 3
    z = lax.broadcasted_iota(jnp.int32, (8, 128), 1) & 7
    tag = strip_tags(at_ref, tag_ref)
    density, heat = zero, zero
    walls = []
    for side, at in ((0, 0), (1, 7)):
        for level in range(3):
            here = (z == at) & (tag == level)
            n = jnp.where(here, m[13] * (1.0 / MASS[side][level]), 0.0)
            heat = jnp.where(here, n * ENERGY[side][level] - m[14], heat)
            walls.append(n * WALL_T[side][level] ** -1.5)
    for r, c in enumerate(expo + poly + walls + [zero] * 10):
        table[pl.ds(r * 8, 8), :] = c
    table[pl.ds(384, 8), :] = rate
    n = 4
    right_ref[...] = jnp.zeros(right_ref.shape, BF16)

    def pieces(value, count):
        out = []
        for _ in range(count):
            piece = value.astype(BF16)
            out.append(piece)
            value = value - piece.astype(F32)
        return out

    for k in range(n):
        col = column_of(forward, k)
        for hf in range(2):
            j = col * 2 + hf
            at = k * COL + hf * 128
            keep_ref[pl.ds(k * 2 + hf, 1), :] = table[pl.ds(384 + j, 1), :]
            for kind in range(2):
                lanes = pl.ds(kind * n * COL + at, 128)
                first, second, third = pieces(table[pl.ds(kind * 128 + j, 16, stride=8), :], 3)
                for g, piece in enumerate((first, second, third, first, second)):
                    right_ref[pl.ds(g * 16, 16), lanes] = piece
            wall = table[pl.ds(256 + j, 16, stride=8), :]
            twice = table[pl.ds(256 + j, 6, stride=8), :]
            twice = jnp.concatenate([twice, twice, jnp.zeros((4, 128), F32)], axis=0)
            lanes = pl.ds(2 * n * COL + at, 128)
            right_ref[pl.ds(80, 16), lanes] = pieces(twice, 1)[0]
            right_ref[pl.ds(96, 16), lanes] = pieces(wall, 2)[1]
    return heat


def field_scratch():
    return [pltpu.VMEM((128, 3 * CELLS), BF16), pltpu.VMEM((8, 128), F32), pltpu.VMEM((392, 128), F32)]


def put_heat(heat, table, out_ref):
    lane = lax.broadcasted_iota(jnp.int32, (128, 64), 0)
    to = lax.broadcasted_iota(jnp.int32, (128, 64), 1)
    pick = (lane == (to & 15) * 8 + 7 * (to >> 5)).astype(F32).astype(BF16)
    total = jnp.zeros((8, 64), F32)
    for _ in range(3):
        piece = heat.astype(BF16)
        total = total + jnp.dot(piece, pick, preferred_element_type=F32)
        heat = heat - piece.astype(F32)
    odd = lax.broadcasted_iota(jnp.int32, (8, 64), 0) & 1
    half = (lax.broadcasted_iota(jnp.int32, (8, 64), 1) >> 4) & 1
    total = jnp.where(odd == half, total, 0.0)
    table[pl.ds(0, 8), pl.ds(0, 64)] = total
    for x in range(4):
        for side in range(2):
            lanes = pl.ds(side * 32, 32)
            out_ref[x, pl.ds(side, 1), :] = table[pl.ds(2 * x, 1), lanes] + table[pl.ds(2 * x + 1, 1), lanes]


def products(n, phi_ref, right_ref, prod):
    phi = phi_ref[...]
    for k in range(3 * n):
        cols = pl.ds(k * COL, COL)
        prod[:, cols] = jnp.dot(phi, right_ref[:, cols], preferred_element_type=F32)


def drift_of(coefs, h, upwind):
    cx, cyp, cym, czp, czm, spill = coefs
    lane = lax.broadcasted_iota(jnp.int32, (1, 128), 1)
    plus = [pltpu.roll(a, 8, 1) for a in h]
    minus = [pltpu.roll(a, 120, 1) for a in h]
    out = []
    for hf in range(2):
        before = jnp.where(lane < 8, plus[1 - hf], plus[hf])
        after = jnp.where(lane >= 120, minus[1 - hf], minus[hf])
        new = h[hf] - spill * h[hf]
        new = new + (cyp * before + cym * after)
        new = new + (czp * pltpu.roll(h[hf], 1, 1) + czm * pltpu.roll(h[hf], 127, 1))
        if upwind is not None:
            new = new + cx * upwind[hf]
        out.append(new)
    return out


def read_coefs(coef_ref, rows):
    return [coef_ref[rows, pl.ds(c * 128, 128)] for c in range(6)]


def drift_kernel(dir_ref, phi_any, *refs, start, size, first_step):
    steps = 96
    count = size // steps
    if first_step:
        state_any, out_any, phi, state, out, coef, sems, out_sems = refs
        spans = [(pl.ds((start + q * steps) * 8, steps * 8), pl.ds(q * steps * 8, steps * 8)) for q in range(count)]
        pairs = [[(state_any.at[a], state.at[b])] for a, b in spans]
    else:
        state_any, halo_any, out_any, phi, state, halo, out, coef, sems, out_sems = refs
        spans = [(pl.ds(start + q * steps, steps), pl.ds(q * steps, steps)) for q in range(count)]
        pairs = [[(state_any.at[a], state.at[b])] for a, b in spans]
        pairs[0].append((halo_any.at[pl.ds(start * 2, size * 2)], halo))
    flat_pairs = [(phi_any.at[pl.ds(start, size)], phi)] + [pair for group in pairs for pair in group]
    copies = fetch(sems, *flat_pairs)
    forward = dir_ref[0]
    copies[0].wait()
    coef[...] = coefs_of(phi[...], 6)
    step = 32
    at = 1
    outs = []
    for q in range(count):
        settle(copies[at : at + len(pairs[q])])
        at += len(pairs[q])

        def body(k, carry):
            first = pl.multiple_of(q * steps + k * step, step)
            rows = pl.ds(first, step)
            coefs = read_coefs(coef, rows)
            upwind = None
            for i in range(4):
                if first_step:
                    col = column_of(forward, i)
                    h = [state[pl.ds(first * 8 + hf * 4 + col, step, stride=8), :] for hf in range(2)]
                else:
                    h = [state[rows, pl.ds(i * COL + hf * 128, 128)] for hf in range(2)]
                    if i == 0:
                        h = [a + coefs[0] * halo[pl.ds(first * 2 + hf, step, stride=2), :] for hf, a in enumerate(h)]
                for hf, new in enumerate(drift_of(coefs, h, upwind)):
                    out[rows, pl.ds(i * COL + hf * 128, 128)] = new
                upwind = h
            return carry

        lax.fori_loop(0, steps // step, body, 0)
        rows = pl.ds(q * steps, steps)
        outs.append(pltpu.make_async_copy(out.at[rows], out_any.at[rows], out_sems.at[q]))
        outs[-1].start()
    settle(outs)


def drift(forward, phi, piece, *states):
    first_step = len(states) == 1
    start, size = piece

    def kernel(*refs):
        drift_kernel(*refs, start=start, size=size, first_step=first_step)

    if first_step:
        held = [pltpu.VMEM((size * 8, 128), F32)]
    else:
        held = [pltpu.VMEM((size, CELLS), F32), pltpu.VMEM((size * 2, 128), F32)]
    return pl.pallas_call(
        kernel,
        in_specs=[smem()] + [anywhere()] * (1 + len(states)),
        out_specs=anywhere(),
        out_shape=shape(size, CELLS),
        scratch_shapes=[pltpu.VMEM((size, 128), BF16)]
        + held
        + [
            pltpu.VMEM((size, CELLS), F32),
            pltpu.VMEM((size, 768), F32),
            pltpu.SemaphoreType.DMA((2 + size // 96,)),
            pltpu.SemaphoreType.DMA((size // 96,)),
        ],
        compiler_params=params(),
        cost_estimate=cost(DRIFT_COST),
        name="drift",
    )(forward, phi, *states)


def sweep(column, drifted, rate_ref, prod, put, start, stop):
    step = 32

    def body(k, carry):
        first = pl.multiple_of(k * step, step)
        rows = pl.ds(first, step)
        for i in range(4):
            for hf in range(2):
                at = i * COL + hf * 128
                expo = prod[rows, pl.ds(at, 128)]
                poly = prod[rows, pl.ds(CELLS + at, 128)]
                ghost = prod[rows, pl.ds(2 * CELLS + at, 128)]
                new = jnp.exp2(expo) * poly + ghost
                new = new + drifted[rows, pl.ds(at, 128)]
                new = new - rate_ref[pl.ds(2 * i + hf, 1), :] * column(i, hf, first, step)
                put(i, hf, first, step, new)
        return carry

    lax.fori_loop(start // step, stop // step, body, 0)


def fetch_parts(sems, pieces, drifted_any, drifted, state_any, state, scale):
    size = NSLOT // PARTS
    pairs, counts = [], []
    left = list(zip(pieces, drifted_any, strict=True))
    for p in range(PARTS):
        rows = pl.ds(p * size * scale, size * scale)
        group = [(state_any.at[rows], state.at[rows])]
        while left and left[0][0][0] < (p + 1) * size:
            (start, count), ref = left.pop(0)
            group.append((ref, drifted.at[pl.ds(start, count)]))
        pairs += group
        counts.append(len(group))
    copies = fetch(sems, *pairs)
    return [copies[sum(counts[:p]) : sum(counts[: p + 1])] for p in range(PARTS)]


def first_kernel(
    drifted_any, dir_ref, at_ref, in_ref, m0_ref, tag_ref, phi_ref, left_ref, h1_any, edge_any, m_ref,
    right, keep, table, prod, whole, drifted, phi, left, h1, edge, high_ref, low_ref, sems, part_sems, out_sems,
):
    forward = dir_ref[0]
    copies = fetch(sems, (phi_ref, phi), (left_ref, left))
    parts = fetch_parts(part_sems, PIECES[0], drifted_any, drifted, in_ref, whole, 8)
    clear_tail(high_ref, low_ref)
    put_fields(forward, m0_ref, at_ref, tag_ref, right, keep, table)
    settle(copies)
    products(4, phi, right, prod)

    def column(i, hf, first, step):
        return whole[pl.ds(first * 8 + hf * 4 + column_of(forward, i), step, stride=8), :]

    def put(i, hf, first, step, new):
        rows = pl.ds(first, step)
        cols = pl.ds(i * COL + hf * 128, 128)
        h1[rows, cols] = new
        if i == 3:
            edge[pl.ds(first * 2 + hf, step, stride=2), :] = new
        split_into(new, rows, cols, high_ref, low_ref)

    size = NSLOT // PARTS
    outs = []
    for p in range(PARTS):
        settle(parts[p])
        sweep(column, drifted, keep, prod, put, p * size, p * size + size)
        rows = pl.ds(p * size, size)
        outs.append(pltpu.make_async_copy(h1.at[rows], h1_any.at[rows], out_sems.at[p]))
        outs[-1].start()
    outs.append(pltpu.make_async_copy(edge, edge_any, out_sems.at[PARTS]))
    outs[-1].start()
    put_moments(forward, left, high_ref, low_ref, m_ref)
    settle(outs)


def first_step(forward, at, flat, drifted, m, tags, phi, left):
    n = len(drifted)

    def kernel(*refs):
        first_kernel(refs[3 : 3 + n], *refs[:3], *refs[3 + n :])

    return pl.pallas_call(
        kernel,
        in_specs=[smem(), smem()] + [anywhere()] * (1 + n) + [spec(), spec(), anywhere(), anywhere()],
        out_specs=[anywhere(), anywhere(), spec()],
        out_shape=[shape(NSLOT, CELLS), shape(NSLOT * 2, 128), shape(128, 128)],
        scratch_shapes=field_scratch()
        + [
            pltpu.VMEM((NSLOT, 3 * CELLS), F32),
            pltpu.VMEM((NSLOT * 8, 128), F32),
            pltpu.VMEM((NSLOT, CELLS), F32),
            pltpu.VMEM((NSLOT, 128), BF16),
            pltpu.VMEM((48, NPAD), BF16),
            pltpu.VMEM((NSLOT, CELLS), F32),
            pltpu.VMEM((NSLOT * 2, 128), F32),
            pltpu.VMEM((NPAD, CELLS), BF16),
            pltpu.VMEM((NPAD, CELLS), BF16),
            pltpu.SemaphoreType.DMA((2,)),
            pltpu.SemaphoreType.DMA((PARTS + n,)),
            pltpu.SemaphoreType.DMA((PARTS + 1,)),
        ],
        compiler_params=params(53.7),
        cost_estimate=cost(FIRST_COST),
        name="first_step",
    )(forward, at, flat, *drifted, m, tags, phi, left)


def inflow_kernel(dir_ref, halo_any, m_any, out_ref, m_ref, flux, sems):
    copies = fetch(sems, (halo_any.at[pl.ds(HALO, 32)], flux), (m_any, m_ref))
    row = column_of(dir_ref[0], 0) * 2
    settle(copies)
    out_ref[...] = m_ref[...]
    for half in range(2):
        for k in range(2):
            at = pl.ds(64 * k + row + half, 8, stride=8)
            out_ref[at, :] = m_ref[at, :] + flux[pl.ds((half * 2 + k) * 8, 8), :]


def inflow(forward, halo, m):
    return pl.pallas_call(
        inflow_kernel,
        in_specs=[smem(), anywhere(), anywhere()],
        out_specs=spec(),
        out_shape=shape(128, 128),
        scratch_shapes=[pltpu.VMEM((128, 128), F32), pltpu.VMEM((32, 128), F32), pltpu.SemaphoreType.DMA((2,))],
        compiler_params=params(53),
        name="inflow",
    )(forward, halo, m)


def second_kernel(
    drifted_any, dir_ref, at_ref, h_any, halo_any, m0_ref, tag_ref, phi_any, out_any, pre_any, heat_ref,
    right, keep, table, prod, h, halo, drifted, phi, cx, out_ref, pre_ref, sems, part_sems, out_sems,
):
    forward = dir_ref[0]
    copies = fetch(sems, (phi_any, phi), (halo_any.at[pl.ds(0, HALO)], halo))
    parts = fetch_parts(part_sems, PIECES[1], drifted_any, drifted, h_any, h, 1)
    heat = put_fields(forward, m0_ref, at_ref, tag_ref, right, keep, table)
    copies[0].wait()
    products(4, phi, right, prod)
    cx[...] = coefs_of(phi[...], 1)
    copies[1].wait()

    def column(i, hf, first, step):
        rows = pl.ds(first, step)
        state = h[rows, pl.ds(i * COL + hf * 128, 128)]
        if i == 0:
            state = state + cx[rows, :] * halo[pl.ds(first * 2 + hf, step, stride=2), :]
        return state

    def put(i, hf, first, step, new):
        out_ref[pl.ds(first * 8 + hf * 4 + column_of(forward, i), step, stride=8), :] = new
        if i == 0:
            pre_ref[pl.ds(first * 2 + hf, step, stride=2), :] = new

    size = NSLOT // PARTS
    outs = []
    for p in range(PARTS):
        settle(parts[p])
        sweep(column, drifted, keep, prod, put, p * size, p * size + size)
        rows = pl.ds(p * size * 8, size * 8)
        outs.append(pltpu.make_async_copy(out_ref.at[rows], out_any.at[rows], out_sems.at[p]))
        outs[-1].start()
    outs.append(pltpu.make_async_copy(pre_ref, pre_any, out_sems.at[PARTS]))
    outs[-1].start()
    put_heat(heat, table, heat_ref)
    settle(outs)


def second_step(forward, at, h, halo, drifted, m, tags, phi):
    n = len(drifted)

    def kernel(*refs):
        second_kernel(refs[4 : 4 + n], *refs[:4], *refs[4 + n :])

    return pl.pallas_call(
        kernel,
        in_specs=[smem(), smem()] + [anywhere()] * (2 + n) + [spec(), spec(), anywhere()],
        out_specs=[anywhere(), anywhere(), spec()],
        out_shape=[shape(NSLOT * 8, 128), shape(NSLOT * 2, 128), shape(4, 2, 32)],
        scratch_shapes=field_scratch()
        + [
            pltpu.VMEM((NSLOT, 3 * CELLS), F32),
            pltpu.VMEM((NSLOT, CELLS), F32),
            pltpu.VMEM((NSLOT * 2, 128), F32),
            pltpu.VMEM((NSLOT, CELLS), F32),
            pltpu.VMEM((NSLOT, 128), BF16),
            pltpu.VMEM((NSLOT, 128), F32),
            pltpu.VMEM((NSLOT * 8, 128), F32),
            pltpu.VMEM((NSLOT * 2, 128), F32),
            pltpu.SemaphoreType.DMA((2,)),
            pltpu.SemaphoreType.DMA((PARTS + n,)),
            pltpu.SemaphoreType.DMA((PARTS + 1,)),
        ],
        compiler_params=params(53.7),
        cost_estimate=cost(SECOND_COST),
        name="second_step",
    )(forward, at, h, halo, *drifted, m, tags, phi)


def last_kernel(dir_ref, h_any, pre_any, halo_any, phi_any, out_any, pre, halo, phi, sems, out_sems):
    del h_any
    size = HALO // LAST_PARTS
    spans = [pl.ds(p * size, size) for p in range(LAST_PARTS)]
    pairs = [(phi_any, phi)]
    for rows in spans:
        pairs += [(pre_any.at[rows], pre.at[rows]), (halo_any.at[rows], halo.at[rows])]
    copies = fetch(sems, *pairs)
    copies[0].wait()
    cx = coefs_of(phi[...], 1)
    column = column_rows(out_any, column_of(dir_ref[0], 0))
    outs = []
    for p, rows in enumerate(spans):
        settle(copies[1 + 2 * p : 3 + 2 * p])
        part = cx[p * (size // 2) : (p + 1) * (size // 2)]
        for half in range(2):
            at = pl.ds(p * size + half, size // 2, stride=2)
            pre[at, :] = pre[at, :] + part * halo[at, :]
        outs.append(pltpu.make_async_copy(pre.at[rows], column.at[rows], out_sems.at[p]))
        outs[-1].start()
    settle(outs)


def last(forward, h, pre, halo, phi):
    return pl.pallas_call(
        last_kernel,
        in_specs=[smem()] + [anywhere()] * 4,
        out_specs=anywhere(),
        out_shape=shape(NSLOT * 8, 128),
        input_output_aliases={1: 0},
        scratch_shapes=[
            pltpu.VMEM((NSLOT * 2, 128), F32),
            pltpu.VMEM((NSLOT * 2, 128), F32),
            pltpu.VMEM((NSLOT, 128), BF16),
            pltpu.SemaphoreType.DMA((1 + 2 * LAST_PARTS,)),
            pltpu.SemaphoreType.DMA((LAST_PARTS,)),
        ],
        compiler_params=params(),
        name="last",
    )(forward, h, pre, halo, phi)


def body(state, velocity_order, wall_tag):
    forward = upstream_first().reshape(1)
    at = lax.axis_index("space").astype(jnp.int32).reshape(1)
    flat = state.reshape(NSLOT, 4, 2, 128).transpose(0, 2, 1, 3).reshape(NSLOT * 8, 128)
    near, m, left, phi = unpack(forward, flat, velocity_order)
    drifted = [drift(forward, phi, piece, flat) for piece in PIECES[0]]
    m, drifted[0] = lax.optimization_barrier((over_y(m), drifted[0]))
    (near,) = hold(m, near)
    near = downstream(near)
    tags = jnp.transpose(wall_tag, (1, 2, 0)).reshape(64, 64)
    m, drifted = over_rest(over_x(m), *drifted)
    h1, edge, m = first_step(forward, at, flat, drifted, m, tags, phi, left)
    drifted = [drift(forward, phi, piece, h1, near) for piece in PIECES[1]]
    m, drifted[0] = lax.optimization_barrier((over_y(inflow(forward, near, m)), drifted[0]))
    m, drifted[1] = lax.optimization_barrier((over_x(m), drifted[1]))
    (edge,) = hold(m, edge)
    edge = downstream(edge)
    m, drifted = over_rest(m, *drifted)
    out, pre, wall_heat = second_step(forward, at, h1, near, drifted, m, tags, phi)
    out = last(forward, out, pre, edge, phi)
    state_next = out.reshape(NSLOT, 2, 4, 128).transpose(0, 2, 1, 3).reshape(NSLOT, 4, 256)
    return state_next, wall_heat


def solution(mesh):
    return jax.shard_map(
        body,
        mesh=mesh,
        in_specs=(P("vel", "space", None), P("vel"), P()),
        out_specs=(P("vel", "space", None), P("space", None, None)),
        check_vma=False,
    )
```

```python
import math

import jax
import jax.numpy as jnp
import numpy as np
from jax import lax
from jax.experimental import pallas as pl
from jax.experimental.pallas import tpu as pltpu
from jax.sharding import PartitionSpec as P

NV1 = 24
NSLOT = 864
NPAD = 896
CELLS = 1024
COL = 256
SPACING = 12.0 / NV1
TOP = (NV1 - 1) * 0.5 * SPACING
KD = 0.3 / TOP
DT = 0.3 / (8 * TOP)
WEIGHT = SPACING**3 / (2.0 * math.pi) ** 1.5
LOG2E = 1.0 / math.log(2.0)
WALL_T = [[b * (0.7 + 0.3 * level) for level in range(3)] for b in (1.4, 0.7)]
AXES = ("vel", "space")
F32 = jnp.float32
BF16 = jnp.bfloat16


def wall_norms():
    line = (2 * np.arange(NV1) - (NV1 - 1)) * 0.5 * SPACING
    cx, cy, cz = np.meshgrid(line, line, line, indexing="ij")
    sq = cx**2 + cy**2 + cz**2
    mass, energy = [], []
    for side in range(2):
        out = np.maximum(cz if side == 0 else -cz, 0.0) * WEIGHT
        prof = [out * t**-1.5 * np.exp(-sq / (2.0 * t)) for t in WALL_T[side]]
        mass.append([float(p.sum()) for p in prof])
        energy.append([float((p * 0.5 * sq).sum()) for p in prof])
    return mass, energy


MASS, ENERGY = wall_norms()


def device_of(i):
    v, s = divmod(i, 16)
    x, r = divmod(v, 4)
    return x, r >> 1, r & 1, s


def index_of(x, y, core, s):
    return ((x % 4 * 2 + y % 2) * 2 + core % 2) * 16 + s % 16


def permute(value, move):
    return lax.ppermute(value, AXES, [(i, index_of(*move(*device_of(i)))) for i in range(256)])


def downstream(value):
    return permute(value, lambda x, y, c, s: (x, y, c, s - 1 if x < 2 else s + 1))


def over_y(part):
    return part + permute(part, lambda x, y, c, s: (x, y ^ 1, c, s))


def over_x(part):
    return part + permute(part, lambda x, y, c, s: (x ^ 1, y, c, s))


def over_rest(part, *work):
    part = part + permute(part, lambda x, y, c, s: (x ^ 2, y, c, s))
    part, *work = lax.optimization_barrier((part, *work))
    return part + permute(part, lambda x, y, c, s: (x, y, c ^ 1, s)), work


def hold(token, *values):
    def kernel(*refs):
        del refs

    place = pl.BlockSpec(memory_space=pl.ANY)
    return pl.pallas_call(
        kernel,
        in_specs=[spec()] + [place] * len(values),
        out_specs=[place] * len(values),
        out_shape=[shape(*v.shape) for v in values],
        input_output_aliases={k + 1: k for k in range(len(values))},
        compiler_params=params(53),
        cost_estimate=cost(HOLD_COST),
        name="hold",
    )(token, *values)


def upstream_first():
    return (lax.axis_index("vel") >= 8).astype(jnp.int32)


def column_of(forward, i):
    return jnp.where(forward == 1, i, 3 - i)


def spec():
    return pl.BlockSpec(memory_space=pltpu.VMEM)


def anywhere():
    return pl.BlockSpec(memory_space=pltpu.HBM)


def smem():
    return pl.BlockSpec(memory_space=pltpu.SMEM)


def params(mib=63.5):
    return pltpu.CompilerParams(vmem_limit_bytes=int(mib * 2**20))


def cost(us):
    return pl.CostEstimate(flops=int(us * 1.15e9), bytes_accessed=10_000, transcendentals=0)


def shape(*dims, dtype=F32):
    return jax.ShapeDtypeStruct(dims, dtype)


def settle(copies):
    for copy in copies:
        copy.wait()


def fetch(sems, *pairs):
    copies = [pltpu.make_async_copy(src, dst, sems.at[k]) for k, (src, dst) in enumerate(pairs)]
    for copy in copies:
        copy.start()
    return copies


def high(a):
    return a.astype(BF16).astype(F32)


def velocity_rows(order_ref, padded):
    padded[...] = jnp.zeros((1, NPAD), jnp.int32)
    padded[:, pl.ds(0, NSLOT)] = order_ref[...].reshape(1, NSLOT)
    order = padded[...]
    upper = (order * 43691) >> 20
    kx = (upper * 43691) >> 20
    ky = upper - kx * NV1
    kz = order - upper * NV1
    live = (lax.broadcasted_iota(jnp.int32, (1, NPAD), 1) < NSLOT).astype(F32)

    def coordinate(k):
        return (2 * k - (NV1 - 1)).astype(F32) * (0.5 * SPACING) * live

    cx, cy, cz = coordinate(kx), coordinate(ky), coordinate(kz)
    sq = cx * cx + cy * cy + cz * cz
    phi = [live, cx, cy, cz, cx * cx, cy * cy, cz * cz, cx * cy, cx * cz, cy * cz, cx * sq, cy * sq, cz * sq]
    return cx, cy, cz, sq, phi


def put_left(order_ref, padded, table, left_ref):
    _, _, cz, sq, phi = velocity_rows(order_ref, padded)
    zero = jnp.zeros_like(cz)
    down, up = jnp.maximum(-cz, 0.0), jnp.maximum(cz, 0.0)
    sums = phi + [down, down * (0.5 * sq), zero] + [zero] * 5 + [up, up * (0.5 * sq), zero]
    for r, a in enumerate(sums):
        table[pl.ds(r, 1), :] = high(a)
        table[pl.ds(24 + r, 1), :] = a - high(a)
    left_ref[...] = table[pl.ds(0, 48), :].astype(BF16)


def put_phi(order_ref, padded, table, phi_ref):
    cx, cy, cz, sq, phi = velocity_rows(order_ref, padded)
    zero = jnp.zeros_like(cx)
    down, up = jnp.maximum(-cz, 0.0), jnp.maximum(cz, 0.0)
    ghost = []
    for side, out in ((0, up), (1, down)):
        ghost += [out * KD * jnp.exp(sq * (-0.5 / t)) for t in WALL_T[side]]
    rows = []
    for _ in range(3):
        rows += [high(a) for a in phi] + [zero] * 3
    for _ in range(2):
        rows += [a - high(a) for a in phi] + [zero] * 3
    rows += [high(a) for a in ghost] + [high(a - high(a)) for a in ghost] + [zero] * 4
    rows += [high(a) for a in ghost] + [zero] * 10
    rows += [jnp.abs(cx), jnp.maximum(cy, 0.0), jnp.maximum(-cy, 0.0), up, down]
    rows += [jnp.abs(cx) + jnp.abs(cy) + jnp.abs(cz)] + [zero] * 10
    for r, a in enumerate(rows):
        table[pl.ds(r, 1), :] = a
    turned = table[...].T.astype(BF16)
    phi_ref[...] = turned[:NSLOT]


def coefs_of(phi, kinds):
    row = lax.broadcasted_iota(jnp.int32, (128, 128 * kinds), 0)
    lane = lax.broadcasted_iota(jnp.int32, (128, 128 * kinds), 1)
    kind, z = lane >> 7, lane & 7
    drop = ((kind == 3) & (z == 0)) | ((kind == 4) & (z == 7))
    pick = ((row == 112 + kind) & jnp.logical_not(drop)).astype(F32).astype(BF16)
    return jnp.dot(phi, pick, preferred_element_type=F32) * KD


def clear_tail(high_ref, low_ref):
    tail = jnp.zeros((NPAD - NSLOT, high_ref.shape[1]), BF16)
    high_ref[pl.ds(NSLOT, NPAD - NSLOT), :] = tail
    low_ref[pl.ds(NSLOT, NPAD - NSLOT), :] = tail


def sums_of(left, high, low):
    total = jnp.dot(left, high, preferred_element_type=F32) + jnp.dot(left, low, preferred_element_type=F32)
    total = total[:24] + total[24:]
    sub = lax.broadcasted_iota(jnp.int32, (8, 128), 0)
    lane = lax.broadcasted_iota(jnp.int32, (8, 128), 1)
    top = (sub >= 5) & ((lane & 7) >= 4)
    out = []
    for half in range(2):
        part = total[:, half * 128 : half * 128 + 128]
        out.append((part[0:8], jnp.where(top, part[16:24], part[8:16])))
    return out


def put_moments(forward, left_ref, high_ref, low_ref, out_ref):
    left = left_ref[...]
    for i in range(4):
        cols = pl.ds(i * COL, COL)
        row = column_of(forward, i) * 2
        for half, (low, mid) in enumerate(sums_of(left, high_ref[:, cols], low_ref[:, cols])):
            out_ref[pl.ds(row + half, 8, stride=8), :] = low
            out_ref[pl.ds(64 + row + half, 8, stride=8), :] = mid


def split_into(value, rows, cols, high_ref, low_ref):
    high = value.astype(BF16)
    high_ref[rows, cols] = high
    low_ref[rows, cols] = (value - high.astype(F32)).astype(BF16)


PARTS = 9
LAST_PARTS = 3
HALO = 2 * NSLOT
PIECES = (((0, 192), (192, 672)), ((0, 192), (192, 192), (384, 480)))
FIRST_COST, SECOND_COST, HOLD_COST = 5, 5, 3
DRIFT_COST = 3


def column_rows(ref, col):
    return ref.reshape(NSLOT * 2, 4, 128).at[:, col, :]


def unpack_kernel(
    dir_ref, in_ref, order_ref, near_any, m_ref, left_any, phi_any,
    left_ref, phi_ref, flux, flux_high, flux_low, whole, high_ref, low_ref, table, padded, sems, out_sems,
):
    forward = dir_ref[0]
    size = NSLOT // PARTS
    spans = [pl.ds(p * size * 8, size * 8) for p in range(PARTS)]
    copies = fetch(sems, *[(in_ref.at[a], whole.at[a]) for a in spans])
    put_phi(order_ref, padded, table, phi_ref)
    put_left(order_ref, padded, table, left_ref)
    clear_tail(high_ref, low_ref)
    clear_tail(flux_high, flux_low)
    step = 96

    for p in range(PARTS):
        copies[p].wait()

        def body(k, carry):
            first = pl.multiple_of(p * size + k * step, 16)
            rows = pl.ds(first, step)
            for i in range(4):
                for half in range(2):
                    start = first * 8 + half * 4 + column_of(forward, i)
                    part = whole[pl.ds(start, step, stride=8), :]
                    split_into(part, rows, pl.ds(i * COL + half * 128, 128), high_ref, low_ref)
            return carry

        lax.fori_loop(0, size // step, body, 0)
    col = column_of(forward, 3)
    near = column_rows(whole, col)
    outs = fetch(out_sems, (near, near_any.at[pl.ds(0, HALO)]), (left_ref, left_any), (phi_ref, phi_any))
    cx = coefs_of(phi_ref[...], 1)
    for half in range(2):
        share = cx * whole[pl.ds(half * 4 + col, NSLOT, stride=8), :]
        split_into(share, pl.ds(0, NSLOT), pl.ds(half * 128, 128), flux_high, flux_low)
    for half, parts in enumerate(sums_of(left_ref[...], flux_high[...], flux_low[...])):
        for k, part in enumerate(parts):
            flux[pl.ds((half * 2 + k) * 8, 8), :] = part
    outs += [pltpu.make_async_copy(flux, near_any.at[pl.ds(HALO, 32)], out_sems.at[3])]
    outs[-1].start()
    put_moments(forward, left_ref, high_ref, low_ref, m_ref)
    settle(outs)


def unpack(forward, flat, order):
    return pl.pallas_call(
        unpack_kernel,
        in_specs=[smem(), anywhere(), spec()],
        out_specs=[anywhere(), spec(), anywhere(), anywhere()],
        out_shape=[
            shape(HALO + 32, 128), shape(128, 128), shape(48, NPAD, dtype=BF16), shape(NSLOT, 128, dtype=BF16)
        ],
        scratch_shapes=[
            pltpu.VMEM((48, NPAD), BF16),
            pltpu.VMEM((NSLOT, 128), BF16),
            pltpu.VMEM((32, 128), F32),
            pltpu.VMEM((NPAD, COL), BF16),
            pltpu.VMEM((NPAD, COL), BF16),
            pltpu.VMEM((NSLOT * 8, 128), F32),
            pltpu.VMEM((NPAD, CELLS), BF16),
            pltpu.VMEM((NPAD, CELLS), BF16),
            pltpu.VMEM((128, NPAD), F32),
            pltpu.VMEM((1, NPAD), jnp.int32),
            pltpu.SemaphoreType.DMA((PARTS,)),
            pltpu.SemaphoreType.DMA((4,)),
        ],
        compiler_params=params(),
        name="unpack",
    )(forward, flat, order)


def strip_tags(at_ref, tag_ref):
    row = lax.broadcasted_iota(jnp.int32, (8, 64), 0)
    x = lax.broadcasted_iota(jnp.int32, (8, 64), 1)
    strip = (x == at_ref[0] * 4 + (row >> 1)).astype(F32).astype(BF16)
    picked = lax.dot_general(
        strip, tag_ref[...].astype(F32).astype(BF16), (((1,), (1,)), ((), ())), preferred_element_type=F32
    )
    row = lax.broadcasted_iota(jnp.int32, (64, COL), 0)
    lane = lax.broadcasted_iota(jnp.int32, (64, COL), 1)
    spread = row == ((lane >> 2) & 1) * 32 + (lane >> 3)
    spread = jnp.dot(picked.astype(BF16), spread.astype(F32).astype(BF16), preferred_element_type=F32)
    odd = (lax.broadcasted_iota(jnp.int32, (8, 128), 0) & 1) == 1
    return jnp.where(odd, spread[:, 128:], spread[:, :128]).astype(jnp.int32)


def put_fields(forward, m_ref, at_ref, tag_ref, right_ref, keep_ref, table):
    m = [m_ref[pl.ds(f * 8, 8), :] * WEIGHT for f in range(15)]
    rho = m[0]
    inv = 1.0 / rho
    u = [a * inv for a in m[1:4]]
    energy = m[4] + m[5] + m[6]
    usq = u[0] * u[0] + u[1] * u[1] + u[2] * u[2]
    temp = (energy * inv - usq) * (1.0 / 3.0)
    stress = [[m[4], m[7], m[8]], [m[7], m[5], m[9]], [m[8], m[9], m[6]]]
    q = []
    for i in range(3):
        pu = stress[i][0] * u[0] + stress[i][1] * u[1] + stress[i][2] * u[2]
        q.append(0.5 * (m[10 + i] - 2.0 * pu - u[i] * energy + 2.0 * rho * usq * u[i]))
    log_t = jnp.log(temp)
    inv_t = 1.0 / temp
    rate = (DT / 0.05) * rho * jnp.exp(0.19 * log_t)
    amp = rate * rho * jnp.exp(-1.5 * log_t)
    half = (0.5 * LOG2E) * inv_t
    zero = jnp.zeros_like(rho)
    expo = [-half * usq] + [2.0 * half * a for a in u] + [-half] * 3 + [zero] * 9
    scale = inv * inv_t * inv_t * (1.0 / 15.0)
    a = [b * scale for b in q]
    s0 = u[0] * a[0] + u[1] * a[1] + u[2] * a[2]
    s1 = usq * inv_t - 5.0
    poly = [amp * (1.0 - s0 * s1)]
    poly += [amp * (a[i] * s1 + 2.0 * s0 * u[i] * inv_t) for i in range(3)]
    front = amp * inv_t
    poly += [-front * (2.0 * a[i] * u[i] + s0) for i in range(3)]
    poly += [-2.0 * front * (a[i] * u[j] + a[j] * u[i]) for i, j in ((0, 1), (0, 2), (1, 2))]
    poly += [front * a[i] for i in range(3)] + [zero] * 3
    z = lax.broadcasted_iota(jnp.int32, (8, 128), 1) & 7
    tag = strip_tags(at_ref, tag_ref)
    density, heat = zero, zero
    walls = []
    for side, at in ((0, 0), (1, 7)):
        for level in range(3):
            here = (z == at) & (tag == level)
            n = jnp.where(here, m[13] * (1.0 / MASS[side][level]), 0.0)
            heat = jnp.where(here, n * ENERGY[side][level] - m[14], heat)
            walls.append(n * WALL_T[side][level] ** -1.5)
    for r, c in enumerate(expo + poly + walls + [zero] * 10):
        table[pl.ds(r * 8, 8), :] = c
    table[pl.ds(384, 8), :] = rate
    n = 4
    right_ref[...] = jnp.zeros(right_ref.shape, BF16)

    def pieces(value, count):
        out = []
        for _ in range(count):
            piece = value.astype(BF16)
            out.append(piece)
            value = value - piece.astype(F32)
        return out

    for k in range(n):
        col = column_of(forward, k)
        for hf in range(2):
            j = col * 2 + hf
            at = k * COL + hf * 128
            keep_ref[pl.ds(k * 2 + hf, 1), :] = table[pl.ds(384 + j, 1), :]
            for kind in range(2):
                lanes = pl.ds(kind * n * COL + at, 128)
                first, second, third = pieces(table[pl.ds(kind * 128 + j, 16, stride=8), :], 3)
                for g, piece in enumerate((first, second, third, first, second)):
                    right_ref[pl.ds(g * 16, 16), lanes] = piece
            wall = table[pl.ds(256 + j, 16, stride=8), :]
            twice = table[pl.ds(256 + j, 6, stride=8), :]
            twice = jnp.concatenate([twice, twice, jnp.zeros((4, 128), F32)], axis=0)
            lanes = pl.ds(2 * n * COL + at, 128)
            right_ref[pl.ds(80, 16), lanes] = pieces(twice, 1)[0]
            right_ref[pl.ds(96, 16), lanes] = pieces(wall, 2)[1]
    return heat


def field_scratch():
    return [pltpu.VMEM((128, 3 * CELLS), BF16), pltpu.VMEM((8, 128), F32), pltpu.VMEM((392, 128), F32)]


def put_heat(heat, table, out_ref):
    lane = lax.broadcasted_iota(jnp.int32, (128, 64), 0)
    to = lax.broadcasted_iota(jnp.int32, (128, 64), 1)
    pick = (lane == (to & 15) * 8 + 7 * (to >> 5)).astype(F32).astype(BF16)
    total = jnp.zeros((8, 64), F32)
    for _ in range(3):
        piece = heat.astype(BF16)
        total = total + jnp.dot(piece, pick, preferred_element_type=F32)
        heat = heat - piece.astype(F32)
    odd = lax.broadcasted_iota(jnp.int32, (8, 64), 0) & 1
    half = (lax.broadcasted_iota(jnp.int32, (8, 64), 1) >> 4) & 1
    total = jnp.where(odd == half, total, 0.0)
    table[pl.ds(0, 8), pl.ds(0, 64)] = total
    for x in range(4):
        for side in range(2):
            lanes = pl.ds(side * 32, 32)
            out_ref[x, pl.ds(side, 1), :] = table[pl.ds(2 * x, 1), lanes] + table[pl.ds(2 * x + 1, 1), lanes]


def products(n, phi_ref, right_ref, prod):
    phi = phi_ref[...]
    for k in range(3 * n):
        cols = pl.ds(k * COL, COL)
        prod[:, cols] = jnp.dot(phi, right_ref[:, cols], preferred_element_type=F32)


def drift_of(coefs, h, upwind):
    cx, cyp, cym, czp, czm, spill = coefs
    lane = lax.broadcasted_iota(jnp.int32, (1, 128), 1)
    plus = [pltpu.roll(a, 8, 1) for a in h]
    minus = [pltpu.roll(a, 120, 1) for a in h]
    out = []
    for hf in range(2):
        before = jnp.where(lane < 8, plus[1 - hf], plus[hf])
        after = jnp.where(lane >= 120, minus[1 - hf], minus[hf])
        new = h[hf] - spill * h[hf]
        new = new + (cyp * before + cym * after)
        new = new + (czp * pltpu.roll(h[hf], 1, 1) + czm * pltpu.roll(h[hf], 127, 1))
        if upwind is not None:
            new = new + cx * upwind[hf]
        out.append(new)
    return out


def read_coefs(coef_ref, rows):
    return [coef_ref[rows, pl.ds(c * 128, 128)] for c in range(6)]


def drift_kernel(dir_ref, phi_any, *refs, start, size, first_step):
    steps = 96
    count = size // steps
    if first_step:
        state_any, out_any, phi, state, out, coef, sems, out_sems = refs
        spans = [(pl.ds((start + q * steps) * 8, steps * 8), pl.ds(q * steps * 8, steps * 8)) for q in range(count)]
        pairs = [[(state_any.at[a], state.at[b])] for a, b in spans]
    else:
        state_any, halo_any, out_any, phi, state, halo, out, coef, sems, out_sems = refs
        spans = [(pl.ds(start + q * steps, steps), pl.ds(q * steps, steps)) for q in range(count)]
        pairs = [[(state_any.at[a], state.at[b])] for a, b in spans]
        pairs[0].append((halo_any.at[pl.ds(start * 2, size * 2)], halo))
    flat_pairs = [(phi_any.at[pl.ds(start, size)], phi)] + [pair for group in pairs for pair in group]
    copies = fetch(sems, *flat_pairs)
    forward = dir_ref[0]
    copies[0].wait()
    coef[...] = coefs_of(phi[...], 6)
    step = 32
    at = 1
    outs = []
    for q in range(count):
        settle(copies[at : at + len(pairs[q])])
        at += len(pairs[q])

        def body(k, carry):
            first = pl.multiple_of(q * steps + k * step, step)
            rows = pl.ds(first, step)
            coefs = read_coefs(coef, rows)
            upwind = None
            for i in range(4):
                if first_step:
                    col = column_of(forward, i)
                    h = [state[pl.ds(first * 8 + hf * 4 + col, step, stride=8), :] for hf in range(2)]
                else:
                    h = [state[rows, pl.ds(i * COL + hf * 128, 128)] for hf in range(2)]
                    if i == 0:
                        h = [a + coefs[0] * halo[pl.ds(first * 2 + hf, step, stride=2), :] for hf, a in enumerate(h)]
                for hf, new in enumerate(drift_of(coefs, h, upwind)):
                    out[rows, pl.ds(i * COL + hf * 128, 128)] = new
                upwind = h
            return carry

        lax.fori_loop(0, steps // step, body, 0)
        rows = pl.ds(q * steps, steps)
        outs.append(pltpu.make_async_copy(out.at[rows], out_any.at[rows], out_sems.at[q]))
        outs[-1].start()
    settle(outs)


def drift(forward, phi, piece, *states):
    first_step = len(states) == 1
    start, size = piece

    def kernel(*refs):
        drift_kernel(*refs, start=start, size=size, first_step=first_step)

    if first_step:
        held = [pltpu.VMEM((size * 8, 128), F32)]
    else:
        held = [pltpu.VMEM((size, CELLS), F32), pltpu.VMEM((size * 2, 128), F32)]
    return pl.pallas_call(
        kernel,
        in_specs=[smem()] + [anywhere()] * (1 + len(states)),
        out_specs=anywhere(),
        out_shape=shape(size, CELLS),
        scratch_shapes=[pltpu.VMEM((size, 128), BF16)]
        + held
        + [
            pltpu.VMEM((size, CELLS), F32),
            pltpu.VMEM((size, 768), F32),
            pltpu.SemaphoreType.DMA((2 + size // 96,)),
            pltpu.SemaphoreType.DMA((size // 96,)),
        ],
        compiler_params=params(),
        cost_estimate=cost(DRIFT_COST),
        name="drift",
    )(forward, phi, *states)


def sweep(column, drifted, rate_ref, prod, put, start, stop):
    step = 32

    def body(k, carry):
        first = pl.multiple_of(k * step, step)
        rows = pl.ds(first, step)
        for i in range(4):
            for hf in range(2):
                at = i * COL + hf * 128
                expo = prod[rows, pl.ds(at, 128)]
                poly = prod[rows, pl.ds(CELLS + at, 128)]
                ghost = prod[rows, pl.ds(2 * CELLS + at, 128)]
                new = jnp.exp2(expo) * poly + ghost
                new = new + drifted[rows, pl.ds(at, 128)]
                new = new - rate_ref[pl.ds(2 * i + hf, 1), :] * column(i, hf, first, step)
                put(i, hf, first, step, new)
        return carry

    lax.fori_loop(start // step, stop // step, body, 0)


def fetch_parts(sems, pieces, drifted_any, drifted, state_any, state, scale):
    size = NSLOT // PARTS
    pairs, counts = [], []
    left = list(zip(pieces, drifted_any, strict=True))
    for p in range(PARTS):
        rows = pl.ds(p * size * scale, size * scale)
        group = [(state_any.at[rows], state.at[rows])]
        while left and left[0][0][0] < (p + 1) * size:
            (start, count), ref = left.pop(0)
            group.append((ref, drifted.at[pl.ds(start, count)]))
        pairs += group
        counts.append(len(group))
    copies = fetch(sems, *pairs)
    return [copies[sum(counts[:p]) : sum(counts[: p + 1])] for p in range(PARTS)]


def first_kernel(
    drifted_any, dir_ref, at_ref, in_ref, m0_ref, tag_ref, phi_ref, left_ref, h1_any, edge_any, m_ref,
    right, keep, table, prod, whole, drifted, phi, left, h1, edge, high_ref, low_ref, sems, part_sems, out_sems,
):
    forward = dir_ref[0]
    copies = fetch(sems, (phi_ref, phi), (left_ref, left))
    parts = fetch_parts(part_sems, PIECES[0], drifted_any, drifted, in_ref, whole, 8)
    clear_tail(high_ref, low_ref)
    put_fields(forward, m0_ref, at_ref, tag_ref, right, keep, table)
    settle(copies)
    products(4, phi, right, prod)

    def column(i, hf, first, step):
        return whole[pl.ds(first * 8 + hf * 4 + column_of(forward, i), step, stride=8), :]

    def put(i, hf, first, step, new):
        rows = pl.ds(first, step)
        cols = pl.ds(i * COL + hf * 128, 128)
        h1[rows, cols] = new
        if i == 3:
            edge[pl.ds(first * 2 + hf, step, stride=2), :] = new
        split_into(new, rows, cols, high_ref, low_ref)

    size = NSLOT // PARTS
    outs = []
    for p in range(PARTS):
        settle(parts[p])
        sweep(column, drifted, keep, prod, put, p * size, p * size + size)
        rows = pl.ds(p * size, size)
        outs.append(pltpu.make_async_copy(h1.at[rows], h1_any.at[rows], out_sems.at[p]))
        outs[-1].start()
    outs.append(pltpu.make_async_copy(edge, edge_any, out_sems.at[PARTS]))
    outs[-1].start()
    put_moments(forward, left, high_ref, low_ref, m_ref)
    settle(outs)


def first_step(forward, at, flat, drifted, m, tags, phi, left):
    n = len(drifted)

    def kernel(*refs):
        first_kernel(refs[3 : 3 + n], *refs[:3], *refs[3 + n :])

    return pl.pallas_call(
        kernel,
        in_specs=[smem(), smem()] + [anywhere()] * (1 + n) + [spec(), spec(), anywhere(), anywhere()],
        out_specs=[anywhere(), anywhere(), spec()],
        out_shape=[shape(NSLOT, CELLS), shape(NSLOT * 2, 128), shape(128, 128)],
        scratch_shapes=field_scratch()
        + [
            pltpu.VMEM((NSLOT, 3 * CELLS), F32),
            pltpu.VMEM((NSLOT * 8, 128), F32),
            pltpu.VMEM((NSLOT, CELLS), F32),
            pltpu.VMEM((NSLOT, 128), BF16),
            pltpu.VMEM((48, NPAD), BF16),
            pltpu.VMEM((NSLOT, CELLS), F32),
            pltpu.VMEM((NSLOT * 2, 128), F32),
            pltpu.VMEM((NPAD, CELLS), BF16),
            pltpu.VMEM((NPAD, CELLS), BF16),
            pltpu.SemaphoreType.DMA((2,)),
            pltpu.SemaphoreType.DMA((PARTS + n,)),
            pltpu.SemaphoreType.DMA((PARTS + 1,)),
        ],
        compiler_params=params(53.7),
        cost_estimate=cost(FIRST_COST),
        name="first_step",
    )(forward, at, flat, *drifted, m, tags, phi, left)


def inflow_kernel(dir_ref, halo_any, m_any, out_ref, m_ref, flux, sems):
    copies = fetch(sems, (halo_any.at[pl.ds(HALO, 32)], flux), (m_any, m_ref))
    row = column_of(dir_ref[0], 0) * 2
    settle(copies)
    out_ref[...] = m_ref[...]
    for half in range(2):
        for k in range(2):
            at = pl.ds(64 * k + row + half, 8, stride=8)
            out_ref[at, :] = m_ref[at, :] + flux[pl.ds((half * 2 + k) * 8, 8), :]


def inflow(forward, halo, m):
    return pl.pallas_call(
        inflow_kernel,
        in_specs=[smem(), anywhere(), anywhere()],
        out_specs=spec(),
        out_shape=shape(128, 128),
        scratch_shapes=[pltpu.VMEM((128, 128), F32), pltpu.VMEM((32, 128), F32), pltpu.SemaphoreType.DMA((2,))],
        compiler_params=params(53),
        name="inflow",
    )(forward, halo, m)


def second_kernel(
    drifted_any, dir_ref, at_ref, h_any, halo_any, m0_ref, tag_ref, phi_any, out_any, pre_any, heat_ref,
    right, keep, table, prod, h, halo, drifted, phi, cx, out_ref, pre_ref, sems, part_sems, out_sems,
):
    forward = dir_ref[0]
    copies = fetch(sems, (phi_any, phi), (halo_any.at[pl.ds(0, HALO)], halo))
    parts = fetch_parts(part_sems, PIECES[1], drifted_any, drifted, h_any, h, 1)
    heat = put_fields(forward, m0_ref, at_ref, tag_ref, right, keep, table)
    copies[0].wait()
    products(4, phi, right, prod)
    cx[...] = coefs_of(phi[...], 1)
    copies[1].wait()

    def column(i, hf, first, step):
        rows = pl.ds(first, step)
        state = h[rows, pl.ds(i * COL + hf * 128, 128)]
        if i == 0:
            state = state + cx[rows, :] * halo[pl.ds(first * 2 + hf, step, stride=2), :]
        return state

    def put(i, hf, first, step, new):
        out_ref[pl.ds(first * 8 + hf * 4 + column_of(forward, i), step, stride=8), :] = new
        if i == 0:
            pre_ref[pl.ds(first * 2 + hf, step, stride=2), :] = new

    size = NSLOT // PARTS
    outs = []
    for p in range(PARTS):
        settle(parts[p])
        sweep(column, drifted, keep, prod, put, p * size, p * size + size)
        rows = pl.ds(p * size * 8, size * 8)
        outs.append(pltpu.make_async_copy(out_ref.at[rows], out_any.at[rows], out_sems.at[p]))
        outs[-1].start()
    outs.append(pltpu.make_async_copy(pre_ref, pre_any, out_sems.at[PARTS]))
    outs[-1].start()
    put_heat(heat, table, heat_ref)
    settle(outs)


def second_step(forward, at, h, halo, drifted, m, tags, phi):
    n = len(drifted)

    def kernel(*refs):
        second_kernel(refs[4 : 4 + n], *refs[:4], *refs[4 + n :])

    return pl.pallas_call(
        kernel,
        in_specs=[smem(), smem()] + [anywhere()] * (2 + n) + [spec(), spec(), anywhere()],
        out_specs=[anywhere(), anywhere(), spec()],
        out_shape=[shape(NSLOT * 8, 128), shape(NSLOT * 2, 128), shape(4, 2, 32)],
        scratch_shapes=field_scratch()
        + [
            pltpu.VMEM((NSLOT, 3 * CELLS), F32),
            pltpu.VMEM((NSLOT, CELLS), F32),
            pltpu.VMEM((NSLOT * 2, 128), F32),
            pltpu.VMEM((NSLOT, CELLS), F32),
            pltpu.VMEM((NSLOT, 128), BF16),
            pltpu.VMEM((NSLOT, 128), F32),
            pltpu.VMEM((NSLOT * 8, 128), F32),
            pltpu.VMEM((NSLOT * 2, 128), F32),
            pltpu.SemaphoreType.DMA((2,)),
            pltpu.SemaphoreType.DMA((PARTS + n,)),
            pltpu.SemaphoreType.DMA((PARTS + 1,)),
        ],
        compiler_params=params(53.7),
        cost_estimate=cost(SECOND_COST),
        name="second_step",
    )(forward, at, h, halo, *drifted, m, tags, phi)


def last_kernel(dir_ref, h_any, pre_any, halo_any, phi_any, out_any, pre, halo, phi, sems, out_sems):
    del h_any
    size = HALO // LAST_PARTS
    spans = [pl.ds(p * size, size) for p in range(LAST_PARTS)]
    pairs = [(phi_any, phi)]
    for rows in spans:
        pairs += [(pre_any.at[rows], pre.at[rows]), (halo_any.at[rows], halo.at[rows])]
    copies = fetch(sems, *pairs)
    copies[0].wait()
    cx = coefs_of(phi[...], 1)
    column = column_rows(out_any, column_of(dir_ref[0], 0))
    outs = []
    for p, rows in enumerate(spans):
        settle(copies[1 + 2 * p : 3 + 2 * p])
        part = cx[p * (size // 2) : (p + 1) * (size // 2)]
        for half in range(2):
            at = pl.ds(p * size + half, size // 2, stride=2)
            pre[at, :] = pre[at, :] + part * halo[at, :]
        outs.append(pltpu.make_async_copy(pre.at[rows], column.at[rows], out_sems.at[p]))
        outs[-1].start()
    settle(outs)


def last(forward, h, pre, halo, phi):
    return pl.pallas_call(
        last_kernel,
        in_specs=[smem()] + [anywhere()] * 4,
        out_specs=anywhere(),
        out_shape=shape(NSLOT * 8, 128),
        input_output_aliases={1: 0},
        scratch_shapes=[
            pltpu.VMEM((NSLOT * 2, 128), F32),
            pltpu.VMEM((NSLOT * 2, 128), F32),
            pltpu.VMEM((NSLOT, 128), BF16),
            pltpu.SemaphoreType.DMA((1 + 2 * LAST_PARTS,)),
            pltpu.SemaphoreType.DMA((LAST_PARTS,)),
        ],
        compiler_params=params(),
        name="last",
    )(forward, h, pre, halo, phi)


def body(state, velocity_order, wall_tag):
    forward = upstream_first().reshape(1)
    at = lax.axis_index("space").astype(jnp.int32).reshape(1)
    flat = state.reshape(NSLOT, 4, 2, 128).transpose(0, 2, 1, 3).reshape(NSLOT * 8, 128)
    near, m, left, phi = unpack(forward, flat, velocity_order)
    drifted = [drift(forward, phi, piece, flat) for piece in PIECES[0]]
    m, drifted[0] = lax.optimization_barrier((over_y(m), drifted[0]))
    (near,) = hold(m, near)
    near = downstream(near)
    tags = jnp.transpose(wall_tag, (1, 2, 0)).reshape(64, 64)
    m, drifted = over_rest(over_x(m), *drifted)
    h1, edge, m = first_step(forward, at, flat, drifted, m, tags, phi, left)
    drifted = [drift(forward, phi, piece, h1, near) for piece in PIECES[1]]
    m, drifted[0] = lax.optimization_barrier((over_y(inflow(forward, near, m)), drifted[0]))
    m, drifted[1] = lax.optimization_barrier((over_x(m), drifted[1]))
    (edge,) = hold(m, edge)
    edge = downstream(edge)
    m, drifted = over_rest(m, *drifted)
    out, pre, wall_heat = second_step(forward, at, h1, near, drifted, m, tags, phi)
    out = last(forward, out, pre, edge, phi)
    state_next = out.reshape(NSLOT, 2, 4, 128).transpose(0, 2, 1, 3).reshape(NSLOT, 4, 256)
    return state_next, wall_heat


def solution(mesh):
    return jax.shard_map(
        body,
        mesh=mesh,
        in_specs=(P("vel", "space", None), P("vel"), P()),
        out_specs=(P("vel", "space", None), P("space", None, None)),
        check_vma=False,
    )
```
